32 devices in a mesh: dp: 8 (over z, y), tensor: 4 (over x, core).
Axes of the slice: x: 2, y: 2, z: 4, core: 2. Of those that a mesh axis runs over, the one named last changes fastest.
Arguments:
- image_tokens: bfloat16 [18816, 512], P(('dp', 'tensor')), may hold values from -6 to 6
- tag_tokens: bfloat16 [12288, 512], P(('dp', 'tensor')), may hold values from -6 to 6
- image_cotangent: bfloat16 [18816, 512], P(('dp', 'tensor')), may hold values from -6 to 6
- tag_cotangent: bfloat16 [12288, 512], P(('dp', 'tensor')), may hold values from -6 to 6
- tag_lengths: int32 [24], P('dp'), may hold values from 1 to 512, 6144 in all
- slot_blocks: int32 [80], replicated, may hold values from 0 to 79, as said below
- master_blocks: float32 [4, 80, 128, 128], P('tensor', 'dp'), as said below
- left_factor: float32 [4, 80, 128, 128], P('tensor', 'dp'), as said below
- right_factor: float32 [4, 80, 128, 128], P('tensor', 'dp'), as said below
- left_root: float32 [4, 80, 128, 128], P('tensor', 'dp'), as said below
- right_root: float32 [4, 80, 128, 128], P('tensor', 'dp'), as said below
- vector_master: float32 [10, 512], P(None, 'dp'), as said below
- vector_moment: float32 [10, 512], P(None, 'dp'), as said below
Outputs:
- encoder_out: bfloat16 [18816, 512], P(('dp', 'tensor'))
- tag_output: bfloat16 [12288, 512], P(('dp', 'tensor'))
- image_gradient: float32 [18816, 512], P(('dp', 'tensor'))
- tag_gradient: float32 [12288, 512], P(('dp', 'tensor'))
- block_gradient: float32 [4, 80, 128, 128], P('tensor', 'dp')
- left_updated: float32 [4, 80, 128, 128], P('tensor', 'dp')
- right_updated: float32 [4, 80, 128, 128], P('tensor', 'dp')
- master_updated: float32 [4, 80, 128, 128], P('tensor', 'dp')
- master_copy: bfloat16 [4, 80, 128, 128], P('tensor', 'dp')
- vector_gradient: float32 [10, 512], P(None, 'dp')
- moment_updated: float32 [10, 512], P(None, 'dp')
- vector_updated: float32 [10, 512], P(None, 'dp')
The draws below stay inside these ranges and needn't reach their ends.
Inputs may be any that keep to these rules, and one draw needn't show every extreme that they name: `slot_blocks`: each of 0 to 79 appears once; a slot holding 80 or more holds no tile. `tag_lengths`: one sequence has 512 live tags. `master_blocks`: master weights. `left_factor`: symmetric. `right_factor`: symmetric. `left_root`: symmetric. `right_root`: symmetric. `vector_master`: gains and shifts. `vector_moment`: every entry is positive.
All inputs are finite; a program needn't handle non-finite values. No bound on the sum of `tag_lengths` on one device may be relied on, other than what follows from the above.
Results may differ from the reference program's by a relative error of at most 0.019.
Values may be sent and summed in bfloat16 or wider, within the bound.
No kernel may reach another device: no remote copies, remote signals or barrier semaphores. Data moves between devices by JAX's collectives and lax.ppermute only.
A program may use at most 128 MiB of HBM per device.

```python
import math
import jax
import jax.numpy as jnp
import numpy as np
from jax import lax

D = 512
HEADS = 8
HEAD_DIM = 64
FF = 1024
ENC_TOK = 784
TAGS = 512
TILE_SIDE = 128
TENSOR_INDICES = 4
HC = 128
HID = 256
TILES_PER_INDEX = 80
SLOT_COUNT = 80
IMAGES = 24
ENC_ROWS = 18816
TAG_ROWS = 12288
LIVE = 6144


def block_scales():
    row_tiles = D // TILE_SIDE
    head_tiles = HC // TILE_SIDE
    hidden_tiles = HID // TILE_SIDE
    encoder_sum = math.sqrt(ENC_ROWS)
    tag_total = math.sqrt(LIVE)
    starting_scale = D ** (-0.5)
    down_scale = FF ** (-0.5)
    encoder_boost = math.sqrt(ENC_TOK / 3.0)
    tag_boost = math.sqrt(max(TAGS / 12.0, 1.0))
    category_table = [(3 * row_tiles * head_tiles, starting_scale, encoder_sum), (head_tiles * row_tiles, starting_scale * encoder_boost, encoder_sum / encoder_boost), (row_tiles * hidden_tiles, starting_scale, 0.5 * encoder_sum), (hidden_tiles * row_tiles, down_scale, 0.7 * encoder_sum), (3 * row_tiles * head_tiles, starting_scale, tag_total), (head_tiles * row_tiles, starting_scale * tag_boost, tag_total / tag_boost), (row_tiles * head_tiles, starting_scale, tag_total), (2 * row_tiles * head_tiles, starting_scale, 0.6 * encoder_sum), (head_tiles * row_tiles, starting_scale * encoder_boost, tag_total / encoder_boost), (row_tiles * hidden_tiles, starting_scale, 0.5 * tag_total), (hidden_tiles * row_tiles, down_scale, 0.7 * tag_total)]
    spread_amount = [np.full(category_entry[0], category_entry[1]) for category_entry in category_table] + [np.full(SLOT_COUNT - TILES_PER_INDEX, starting_scale)]
    typical_level = [np.full(category_entry[0], category_entry[2]) for category_entry in category_table] + [np.full(SLOT_COUNT - TILES_PER_INDEX, tag_total)]
    return (np.concatenate(spread_amount).astype(np.float32), np.concatenate(typical_level).astype(np.float32))


def slot_order(key):
    return jax.random.permutation(jax.random.fold_in(key, 11), SLOT_COUNT)


def slot_scales(key):
    spread_amount, typical_level = block_scales()
    permuted = slot_order(key)
    return (jnp.asarray(spread_amount)[permuted], jnp.asarray(typical_level)[permuted])


def draw_slot_blocks(key, part):
    return slot_order(key).astype(jnp.int32)


def draw_master_blocks(key, part):
    spread_amount, typical_level = slot_scales(key)
    normal_draw = jax.random.normal(jax.random.fold_in(key, 21), (TENSOR_INDICES, SLOT_COUNT, TILE_SIDE, TILE_SIDE), jnp.float32)
    return normal_draw * spread_amount[None, :, None, None]


def factor_draw(key, random_salt):
    spread_amount, typical_level = slot_scales(key)
    stat_level = TILE_SIDE * typical_level * typical_level
    multiplier = jnp.exp(jax.random.uniform(jax.random.fold_in(key, random_salt), (TENSOR_INDICES, SLOT_COUNT, 1, 1), jnp.float32) * math.log(4.0))
    normal_draw = jax.random.normal(jax.random.fold_in(key, random_salt + 1), (TENSOR_INDICES, SLOT_COUNT, TILE_SIDE, TILE_SIDE), jnp.float32)
    symmetric = (normal_draw + jnp.swapaxes(normal_draw, 2, 3)) * (0.02 / math.sqrt(2.0))
    identity = jnp.eye(TILE_SIDE, dtype=jnp.float32)
    return stat_level[None, :, None, None] * (multiplier * identity + symmetric)


def root_draw(key, random_salt):
    spread_amount, typical_level = slot_scales(key)
    amplitude = jnp.sqrt(spread_amount / typical_level)
    diagonal_part = jnp.exp((jax.random.uniform(jax.random.fold_in(key, random_salt), (TENSOR_INDICES, SLOT_COUNT, TILE_SIDE), jnp.float32) * 2.0 - 1.0) * math.log(2.0))
    normal_draw = jax.random.normal(jax.random.fold_in(key, random_salt + 1), (TENSOR_INDICES, SLOT_COUNT, TILE_SIDE, TILE_SIDE), jnp.float32)
    symmetric = (normal_draw + jnp.swapaxes(normal_draw, 2, 3)) * (0.35 / math.sqrt(2.0 * TILE_SIDE))
    identity = jnp.eye(TILE_SIDE, dtype=jnp.float32)
    return amplitude[None, :, None, None] * (diagonal_part[..., None] * identity + symmetric)


def draw_left_factor(key, part):
    return factor_draw(key, 31)


def draw_right_factor(key, part):
    return factor_draw(key, 33)


def draw_left_root(key, part):
    return root_draw(key, 35)


def draw_right_root(key, part):
    return root_draw(key, 37)


def draw_vector_master(key, part):
    normal_draw = jax.random.normal(jax.random.fold_in(key, 41), (10, D), jnp.float32)
    parity = (jnp.arange(10) % 2 == 0)[:, None]
    return jnp.where(parity, 1.0 + 0.15 * normal_draw, 0.3 * normal_draw)


def draw_vector_moment(key, part):
    row_scale = jnp.asarray(np.array([ENC_ROWS] * 4 + [LIVE] * 6, dtype=np.float32))
    factor = jnp.exp(jax.random.uniform(jax.random.fold_in(key, 51), (10, D), jnp.float32) * math.log(4.0))
    return 1.44 * row_scale[:, None] * factor


def block_scale(own_key, extent, split, low, high):
    factor_of = 1.0
    for axis_at, blocks in split:
        steps = jax.random.uniform(jax.random.fold_in(jax.random.fold_in(own_key, 6), axis_at), (blocks,), jnp.float32, low / len(split), high / len(split))
        factor_of = factor_of * jnp.repeat(jnp.exp(steps), extent[axis_at] // blocks).reshape((-1,) + (1,) * (len(extent) - 1 - axis_at))
    return factor_of


def split_up(amount, total, limit, lean):
    weights = [(1 << 20) // math.isqrt(rank ** lean) + 1 for rank in range(2, amount + 1)]
    rest, holding = total - limit - (amount - 1), [1] * (amount - 1)
    while rest > 0:
        movable = [i for i in range(amount - 1) if holding[i] < limit]
        mass, remaining = sum([weights[i] for i in movable]), rest
        for i in movable:
            extra = min(limit - holding[i], max(1, remaining * weights[i] // mass), rest)
            holding[i] = holding[i] + extra
            rest = rest - extra
    return np.array([limit] + holding)


def uneven(stream_key, count, total, reach, lean):
    if count == 2:
        one = jax.random.randint(stream_key, (), max(1, total - reach), min(reach, total - 1) + 1)
        return jnp.stack([one, total - one])
    tallies = jnp.asarray(split_up(count, total, reach, lean), jnp.int32)
    pairs = (count - 1) // 2
    source_of, sink = tallies[1:1 + 2 * pairs:2], tallies[2:2 + 2 * pairs:2]
    room = jnp.minimum(source_of - 1, reach - sink)
    passed = jax.random.randint(jax.random.fold_in(stream_key, 1), (pairs,), 0, 1 << 20) % (room + 1)
    tallies = tallies.at[1:1 + 2 * pairs:2].set(source_of - passed).at[2:2 + 2 * pairs:2].set(sink + passed)
    return tallies[jax.random.permutation(jax.random.fold_in(stream_key, 2), count)]


def scatter_about(rng, extent, deviation, reach, cuts=(), held_as=jnp.bfloat16):
    values = deviation * jax.random.normal(rng, extent, jnp.float32)
    if cuts:
        values = values * block_scale(rng, extent, cuts, -0.22, 0.18)
    return jnp.clip(values, -reach, reach).astype(held_as)


def setup_inputs(seed: int = 0) -> dict:
    key_of = jax.random.split(jax.random.key(seed), 14)
    return {
        "image_tokens": scatter_about(key_of[0], (ENC_ROWS, D), 1.0, 6.0, ((0, 32),)),
        "tag_tokens": scatter_about(key_of[1], (TAG_ROWS, D), 1.0, 6.0, ((0, 32),)),
        "image_cotangent": scatter_about(key_of[2], (ENC_ROWS, D), 1.0, 6.0, ((0, 32),)),
        "tag_cotangent": scatter_about(key_of[3], (TAG_ROWS, D), 1.0, 6.0, ((0, 32),)),
        "tag_lengths": uneven(key_of[4], IMAGES, IMAGES * TAGS // 2, TAGS, 2).astype(jnp.int32),
        "slot_blocks": draw_slot_blocks(jax.random.fold_in(key_of[13], 71), 0),
        "master_blocks": draw_master_blocks(jax.random.fold_in(key_of[13], 71), 0),
        "left_factor": draw_left_factor(jax.random.fold_in(key_of[13], 71), 0),
        "right_factor": draw_right_factor(jax.random.fold_in(key_of[13], 71), 0),
        "left_root": draw_left_root(jax.random.fold_in(key_of[13], 71), 0),
        "right_root": draw_right_root(jax.random.fold_in(key_of[13], 71), 0),
        "vector_master": draw_vector_master(jax.random.fold_in(key_of[13], 71), 0),
        "vector_moment": draw_vector_moment(jax.random.fold_in(key_of[13], 71), 0),
    }


NORM_EPSILON = 1e-05
MATRIX_RATE = 0.5
VECTOR_RATE = 0.2
STAT_DECAY = 0.5
MASKED_SCORE = -1e+30

@jax.custom_vjp
def low(v):
    return lax.optimization_barrier(v.astype(jnp.bfloat16)).astype(jnp.float32)

@jax.custom_vjp
def low_back(v):
    return v

def low_keep(v):
    return (low(v), None)

def low_pass(kept, grad):
    return (grad,)

def back_keep(v):
    return (v, None)

def back_low(kept, grad):
    return (low(grad),)
low.defvjp(low_keep, low_pass)
low_back.defvjp(back_keep, back_low)

def rounded(operand):
    return low(low_back(operand))

def smooth_gate(values):
    return jax.nn.gelu(values, approximate=False)

def matmul(former, latter):
    return jnp.dot(former, latter, precision=lax.Precision.HIGHEST, preferred_element_type=jnp.float32)

def layer_norm(residual, norm_gain, norm_shift):
    row_mean = lax.optimization_barrier(jnp.mean(residual, axis=-1, keepdims=True))
    centered = residual - row_mean
    inverse_scale = lax.rsqrt(lax.optimization_barrier(jnp.mean(centered * centered, axis=-1, keepdims=True)) + NORM_EPSILON)
    return centered * inverse_scale * norm_gain + norm_shift

def causal_allowed(item_length, live_count):
    row_index = lax.broadcasted_iota(jnp.int32, (item_length, item_length), 0)
    column_index = lax.broadcasted_iota(jnp.int32, (item_length, item_length), 1)
    return (column_index <= row_index) & (column_index < live_count)

def heads_attend(queries, key_rows, value_rows, allowed):
    query_heads = queries.reshape(queries.shape[0], HEADS, HEAD_DIM)
    key_heads = key_rows.reshape(key_rows.shape[0], HEADS, HEAD_DIM)
    value_heads = value_rows.reshape(value_rows.shape[0], HEADS, HEAD_DIM)
    scores = low_back(jnp.einsum('qhd,khd->hqk', query_heads, key_heads, precision=lax.Precision.HIGHEST) * HEAD_DIM ** (-0.5))
    if allowed is not None:
        scores = jnp.where(allowed[None], scores, MASKED_SCORE)
    attention = low(jax.nn.softmax(scores, axis=-1))
    mixed_rows = jnp.einsum('hqk,khd->qhd', attention, value_heads, precision=lax.Precision.HIGHEST)
    return mixed_rows.reshape(queries.shape[0], HEADS * HEAD_DIM)

def image_item(operands):
    return heads_attend(operands[0], operands[1], operands[2], None)

def tag_item(operands):
    return heads_attend(operands[0], operands[1], operands[2], causal_allowed(TAGS, operands[3]))

def layers_forward(matrices, vectors, image_rows, tag_rows, tag_lengths):
    encoder_query, encoder_key, encoder_value, encoder_output, encoder_up, encoder_down, decoder_query, decoder_key, decoder_value, decoder_output, cross_query, cross_key, cross_value, cross_output, decoder_up, decoder_down = matrices
    image_count = tag_lengths.shape[0]
    queries = rounded(matmul(image_rows, encoder_query)).reshape(image_count, ENC_TOK, -1)
    key_rows = rounded(matmul(image_rows, encoder_key)).reshape(image_count, ENC_TOK, -1)
    value_rows = rounded(matmul(image_rows, encoder_value)).reshape(image_count, ENC_TOK, -1)
    mixed_rows = rounded(lax.map(jax.checkpoint(image_item), (queries, key_rows, value_rows)).reshape(image_count * ENC_TOK, -1))
    after_attention = layer_norm(image_rows + low_back(matmul(mixed_rows, encoder_output)), vectors[0], vectors[1])
    hidden = low(smooth_gate(low_back(matmul(low(after_attention), encoder_up))))
    encoded = layer_norm(after_attention + low_back(matmul(hidden, encoder_down)), vectors[2], vectors[3])
    queries = rounded(matmul(tag_rows, decoder_query)).reshape(image_count, TAGS, -1)
    key_rows = rounded(matmul(tag_rows, decoder_key)).reshape(image_count, TAGS, -1)
    value_rows = rounded(matmul(tag_rows, decoder_value)).reshape(image_count, TAGS, -1)
    mixed_rows = rounded(lax.map(jax.checkpoint(tag_item), (queries, key_rows, value_rows, tag_lengths)).reshape(image_count * TAGS, -1))
    after_self = layer_norm(tag_rows + low_back(matmul(mixed_rows, decoder_output)), vectors[4], vectors[5])
    encoded_low = low(encoded)
    queries = rounded(matmul(low(after_self), cross_query)).reshape(image_count, TAGS, -1)
    key_rows = rounded(matmul(encoded_low, cross_key)).reshape(image_count, ENC_TOK, -1)
    value_rows = rounded(matmul(encoded_low, cross_value)).reshape(image_count, ENC_TOK, -1)
    mixed_rows = rounded(lax.map(jax.checkpoint(image_item), (queries, key_rows, value_rows)).reshape(image_count * TAGS, -1))
    after_cross = layer_norm(after_self + low_back(matmul(mixed_rows, cross_output)), vectors[6], vectors[7])
    hidden = low(smooth_gate(low_back(matmul(low(after_cross), decoder_up))))
    decoded = layer_norm(after_cross + low_back(matmul(hidden, decoder_down)), vectors[8], vectors[9])
    return (encoded, decoded)

def from_blocks(blocks, row_count, column_count):
    return blocks.reshape(row_count // TILE_SIDE, column_count // TILE_SIDE, TILE_SIDE, TILE_SIDE).transpose(0, 2, 1, 3).reshape(row_count, column_count)

def to_blocks(matrix):
    row_count, column_count = matrix.shape
    return matrix.reshape(row_count // TILE_SIDE, TILE_SIDE, column_count // TILE_SIDE, TILE_SIDE).transpose(0, 2, 1, 3).reshape(-1, TILE_SIDE, TILE_SIDE)

def shard_shapes():
    return [(D, 3 * HC), (HC, D), (D, HID), (HID, D), (D, 3 * HC), (HC, D), (D, HC), (D, 2 * HC), (HC, D), (D, HID), (HID, D)]

def column_join(pieces, index, start, stop):
    return jnp.concatenate([shard_piece[index][:, start:stop] for shard_piece in pieces], axis=1)

def row_join(pieces, index):
    return jnp.concatenate([shard_piece[index] for shard_piece in pieces], axis=0)

def assemble(pieces):
    return (column_join(pieces, 0, 0, HC), column_join(pieces, 0, HC, 2 * HC), column_join(pieces, 0, 2 * HC, 3 * HC), row_join(pieces, 1), column_join(pieces, 2, 0, HID), row_join(pieces, 3), column_join(pieces, 4, 0, HC), column_join(pieces, 4, HC, 2 * HC), column_join(pieces, 4, 2 * HC, 3 * HC), row_join(pieces, 5), column_join(pieces, 6, 0, HC), column_join(pieces, 7, 0, HC), column_join(pieces, 7, HC, 2 * HC), row_join(pieces, 8), column_join(pieces, 9, 0, HID), row_join(pieces, 10))

def disassemble(assembled, shard_index):
    head_start = shard_index * HC
    head_stop = head_start + HC
    hidden_start = shard_index * HID
    hidden_stop = hidden_start + HID
    return [jnp.concatenate([assembled[0][:, head_start:head_stop], assembled[1][:, head_start:head_stop], assembled[2][:, head_start:head_stop]], axis=1), assembled[3][head_start:head_stop], assembled[4][:, hidden_start:hidden_stop], assembled[5][hidden_start:hidden_stop], jnp.concatenate([assembled[6][:, head_start:head_stop], assembled[7][:, head_start:head_stop], assembled[8][:, head_start:head_stop]], axis=1), assembled[9][head_start:head_stop], assembled[10][:, head_start:head_stop], jnp.concatenate([assembled[11][:, head_start:head_stop], assembled[12][:, head_start:head_stop]], axis=1), assembled[13][head_start:head_stop], assembled[14][:, hidden_start:hidden_stop], assembled[15][hidden_start:hidden_stop]]

def reference(image_tokens, tag_tokens, image_cotangent, tag_cotangent, tag_lengths, slot_blocks, master_blocks, left_factor, right_factor, left_root, right_root, vector_master, vector_moment):
    placement = jnp.argsort(slot_blocks)[:TILES_PER_INDEX].astype(jnp.int32)
    working = lax.optimization_barrier(master_blocks.astype(jnp.bfloat16)).astype(jnp.float32)
    pieces = []
    for shard_index in range(TENSOR_INDICES):
        ordered = working[shard_index][placement]
        matrices = []
        offset = 0
        for row_count, column_count in shard_shapes():
            number = row_count // TILE_SIDE * (column_count // TILE_SIDE)
            matrices.append(from_blocks(ordered[offset:offset + number], row_count, column_count))
            offset = offset + number
        pieces.append(matrices)
    assembled = assemble(pieces)
    vectors = lax.optimization_barrier(vector_master.astype(jnp.bfloat16)).astype(jnp.float32)
    image_rows = image_tokens.astype(jnp.float32)
    tag_rows = tag_tokens.astype(jnp.float32)
    live_rows = (lax.broadcasted_iota(jnp.int32, (IMAGES, TAGS), 1) < tag_lengths[:, None]).astype(jnp.float32).reshape(-1, 1)

    def forward_only(matrices, vector_values, images_in, tags_in):
        return layers_forward(matrices, vector_values, images_in, tags_in, tag_lengths)
    (encoded, decoded), pullback = jax.vjp(forward_only, assembled, vectors, image_rows, tag_rows)
    delta_matrices, vector_gradient, image_gradient, tag_gradient = pullback((image_cotangent.astype(jnp.float32), tag_cotangent.astype(jnp.float32) * live_rows))
    slot_list = []
    for shard_index in range(TENSOR_INDICES):
        tile_listing = [to_blocks(shard_piece) for shard_piece in disassemble(delta_matrices, shard_index)]
        tile_listing.append(jnp.zeros((SLOT_COUNT - TILES_PER_INDEX, TILE_SIDE, TILE_SIDE), jnp.float32))
        slot_list.append(jnp.concatenate(tile_listing, axis=0)[slot_blocks])
    block_gradient = jnp.stack(slot_list, axis=0)
    highest = lax.Precision.HIGHEST
    left_updated = STAT_DECAY * left_factor + (1.0 - STAT_DECAY) * jnp.einsum('asij,askj->asik', block_gradient, block_gradient, precision=highest)
    right_updated = STAT_DECAY * right_factor + (1.0 - STAT_DECAY) * jnp.einsum('asji,asjk->asik', block_gradient, block_gradient, precision=highest)
    rotated = jnp.einsum('asij,asjk->asik', left_root, block_gradient, precision=highest)
    master_updated = master_blocks - MATRIX_RATE * jnp.einsum('asij,asjk->asik', rotated, right_root, precision=highest)
    moment_updated = STAT_DECAY * vector_moment + (1.0 - STAT_DECAY) * vector_gradient * vector_gradient
    vector_updated = vector_master - VECTOR_RATE * vector_gradient / (jnp.sqrt(moment_updated) + 1e-08)
    return (encoded.astype(jnp.bfloat16), decoded.astype(jnp.bfloat16), image_gradient, tag_gradient, block_gradient, left_updated, right_updated, master_updated, master_updated.astype(jnp.bfloat16), vector_gradient, moment_updated, vector_updated)
```

```python
import jax
import jax.numpy as jnp
from jax import lax
from jax.experimental import pallas as pl
from jax.experimental.pallas import tpu as pltpu
from jax.sharding import PartitionSpec as P

D = 512
HEADS = 8
HEAD_DIM = 64
FF = 1024
TILE = 128
CHUNK = 16
CHUNKS = 5

NORM_EPSILON = 1e-05
MATRIX_RATE = 0.5
VECTOR_RATE = 0.2
STAT_DECAY = 0.5
MASKED_SCORE = -1e30

F32 = jnp.float32
BF16 = jnp.bfloat16
ANY = pl.BlockSpec(memory_space=pl.ANY)
VM = pl.BlockSpec(memory_space=pltpu.VMEM)


def core_pairs():
    return [(i, i ^ 1) for i in range(4)]


def chip_pairs():
    return [(i, i ^ 2) for i in range(4)]


def y_pairs():
    return [(i, i ^ 1) for i in range(8)]


def z_shift(step):
    return [(2 * z + y, 2 * ((z + step) % 4) + y) for z in range(4) for y in range(2)]


def relative_rank(position, size):
    me = lax.axis_index("dp")
    if size != 8:
        return jnp.int32(position)
    swapped, step = divmod(position, 4)
    return 2 * lax.rem(me // 2 - step + 4, 4) + lax.rem(me + swapped, 2)


def target_rank(position, size):
    me = lax.axis_index("dp")
    if size != 8:
        return jnp.int32(position)
    swapped, step = divmod(position, 4)
    return 2 * lax.rem(me // 2 + step, 4) + lax.rem(me + swapped, 2)


def gather_pieces(piece, size):
    if size != 8:
        return list(lax.all_gather(piece, "dp", axis=0, tiled=False))
    column = [piece] + [lax.ppermute(piece, "dp", z_shift(step)) for step in (1, 2, 3)]
    return column + [lax.ppermute(part, "dp", y_pairs()) for part in column]


def sum_pieces(pieces, size):
    if size != 8:
        whole = lax.psum_scatter(
            jnp.stack(pieces).astype(F32), "dp", scatter_dimension=0, tiled=False
        )
        return whole
    column = []
    for step in (1, 2, 3, 0):
        other = lax.ppermute(pieces[4 + step], "dp", y_pairs())
        both = pieces[step].astype(F32) + other.astype(F32)
        if step:
            column.append(lax.ppermute(both.astype(BF16), "dp", z_shift(step)).astype(F32))
        else:
            column.append(both)
    return (column[0] + column[1]) + (column[2] + column[3])


def gather_group(part):
    far = lax.ppermute(part, "tensor", chip_pairs())
    near = lax.ppermute(part, "tensor", core_pairs())
    far_near = lax.ppermute(far, "tensor", core_pairs())
    return (part, near, far, far_near)


def sum_group(parts):
    near = lax.ppermute(parts[1], "tensor", core_pairs())
    far_near = lax.ppermute(parts[3], "tensor", core_pairs())
    far = (parts[2].astype(F32) + far_near.astype(F32)).astype(BF16)
    far = lax.ppermute(far, "tensor", chip_pairs())
    return (parts[0].astype(F32) + near.astype(F32) + far.astype(F32)).astype(BF16)


def sum_over_group(value):
    value = value + lax.ppermute(value, "tensor", core_pairs())
    return value + lax.ppermute(value, "tensor", chip_pairs())


def pull_rows(rows, length):
    shards = lax.axis_size("tensor")
    later = lax.ppermute(rows, "tensor", [(i + 1, i) for i in range(shards - 1)])
    start = lax.axis_index("tensor") * (length - rows.shape[0])
    return lax.dynamic_slice_in_dim(jnp.concatenate([rows, later], axis=0), start, length, axis=0)


def push_rows(item, count):
    shards = lax.axis_size("tensor")
    length = item.shape[0]
    earlier = lax.ppermute(
        item[length - count :], "tensor", [(i, i + 1) for i in range(shards - 1)]
    )
    start = count - lax.axis_index("tensor") * (length - count)
    return lax.dynamic_slice_in_dim(
        jnp.concatenate([earlier, item[:count]], axis=0), start, count, axis=0
    )


def order_tiles(pieces, block_ids, slots):
    total = CHUNK * CHUNKS

    def kernel(ids, *refs):
        sources, out, sem = refs[:-2], refs[-2], refs[-1]

        def copy(p, j, b):
            return pltpu.make_async_copy(
                sources[p].at[pl.ds(j * TILE, TILE)], out.at[pl.ds(b * TILE, TILE)], sem
            )

        for p in range(len(sources)):
            for j in range(slots):
                block = ids[p * slots + j]

                @pl.when(block < total)
                def _():
                    copy(p, j, block).start()

        pltpu.make_async_copy(out, out, sem).wait()

    return pl.pallas_call(
        kernel,
        out_shape=jax.ShapeDtypeStruct((total * TILE, TILE), BF16),
        grid_spec=pltpu.PrefetchScalarGridSpec(
            num_scalar_prefetch=1,
            grid=(1,),
            in_specs=[ANY] * len(pieces),
            out_specs=ANY,
            scratch_shapes=[pltpu.SemaphoreType.DMA],
        ),
        name="order_tiles",
    )(block_ids, *pieces)


def deal_tiles(chunks, vector_rows, slot_of_block, positions, slots):
    count = len(positions)
    rows = slots * TILE + vector_rows.shape[1]

    def kernel(where, *refs):
        sources, extra, out, sem = refs[:CHUNKS], refs[CHUNKS], refs[CHUNKS + 1], refs[CHUNKS + 2]
        for c in range(CHUNKS):
            for k in range(CHUNK):
                pltpu.make_async_copy(
                    sources[c].at[pl.ds(k * TILE, TILE)],
                    out.at[pl.ds(pl.multiple_of(where[c * CHUNK + k], 16), TILE)],
                    sem,
                ).start()
        for p in range(count):
            pltpu.make_async_copy(
                extra.at[p], out.at[pl.ds(p * rows + slots * TILE, rows - slots * TILE)], sem
            ).start()
        for c in range(CHUNKS):
            pltpu.make_async_copy(sources[c], sources[c], sem).wait()
        pltpu.make_async_copy(extra, extra, sem).wait()

    owner = slot_of_block // slots
    place = jnp.zeros_like(owner)
    for p, rank in enumerate(positions):
        place = jnp.where(owner == rank, p, place)
    where = place * rows + lax.rem(slot_of_block, slots) * TILE
    out = pl.pallas_call(
        kernel,
        out_shape=jax.ShapeDtypeStruct((count * rows, TILE), BF16),
        grid_spec=pltpu.PrefetchScalarGridSpec(
            num_scalar_prefetch=1,
            grid=(1,),
            in_specs=[ANY] * (CHUNKS + 1),
            out_specs=ANY,
            scratch_shapes=[pltpu.SemaphoreType.DMA],
        ),
        name="deal_tiles",
    )(where, *chunks, vector_rows)
    return [out[p * rows : (p + 1) * rows] for p in range(count)]


def matmul(former, latter):
    return jnp.dot(former, latter, preferred_element_type=F32)


def times_transpose(former, latter):
    return lax.dot_general(former, latter, (((1,), (1,)), ((), ())), preferred_element_type=F32)


def transpose_times(former, latter):
    return lax.dot_general(former, latter, (((0,), (0,)), ((), ())), preferred_element_type=F32)


def smooth_gate(values):
    return jax.nn.gelu(values, approximate=False)


def gate_backward(preact, incoming):
    result, pullback = jax.vjp(smooth_gate, preact)
    return pullback(incoming)[0]


def norm_forward(residual, norm_gain, norm_shift):
    row_mean = jnp.mean(residual, axis=-1, keepdims=True)
    centered = residual - row_mean
    inverse_scale = lax.rsqrt(jnp.mean(centered * centered, axis=-1, keepdims=True) + NORM_EPSILON)
    normed = centered * inverse_scale
    return (normed * norm_gain + norm_shift, (normed, inverse_scale))


def norm_backward(gradient, stored, norm_gain):
    normed, inverse_scale = stored
    scaled = gradient * norm_gain
    adjusted = (
        scaled
        - jnp.mean(scaled, axis=-1, keepdims=True)
        - normed * jnp.mean(scaled * normed, axis=-1, keepdims=True)
    )
    return (inverse_scale * adjusted, jnp.sum(gradient * normed, axis=0), jnp.sum(gradient, axis=0))


def causal_allowed(item_length, live_count):
    row_index = lax.broadcasted_iota(jnp.int32, (item_length, item_length), 0)
    column_index = lax.broadcasted_iota(jnp.int32, (item_length, item_length), 1)
    return (column_index <= row_index) & (column_index < live_count)


def split_heads(matrix):
    return matrix.reshape(matrix.shape[0], matrix.shape[1] // HEAD_DIM, HEAD_DIM)


def head_scores(queries, key_rows, allowed):
    scores = jnp.einsum(
        "qhd,khd->hqk", split_heads(queries), split_heads(key_rows), preferred_element_type=F32
    ) * HEAD_DIM ** (-0.5)
    if allowed is None:
        return scores
    return jnp.where(allowed[None], scores, MASKED_SCORE)


def attend(queries, key_rows, value_rows, allowed):
    scores = head_scores(queries, key_rows, allowed)
    row_max = jnp.max(scores, axis=-1, keepdims=True)
    log_total = row_max + jnp.log(jnp.sum(jnp.exp(scores - row_max), axis=-1, keepdims=True))
    attention = jnp.exp(scores - log_total).astype(BF16)
    mixed = jnp.einsum("hqk,khd->qhd", attention, split_heads(value_rows), preferred_element_type=F32)
    return (mixed.reshape(queries.shape).astype(BF16), log_total)


def attend_back(queries, key_rows, value_rows, allowed, log_total, delta_mixed):
    scores = head_scores(queries, key_rows, allowed)
    attention = jnp.exp(scores - log_total)
    delta_heads = split_heads(delta_mixed)
    delta_attention = jnp.einsum(
        "qhd,khd->hqk", delta_heads, split_heads(value_rows), preferred_element_type=F32
    )
    delta_values = jnp.einsum(
        "hqk,qhd->khd", attention.astype(BF16), delta_heads, preferred_element_type=F32
    )
    delta_scores = attention * (
        delta_attention - jnp.sum(attention * delta_attention, axis=-1, keepdims=True)
    )
    delta_scores = delta_scores.astype(BF16)
    delta_queries = jnp.einsum(
        "hqk,khd->qhd", delta_scores, split_heads(key_rows), preferred_element_type=F32
    ) * HEAD_DIM ** (-0.5)
    delta_keys = jnp.einsum(
        "hqk,qhd->khd", delta_scores, split_heads(queries), preferred_element_type=F32
    ) * HEAD_DIM ** (-0.5)
    return (
        delta_queries.reshape(queries.shape).astype(BF16),
        delta_keys.reshape(key_rows.shape).astype(BF16),
        delta_values.reshape(value_rows.shape).astype(BF16),
    )


def tall(parts, first, count):
    picked = jnp.stack([p.reshape(CHUNK, TILE, TILE)[first : first + 4 * count] for p in parts])
    picked = picked.reshape(4, 4, count, TILE, TILE)
    return [picked[:, :, c].transpose(1, 2, 0, 3).reshape(D, 4 * TILE) for c in range(count)]


def wide(parts, first, count):
    picked = jnp.stack([p.reshape(CHUNK, TILE, TILE)[first : first + 4 * count] for p in parts])
    picked = picked.reshape(4, count, 4, TILE, TILE)
    return [picked[:, c].transpose(0, 2, 1, 3).reshape(4 * TILE, D) for c in range(count)]


def untall(matrices):
    stacked = jnp.stack([m.astype(BF16).reshape(4, TILE, 4, TILE) for m in matrices])
    stacked = stacked.transpose(3, 1, 0, 2, 4)
    return stacked.reshape(4, -1, TILE, TILE)


def unwide(matrices):
    stacked = jnp.stack([m.astype(BF16).reshape(4, TILE, 4, TILE) for m in matrices])
    stacked = stacked.transpose(1, 0, 3, 2, 4)
    return stacked.reshape(4, -1, TILE, TILE)


def as_parts(*tiles):
    whole = jnp.concatenate(tiles, axis=1).reshape(4, CHUNK * TILE, TILE)
    return [whole[r] for r in range(4)]


def compute(x, y, xc, yc, live, weights, vectors, alive):
    g = [vectors[i : i + 1] for i in range(10)]
    wq, wk, wv = tall(weights[0], 0, 3)
    (wo,) = wide(weights[0], 12, 1)
    w1 = jnp.concatenate(tall(weights[1], 0, 2), axis=1)
    w2 = jnp.concatenate(wide(weights[1], 8, 2), axis=0)
    sq, sk, sv = tall(weights[2], 0, 3)
    (so,) = wide(weights[2], 12, 1)
    (cq,) = tall(weights[3], 0, 1)
    ck, cv = tall(weights[3], 4, 2)
    (co,) = wide(weights[3], 12, 1)
    v1 = jnp.concatenate(tall(weights[4], 0, 2), axis=1)
    v2 = jnp.concatenate(wide(weights[4], 8, 2), axis=0)
    low = lambda a: a.astype(BF16)
    q, k, v = low(matmul(x, wq)), low(matmul(x, wk)), low(matmul(x, wv))
    o, lse = attend(q, k, v, None)
    first, n0 = norm_forward(x.astype(F32) + matmul(o, wo), g[0], g[1])
    pre = matmul(low(first), w1)
    hid = low(smooth_gate(pre))
    enc, n1 = norm_forward(first + matmul(hid, w2), g[2], g[3])
    encl = low(enc)
    allowed = causal_allowed(y.shape[0], live)
    q2, k2, v2_ = low(matmul(y, sq)), low(matmul(y, sk)), low(matmul(y, sv))
    o2, lse2 = attend(q2, k2, v2_, allowed)
    second, n2 = norm_forward(y.astype(F32) + matmul(o2, so), g[4], g[5])
    q3, k3, v3 = low(matmul(low(second), cq)), low(matmul(encl, ck)), low(matmul(encl, cv))
    o3, lse3 = attend(q3, k3, v3, None)
    third, n3 = norm_forward(second + matmul(o3, co), g[6], g[7])
    pre2 = matmul(low(third), v1)
    hid2 = low(smooth_gate(pre2))
    dec, n4 = norm_forward(third + matmul(hid2, v2), g[8], g[9])
    vg = [None] * 10
    rows = lax.broadcasted_iota(jnp.int32, (y.shape[0], 1), 0)
    b = jnp.where((rows < live) & alive, yc.astype(F32), 0.0)
    b, vg[8], vg[9] = norm_backward(b, n4, g[8])
    bl = low(b)
    dh = low(gate_backward(pre2, times_transpose(bl, v2)))
    gv2, gv1 = transpose_times(hid2, bl), transpose_times(low(third), dh)
    b = b + times_transpose(dh, v1)
    b, vg[6], vg[7] = norm_backward(b, n3, g[6])
    bl = low(b)
    do = low(times_transpose(bl, co))
    gco = transpose_times(o3, bl)
    dq, dk, dv = attend_back(q3, k3, v3, None, lse3, do)
    gcq, gck, gcv = transpose_times(low(second), dq), transpose_times(encl, dk), transpose_times(encl, dv)
    denc = times_transpose(dk, ck) + times_transpose(dv, cv)
    b = b + times_transpose(dq, cq)
    b, vg[4], vg[5] = norm_backward(b, n2, g[4])
    bl = low(b)
    do = low(times_transpose(bl, so))
    gso = transpose_times(o2, bl)
    dq, dk, dv = attend_back(q2, k2, v2_, allowed, lse2, do)
    gs = [transpose_times(y, d) for d in (dq, dk, dv)]
    dy = b + times_transpose(dq, sq) + times_transpose(dk, sk) + times_transpose(dv, sv)
    b = jnp.where(alive, xc.astype(F32), 0.0) + denc
    b, vg[2], vg[3] = norm_backward(b, n1, g[2])
    bl = low(b)
    dh = low(gate_backward(pre, times_transpose(bl, w2)))
    gw2, gw1 = transpose_times(hid, bl), transpose_times(low(first), dh)
    b = b + times_transpose(dh, w1)
    b, vg[0], vg[1] = norm_backward(b, n0, g[0])
    bl = low(b)
    do = low(times_transpose(bl, wo))
    gwo = transpose_times(o, bl)
    dq, dk, dv = attend_back(q, k, v, None, lse, do)
    ge = [transpose_times(x, d) for d in (dq, dk, dv)]
    dx = b + times_transpose(dq, wq) + times_transpose(dk, wk) + times_transpose(dv, wv)
    parts = [
        as_parts(untall(ge), unwide([gwo])),
        as_parts(untall([gw1[:, :D], gw1[:, D:]]), unwide([gw2[:D], gw2[D:]])),
        as_parts(untall(gs), unwide([gso])),
        as_parts(untall([gcq]), untall([gck, gcv]), unwide([gco])),
        as_parts(untall([gv1[:, :D], gv1[:, D:]]), unwide([gv2[:D], gv2[D:]])),
    ]
    return encl, low(dec), dx, dy, parts, jnp.stack(vg)


def one_hot(index, count, dtype):
    return (index[:, None] == lax.broadcasted_iota(jnp.int32, (1, count), 1)).astype(dtype)


def local(
    image_tokens,
    tag_tokens,
    image_cotangent,
    tag_cotangent,
    tag_lengths,
    slot_blocks,
    master_blocks,
    left_factor,
    right_factor,
    left_root,
    right_root,
    vector_master,
    vector_moment,
):
    dp = lax.axis_size("dp")
    shards = lax.axis_size("tensor")
    me = lax.axis_index("tensor")
    slots = master_blocks.shape[1]
    items = tag_lengths.shape[0]
    image_length = image_tokens.shape[0] * shards // items
    item_length = tag_tokens.shape[0] * shards // items
    lanes = vector_master.shape[1]
    total = CHUNK * CHUNKS

    def rows_of(value):
        return jnp.pad(value, ((0, 16 - value.shape[0]), (0, TILE - value.shape[1])))

    own = jnp.concatenate(
        [
            master_blocks.astype(BF16).reshape(slots * TILE, TILE),
            rows_of(vector_master.astype(BF16)),
        ],
        axis=0,
    )
    pieces = gather_pieces(own, dp)
    ranks = jnp.stack([relative_rank(p, dp) for p in range(dp)])
    by_rank = jnp.dot(
        one_hot(ranks, dp, F32),
        slot_blocks.reshape(dp, slots).astype(F32),
        precision=lax.Precision.HIGHEST,
    )
    tiles = order_tiles(pieces, by_rank.astype(jnp.int32).reshape(-1), slots)
    vector_list = jnp.stack([p[slots * TILE : slots * TILE + 10, :lanes] for p in pieces])
    vectors = jnp.einsum(
        "pr,pvl->vrl", one_hot(ranks, dp, BF16), vector_list, preferred_element_type=F32
    ).reshape(10, dp * lanes)
    weights = [
        gather_group(tiles[c * CHUNK * TILE : (c + 1) * CHUNK * TILE]) for c in range(CHUNKS)
    ]
    x = pull_rows(image_tokens, image_length)
    y = pull_rows(tag_tokens, item_length)
    xc = pull_rows(image_cotangent, image_length)
    yc = pull_rows(tag_cotangent, item_length)
    alive = me < items
    live = jnp.sum(jnp.where(lax.broadcasted_iota(jnp.int32, (items,), 0) == me, tag_lengths, 0))
    live = jnp.where(alive, live, 1)
    encoded, decoded, dx, dy, parts, vector_grads = compute(
        x, y, xc, yc, live, weights, vectors, alive
    )
    sums = [sum_group(p) for p in parts]
    vector_grads = sum_over_group(vector_grads).reshape(10, dp, lanes)
    targets = jnp.stack([target_rank(p, dp) for p in range(dp)])
    vector_rows = jnp.einsum(
        "pr,vrl->pvl",
        one_hot(targets, dp, F32),
        vector_grads,
        precision=lax.Precision.HIGHEST,
    )
    vector_rows = jnp.pad(vector_rows, ((0, 0), (0, 6), (0, TILE - lanes))).astype(BF16)
    slot_of_block = jnp.sum(
        jnp.where(
            slot_blocks[None, :] == lax.broadcasted_iota(jnp.int32, (total, 1), 0),
            lax.broadcasted_iota(jnp.int32, (1, dp * slots), 1),
            0,
        ),
        axis=1,
    )
    outgoing = deal_tiles(
        sums, vector_rows, slot_of_block, [target_rank(p, dp) for p in range(dp)], slots
    )
    summed = sum_pieces(outgoing, dp)
    dealt = summed[: slots * TILE].reshape(slots, TILE, TILE)
    own_blocks = lax.dynamic_slice_in_dim(slot_blocks, lax.axis_index("dp") * slots, slots)
    dealt = jnp.where((own_blocks < total)[:, None, None], dealt, 0.0)[None]
    vector_gradient = summed[slots * TILE : slots * TILE + 10, :lanes]
    highest = lax.Precision.HIGHEST
    left_updated = STAT_DECAY * left_factor + (1.0 - STAT_DECAY) * jnp.einsum(
        "asij,askj->asik", dealt, dealt, precision=highest
    )
    right_updated = STAT_DECAY * right_factor + (1.0 - STAT_DECAY) * jnp.einsum(
        "asji,asjk->asik", dealt, dealt, precision=highest
    )
    rotated = jnp.einsum("asij,asjk->asik", left_root, dealt, precision=highest)
    master_updated = master_blocks - MATRIX_RATE * jnp.einsum(
        "asij,asjk->asik", rotated, right_root, precision=highest
    )
    moment_updated = (
        STAT_DECAY * vector_moment + (1.0 - STAT_DECAY) * vector_gradient * vector_gradient
    )
    vector_updated = vector_master - VECTOR_RATE * vector_gradient / (
        jnp.sqrt(moment_updated) + 1e-08
    )
    return (
        push_rows(encoded, image_tokens.shape[0]),
        push_rows(decoded, tag_tokens.shape[0]),
        push_rows(dx.astype(BF16), image_tokens.shape[0]).astype(F32),
        push_rows(dy.astype(BF16), tag_tokens.shape[0]).astype(F32),
        dealt,
        left_updated,
        right_updated,
        master_updated,
        master_updated.astype(BF16),
        vector_gradient,
        moment_updated,
        vector_updated,
    )

def solution(mesh):
    in_specs = (
        P(("dp", "tensor"), None),
        P(("dp", "tensor"), None),
        P(("dp", "tensor"), None),
        P(("dp", "tensor"), None),
        P("dp"),
        P(),
        P("tensor", "dp", None, None),
        P("tensor", "dp", None, None),
        P("tensor", "dp", None, None),
        P("tensor", "dp", None, None),
        P("tensor", "dp", None, None),
        P(None, "dp"),
        P(None, "dp"),
    )
    out_specs = (
        P(("dp", "tensor"), None),
        P(("dp", "tensor"), None),
        P(("dp", "tensor"), None),
        P(("dp", "tensor"), None),
        P("tensor", "dp", None, None),
        P("tensor", "dp", None, None),
        P("tensor", "dp", None, None),
        P("tensor", "dp", None, None),
        P("tensor", "dp", None, None),
        P(None, "dp"),
        P(None, "dp"),
        P(None, "dp"),
    )
    return jax.shard_map(local, mesh=mesh, in_specs=in_specs, out_specs=out_specs, check_vma=False)
```

```python
import jax
import jax.numpy as jnp
from jax import lax
from jax.experimental import pallas as pl
from jax.experimental.pallas import tpu as pltpu
from jax.sharding import PartitionSpec as P

D = 512
HEADS = 8
HEAD_DIM = 64
FF = 1024
TILE = 128
CHUNK = 16
CHUNKS = 5

NORM_EPSILON = 1e-05
MATRIX_RATE = 0.5
VECTOR_RATE = 0.2
STAT_DECAY = 0.5
MASKED_SCORE = -1e30

F32 = jnp.float32
BF16 = jnp.bfloat16
ANY = pl.BlockSpec(memory_space=pl.ANY)
VM = pl.BlockSpec(memory_space=pltpu.VMEM)
SM = pl.BlockSpec(memory_space=pltpu.SMEM)


def core_pairs():
    return [(i, i ^ 1) for i in range(4)]


def chip_pairs():
    return [(i, i ^ 2) for i in range(4)]


def y_pairs():
    return [(i, i ^ 1) for i in range(8)]


def z_shift(step):
    return [(2 * z + y, 2 * ((z + step) % 4) + y) for z in range(4) for y in range(2)]


def relative_rank(position, size):
    me = lax.axis_index("dp")
    if size != 8:
        return jnp.int32(position)
    swapped, step = divmod(position, 4)
    return 2 * lax.rem(me // 2 - step + 4, 4) + lax.rem(me + swapped, 2)


def target_rank(position, size):
    me = lax.axis_index("dp")
    if size != 8:
        return jnp.int32(position)
    swapped, step = divmod(position, 4)
    return 2 * lax.rem(me // 2 + step, 4) + lax.rem(me + swapped, 2)


def gather_pieces(piece, size):
    if size != 8:
        return list(lax.all_gather(piece, "dp", axis=0, tiled=False))
    column = [piece] + [lax.ppermute(piece, "dp", z_shift(step)) for step in (1, 2, 3)]
    return column + [lax.ppermute(part, "dp", y_pairs()) for part in column]


def sum_pieces(pieces, size):
    if size != 8:
        whole = lax.psum_scatter(
            jnp.stack(pieces).astype(F32), "dp", scatter_dimension=0, tiled=False
        )
        return whole
    column = []
    for step in (1, 2, 3, 0):
        other = lax.ppermute(pieces[4 + step], "dp", y_pairs())
        both = pieces[step].astype(F32) + other.astype(F32)
        if step:
            column.append(lax.ppermute(both.astype(BF16), "dp", z_shift(step)).astype(F32))
        else:
            column.append(both)
    return (column[0] + column[1]) + (column[2] + column[3])


def gather_group(part):
    far = lax.ppermute(part, "tensor", chip_pairs())
    near = lax.ppermute(part, "tensor", core_pairs())
    far_near = lax.ppermute(far, "tensor", core_pairs())
    return (part, near, far, far_near)


def sum_group(parts):
    near = lax.ppermute(parts[1], "tensor", core_pairs())
    far_near = lax.ppermute(parts[3], "tensor", core_pairs())
    far = (parts[2].astype(F32) + far_near.astype(F32)).astype(BF16)
    far = lax.ppermute(far, "tensor", chip_pairs())
    return (parts[0].astype(F32) + near.astype(F32) + far.astype(F32)).astype(BF16)


def sum_over_group(value):
    value = value + lax.ppermute(value, "tensor", core_pairs())
    return value + lax.ppermute(value, "tensor", chip_pairs())


def pull_rows(rows, length):
    shards = lax.axis_size("tensor")
    later = lax.ppermute(rows, "tensor", [(i + 1, i) for i in range(shards - 1)])
    start = lax.axis_index("tensor") * (length - rows.shape[0])
    return lax.dynamic_slice_in_dim(jnp.concatenate([rows, later], axis=0), start, length, axis=0)


def push_rows(item, count):
    shards = lax.axis_size("tensor")
    length = item.shape[0]
    earlier = lax.ppermute(
        item[length - count :], "tensor", [(i, i + 1) for i in range(shards - 1)]
    )
    start = count - lax.axis_index("tensor") * (length - count)
    return lax.dynamic_slice_in_dim(
        jnp.concatenate([earlier, item[:count]], axis=0), start, count, axis=0
    )


def order_tiles(pieces, block_ids, slots):
    total = CHUNK * CHUNKS

    def kernel(ids, *refs):
        sources, out = refs[:-1], refs[-1]
        for p, source in enumerate(sources):
            for j in range(slots):
                block = ids[0, p * slots + j]

                @pl.when(block < total)
                def _(source=source, j=j, block=block):
                    out[pl.ds(pl.multiple_of(block * TILE, TILE), TILE), :] = source[
                        j * TILE : (j + 1) * TILE, :
                    ]

    return pl.pallas_call(
        kernel,
        out_shape=jax.ShapeDtypeStruct((total * TILE, TILE), BF16),
        in_specs=[SM] + [VM] * len(pieces),
        out_specs=VM,
        compiler_params=pltpu.CompilerParams(vmem_limit_bytes=40 * 2**20),
        name="order_tiles",
    )(block_ids, *pieces)


def deal_tiles(chunks, vector_rows, block_ids, slots):
    count = vector_rows.shape[0]
    extra = vector_rows.shape[1]
    total = CHUNK * CHUNKS
    rows = slots * TILE + extra

    def kernel(ids, *refs):
        sources, more = refs[:CHUNKS], refs[CHUNKS]
        outs, held = refs[CHUNKS + 1 : -1], refs[-1]
        for c, source in enumerate(sources):
            held[c * CHUNK * TILE : (c + 1) * CHUNK * TILE, :] = source[...]
        held[total * TILE :, :] = jnp.zeros((TILE, TILE), BF16)
        for p, out in enumerate(outs):
            for j in range(slots):
                block = jnp.minimum(ids[0, p * slots + j], total)
                out[j * TILE : (j + 1) * TILE, :] = held[
                    pl.ds(pl.multiple_of(block * TILE, TILE), TILE), :
                ]
            out[slots * TILE :, :] = more[p]

    return pl.pallas_call(
        kernel,
        out_shape=[jax.ShapeDtypeStruct((rows, TILE), BF16)] * count,
        in_specs=[SM] + [VM] * (CHUNKS + 1),
        out_specs=[VM] * count,
        scratch_shapes=[pltpu.VMEM(((total + 1) * TILE, TILE), BF16)],
        compiler_params=pltpu.CompilerParams(vmem_limit_bytes=40 * 2**20),
        name="deal_tiles",
    )(block_ids, *chunks, vector_rows)


LOG2E = 1.4426950408889634
SCORE_SCALE = HEAD_DIM ** (-0.5)
SCORE_LOG2 = SCORE_SCALE * LOG2E
PAIRS = HEADS // 2


def matmul(former, latter):
    return jnp.dot(former, latter, preferred_element_type=F32)


def times_transpose(former, latter):
    return lax.dot_general(former, latter, (((1,), (1,)), ((), ())), preferred_element_type=F32)


def transpose_times(former, latter):
    return lax.dot_general(former, latter, (((0,), (0,)), ((), ())), preferred_element_type=F32)


def low(value):
    return value.astype(BF16)


def tile_at(part, index):
    return part[index * TILE : (index + 1) * TILE, :]


def column_matrix(parts, first, count, column):
    return jnp.concatenate(
        [
            jnp.concatenate([tile_at(p, first + a * count + column) for p in parts], axis=1)
            for a in range(4)
        ],
        axis=0,
    )


def row_matrix(parts, first, group):
    return jnp.concatenate(
        [
            jnp.concatenate([tile_at(p, first + 4 * group + b) for b in range(4)], axis=1)
            for p in parts
        ],
        axis=0,
    )


def store_columns(parts, gradient, first, count, column):
    for r, part in enumerate(parts):
        for a in range(4):
            at = (first + a * count + column) * TILE
            part[at : at + TILE, :] = low(
                gradient[a * TILE : (a + 1) * TILE, r * TILE : (r + 1) * TILE]
            )


def store_rows(parts, gradient, first, group):
    for r, part in enumerate(parts):
        for b in range(4):
            at = (first + 4 * group + b) * TILE
            part[at : at + TILE, :] = low(
                gradient[r * TILE : (r + 1) * TILE, b * TILE : (b + 1) * TILE]
            )


def spans(count):
    half = (count // 2 + 15) // 16 * 16
    return [(0, half), (half, count)]


def norm_rows(value):
    mean = jnp.mean(value, axis=-1, keepdims=True)
    centered = value - mean
    scale = lax.rsqrt(jnp.mean(centered * centered, axis=-1, keepdims=True) + NORM_EPSILON)
    return centered * scale, scale


def norm_back(gradient, normed, scale, gain):
    scaled = gradient * gain
    return scale * (
        scaled
        - jnp.mean(scaled, axis=-1, keepdims=True)
        - normed * jnp.mean(scaled * normed, axis=-1, keepdims=True)
    )


def gate_both(value):
    size = jnp.abs(value) * (0.5**0.5)
    turn = 1.0 / (1.0 + 0.3275911 * size)
    bell = jnp.exp2(value * value * (-0.5 * LOG2E))
    series = turn * (
        0.254829592
        + turn * (-0.284496736 + turn * (1.421413741 + turn * (-1.453152027 + turn * 1.061405429)))
    )
    tail = 0.5 * series * bell
    phi = jnp.where(value < 0, tail, 1.0 - tail)
    return value * phi, phi + value * bell * 0.3989422804014327


def half_mask(which):
    lane = lax.broadcasted_iota(jnp.int32, (1, TILE), 1)
    return (lane < HEAD_DIM) if which == 0 else (lane >= HEAD_DIM)


def attend_pairs(q_ref, k_ref, v_ref, o_ref, stat_ref, bias):
    count = q_ref.shape[0]
    keys = k_ref.shape[0]
    ones = jnp.ones((keys, TILE), BF16)
    lane = lax.broadcasted_iota(jnp.int32, (count, TILE), 1)
    stats = jnp.zeros((count, TILE), F32)
    for pair in range(PAIRS):
        cut = slice(pair * TILE, (pair + 1) * TILE)
        queries, key_rows = q_ref[:, cut], k_ref[:, cut]
        values = jnp.concatenate([v_ref[:, cut], ones], axis=1)
        mixed = []
        for which in range(2):
            masked = jnp.where(half_mask(which), queries, jnp.zeros_like(queries))
            scores = times_transpose(masked, key_rows) * SCORE_LOG2
            if bias is not None:
                scores = scores + bias
            top = jnp.max(scores, axis=1, keepdims=True)
            weights = low(jnp.exp2(scores - top))
            both = matmul(weights, values)
            total = both[:, TILE:]
            mixed.append(both[:, :TILE] / total)
            stats = jnp.where(lane == 2 * pair + which, top + jnp.log2(total), stats)
        o_ref[:, cut] = low(jnp.where(half_mask(0), mixed[0], mixed[1]))
    stat_ref[...] = stats.T


def attend_pairs_back(q_ref, k_ref, v_ref, stat_ref, do_ref, delta, dq_ref, dk_ref, dv_ref, kt_ref, dqt_ref, bias):
    kt_ref[...] = k_ref[...].T
    for pair in range(PAIRS):
        cut = slice(pair * TILE, (pair + 1) * TILE)
        queries, key_rows, value_rows, incoming = q_ref[:, cut], k_ref[:, cut], v_ref[:, cut], do_ref[:, cut]
        dk = dv = None
        for which in range(2):
            head = 2 * pair + which
            mask = half_mask(which)
            q_one = jnp.where(mask, queries, jnp.zeros_like(queries))
            do_one = jnp.where(mask, incoming, jnp.zeros_like(incoming))
            scores = times_transpose(key_rows, q_one) * SCORE_LOG2
            if bias is not None:
                scores = scores + bias
            weights = jnp.exp2(scores - stat_ref[head : head + 1, :])
            d_weights = times_transpose(value_rows, do_one)
            d_scores = low(weights * (d_weights - delta[head : head + 1, :]))
            dv_one = matmul(low(weights), do_one)
            dk_one = matmul(d_scores, q_one)
            dv = dv_one if dv is None else dv + dv_one
            dk = dk_one if dk is None else dk + dk_one
            rows = slice(head * HEAD_DIM, (head + 1) * HEAD_DIM)
            dqt_ref[rows, :] = low(matmul(kt_ref[rows, :], d_scores) * SCORE_SCALE)
        dk_ref[:, cut] = low(dk * SCORE_SCALE)
        dv_ref[:, cut] = low(dv)
    dq_ref[...] = dqt_ref[...].T


def row_products(incoming, mixed):
    product = incoming * mixed
    first = low(product)
    rest = low(product - first.astype(F32))
    lane = lax.broadcasted_iota(jnp.int32, (TILE, D), 1) // HEAD_DIM
    row = lax.broadcasted_iota(jnp.int32, (TILE, D), 0)
    pick = (lane == row).astype(BF16)
    return times_transpose(pick, first) + times_transpose(pick, rest)


def struct(shape, dtype):
    return jax.ShapeDtypeStruct(shape, dtype)


def call(kernel, name, outs, scratch, *args, flops=0):
    return pl.pallas_call(
        kernel,
        out_shape=outs,
        in_specs=[pl.BlockSpec(memory_space=pltpu.SMEM) if a.dtype == jnp.int32 else VM for a in args],
        out_specs=[VM] * len(outs),
        scratch_shapes=scratch,
        compiler_params=pltpu.CompilerParams(vmem_limit_bytes=60 * 2**20),
        cost_estimate=pl.CostEstimate(flops=flops, bytes_accessed=4000000, transcendentals=0),
        name=name,
    )(*args)


def part_outs():
    return [struct((CHUNK * TILE, TILE), BF16)] * 4


def causal_bias(count, live, queries_on_rows):
    a = lax.broadcasted_iota(jnp.int32, (count, count), 0)
    b = lax.broadcasted_iota(jnp.int32, (count, count), 1)
    query, key = (a, b) if queries_on_rows else (b, a)
    return jnp.where((key <= query) & (key < live), 0.0, MASKED_SCORE)


def self_forward(x, parts, vectors, norm, live=None):
    rows = x.shape[0]

    def kernel(*refs):
        if live is not None:
            live_ref, *refs = refs
        x_ref, p0, p1, p2, p3, g_ref, first_ref, hat_ref, scale_ref, q_ref, k_ref, v_ref, o_ref, stat_ref = refs
        ps = (p0, p1, p2, p3)
        tokens = x_ref[...]
        for column, ref in enumerate((q_ref, k_ref, v_ref)):
            ref[...] = low(matmul(tokens, column_matrix(ps, 0, 3, column)))
        bias = None if live is None else causal_bias(rows, live_ref[0, 0], True)
        attend_pairs(q_ref, k_ref, v_ref, o_ref, stat_ref, bias)
        hat, scale = norm_rows(
            tokens.astype(F32) + matmul(o_ref[...], row_matrix(ps, 12, 0))
        )
        first_ref[...] = hat * g_ref[2 * norm : 2 * norm + 1, :] + g_ref[2 * norm + 1 : 2 * norm + 2, :]
        hat_ref[...] = low(hat)
        scale_ref[...] = scale

    outs = [struct((rows, D), F32), struct((rows, D), BF16), struct((rows, 1), F32)]
    outs += [struct((rows, D), BF16)] * 4 + [struct((TILE, rows), F32)]
    args = ([] if live is None else [live]) + [x, *parts, vectors]
    return call(kernel, f"self_forward_{norm}", outs, [], *args, flops=10**10)


def ffn_rows(rows_in, w1, w2):
    hid, slope, out = [], [], []
    for a, b in spans(rows_in.shape[0]):
        value, derivative = gate_both(matmul(rows_in[a:b], w1))
        value = low(value)
        hid.append(value)
        slope.append(low(derivative))
        out.append(matmul(value, w2))
    return hid, slope, out


def ffn_weights(ps):
    w1 = jnp.concatenate([column_matrix(ps, 0, 2, c) for c in range(2)], axis=1)
    w2 = jnp.concatenate([row_matrix(ps, 8, c) for c in range(2)], axis=0)
    return w1, w2


def unpack_hidden():
    pass


def ffn_forward(first, parts, vectors, norm):
    rows = first.shape[0]

    def kernel(f_ref, p0, p1, p2, p3, g_ref, enc_ref, hat_ref, scale_ref, hid_ref, slope_ref):
        w1, w2 = ffn_weights((p0, p1, p2, p3))
        for a, b in spans(rows):
            first_rows = f_ref[a:b, :]
            value, slope = gate_both(matmul(low(first_rows), w1))
            value = low(value)
            hid_ref[a:b, :] = value
            slope_ref[a:b, :] = low(slope)
            hat, scale = norm_rows(first_rows + matmul(value, w2))
            enc_ref[a:b, :] = low(hat * g_ref[2 * norm : 2 * norm + 1, :] + g_ref[2 * norm + 1 : 2 * norm + 2, :])
            hat_ref[a:b, :] = low(hat)
            scale_ref[a:b, :] = scale

    outs = [struct((rows, D), BF16), struct((rows, D), BF16), struct((rows, 1), F32)]
    outs += [struct((rows, FF), BF16)] * 2
    return call(kernel, f"ffn_forward_{norm}", outs, [], first, *parts, vectors, flops=3 * 10**9)


def cross_forward(second, encoded, parts, vectors):
    rows, keys = second.shape[0], encoded.shape[0]

    def kernel(s_ref, e_ref, p0, p1, p2, p3, g_ref, third_ref, hat_ref, scale_ref, q_ref, k_ref, v_ref, o_ref, stat_ref):
        ps = (p0, p1, p2, p3)
        q_ref[...] = low(matmul(low(s_ref[...]), column_matrix(ps, 0, 1, 0)))
        k_ref[...] = low(matmul(e_ref[...], column_matrix(ps, 4, 2, 0)))
        v_ref[...] = low(matmul(e_ref[...], column_matrix(ps, 4, 2, 1)))
        attend_pairs(q_ref, k_ref, v_ref, o_ref, stat_ref, None)
        hat, scale = norm_rows(s_ref[...] + matmul(o_ref[...], row_matrix(ps, 12, 0)))
        third_ref[...] = hat * g_ref[6:7, :] + g_ref[7:8, :]
        hat_ref[...] = low(hat)
        scale_ref[...] = scale

    outs = [struct((rows, D), F32), struct((rows, D), BF16), struct((rows, 1), F32)]
    outs += [struct((rows, D), BF16), struct((keys, D), BF16), struct((keys, D), BF16)]
    outs += [struct((rows, D), BF16), struct((TILE, rows), F32)]
    return call(kernel, "cross_forward", outs, [], second, encoded, *parts, vectors, flops=5 * 10**9)


def store_norm(ref, gradient, hat):
    ref[0:1, :] = jnp.sum(gradient * hat, axis=0, keepdims=True)
    ref[1:2, :] = jnp.sum(gradient, axis=0, keepdims=True)


def ffn_both(third, cotangent, live, parts, vectors):
    rows = third.shape[0]

    def kernel(live_ref, t_ref, c_ref, p0, p1, p2, p3, g_ref, dec_ref, back_ref, n_ref, d0, d1, d2, d3, hid_ref, dh_ref, db_ref):
        w1, w2 = ffn_weights((p0, p1, p2, p3))
        grads = (d0, d1, d2, d3)
        gain = g_ref[8:9, :]
        for part, (a, b) in enumerate(spans(rows)):
            third_rows = t_ref[a:b, :]
            value, slope = gate_both(matmul(low(third_rows), w1))
            value = low(value)
            hid_ref[a:b, :] = value
            hat, scale = norm_rows(third_rows + matmul(value, w2))
            dec_ref[a:b, :] = low(hat * gain + g_ref[9:10, :])
            row = lax.broadcasted_iota(jnp.int32, (b - a, 1), 0) + a
            incoming = jnp.where(row < live_ref[0, 0], c_ref[a:b, :].astype(F32), 0.0)
            if part == 0:
                n_ref[...] = jnp.zeros_like(n_ref)
            n_ref[0:1, :] += jnp.sum(incoming * hat, axis=0, keepdims=True)
            n_ref[1:2, :] += jnp.sum(incoming, axis=0, keepdims=True)
            back = norm_back(incoming, hat, scale, gain)
            back_low = low(back)
            db_ref[a:b, :] = back_low
            dh = low(slope * times_transpose(back_low, w2))
            dh_ref[a:b, :] = dh
            back_ref[a:b, :] = back + times_transpose(dh, w1)
        third_low = low(t_ref[...])
        for c in range(2):
            store_columns(grads, transpose_times(third_low, dh_ref[:, c * D : (c + 1) * D]), 0, 2, c)
            store_rows(grads, transpose_times(hid_ref[:, c * D : (c + 1) * D], db_ref[...]), 8, c)

    outs = [struct((rows, D), BF16), struct((rows, D), F32), struct((8, D), F32)] + part_outs()
    scratch = [pltpu.VMEM((rows, FF), BF16), pltpu.VMEM((rows, FF), BF16), pltpu.VMEM((rows, D), BF16)]
    return call(kernel, "ffn_both", outs, scratch, live, third, cotangent, *parts, vectors, flops=10**10)


def ffn_backward(cotangent, more, hat, scale, first, hid, slope, parts, vectors, norm):
    rows = first.shape[0]

    def kernel(c_ref, m_ref, h_ref, s_ref, f_ref, hid_ref, slope_ref, p0, p1, p2, p3, g_ref, back_ref, n_ref, d0, d1, d2, d3, dh_ref, db_ref):
        w1, w2 = ffn_weights((p0, p1, p2, p3))
        grads = (d0, d1, d2, d3)
        n_ref[...] = jnp.zeros_like(n_ref)
        for a, b in spans(rows):
            incoming = c_ref[a:b, :].astype(F32) + m_ref[a:b, :]
            hat_rows = h_ref[a:b, :].astype(F32)
            n_ref[0:1, :] += jnp.sum(incoming * hat_rows, axis=0, keepdims=True)
            n_ref[1:2, :] += jnp.sum(incoming, axis=0, keepdims=True)
            back = norm_back(incoming, hat_rows, s_ref[a:b, :], g_ref[2 * norm : 2 * norm + 1, :])
            back_low = low(back)
            db_ref[a:b, :] = back_low
            dh = low(slope_ref[a:b, :].astype(F32) * times_transpose(back_low, w2))
            dh_ref[a:b, :] = dh
            back_ref[a:b, :] = back + times_transpose(dh, w1)
        first_low = low(f_ref[...])
        for c in range(2):
            store_columns(grads, transpose_times(first_low, dh_ref[:, c * D : (c + 1) * D]), 0, 2, c)
            store_rows(grads, transpose_times(hid_ref[:, c * D : (c + 1) * D], db_ref[...]), 8, c)

    outs = [struct((rows, D), F32), struct((8, D), F32)] + part_outs()
    scratch = [pltpu.VMEM((rows, FF), BF16), pltpu.VMEM((rows, D), BF16)]
    return call(kernel, f"ffn_backward_{norm}", outs, scratch, cotangent, more, hat, scale, first, hid, slope, *parts, vectors, flops=10**10)


def self_backward(back, hat, scale, x, q, k, v, o, stats, parts, vectors, norm, live=None):
    rows = x.shape[0]

    def kernel(*refs):
        if live is not None:
            live_ref, *refs = refs
        (b_ref, h_ref, s_ref, x_ref, q_ref, k_ref, v_ref, o_ref, stat_ref, p0, p1, p2, p3, g_ref,
         dx_ref, n_ref, d0, d1, d2, d3, do_ref, dq_ref, dk_ref, dv_ref, kt_ref, dqt_ref) = refs
        ps, grads = (p0, p1, p2, p3), (d0, d1, d2, d3)
        incoming = b_ref[...]
        hat_rows = h_ref[...].astype(F32)
        n_ref[...] = jnp.zeros_like(n_ref)
        store_norm(n_ref, incoming, hat_rows)
        branch = norm_back(incoming, hat_rows, s_ref[...], g_ref[2 * norm : 2 * norm + 1, :])
        branch_low = low(branch)
        dx_ref[...] = branch
        do = low(times_transpose(branch_low, row_matrix(ps, 12, 0)))
        do_ref[...] = do
        store_rows(grads, transpose_times(o_ref[...], branch_low), 12, 0)
        delta = row_products(do.astype(F32), o_ref[...].astype(F32))
        bias = None if live is None else causal_bias(rows, live_ref[0, 0], False)
        attend_pairs_back(q_ref, k_ref, v_ref, stat_ref, do_ref, delta, dq_ref, dk_ref, dv_ref, kt_ref, dqt_ref, bias)
        xt = x_ref[...].T
        total = dx_ref[...]
        for column, ref in enumerate((dq_ref, dk_ref, dv_ref)):
            total = total + times_transpose(ref[...], column_matrix(ps, 0, 3, column))
            store_columns(grads, matmul(xt, ref[...]), 0, 3, column)
        dx_ref[...] = total

    outs = [struct((rows, D), F32), struct((8, D), F32)] + part_outs()
    scratch = [pltpu.VMEM((rows, D), BF16)] * 4 + [pltpu.VMEM((D, rows), BF16)] * 2
    args = ([] if live is None else [live]) + [back, hat, scale, x, q, k, v, o, stats, *parts, vectors]
    return call(kernel, f"self_backward_{norm}", outs, scratch, *args, flops=2 * 10**10)


def cross_backward(back, hat, scale, second, encoded, q, k, v, o, stats, parts, vectors):
    rows, keys = second.shape[0], encoded.shape[0]

    def kernel(b_ref, h_ref, s_ref, x_ref, e_ref, q_ref, k_ref, v_ref, o_ref, stat_ref, p0, p1, p2, p3, g_ref,
               dx_ref, de_ref, n_ref, d0, d1, d2, d3, do_ref, dq_ref, dk_ref, dv_ref, kt_ref, dqt_ref):
        ps, grads = (p0, p1, p2, p3), (d0, d1, d2, d3)
        incoming = b_ref[...]
        hat_rows = h_ref[...].astype(F32)
        n_ref[...] = jnp.zeros_like(n_ref)
        store_norm(n_ref, incoming, hat_rows)
        branch = norm_back(incoming, hat_rows, s_ref[...], g_ref[6:7, :])
        branch_low = low(branch)
        do = low(times_transpose(branch_low, row_matrix(ps, 12, 0)))
        do_ref[...] = do
        store_rows(grads, transpose_times(o_ref[...], branch_low), 12, 0)
        delta = row_products(do.astype(F32), o_ref[...].astype(F32))
        attend_pairs_back(q_ref, k_ref, v_ref, stat_ref, do_ref, delta, dq_ref, dk_ref, dv_ref, kt_ref, dqt_ref, None)
        dx_ref[...] = branch + times_transpose(dq_ref[...], column_matrix(ps, 0, 1, 0))
        de_ref[...] = times_transpose(dk_ref[...], column_matrix(ps, 4, 2, 0)) + times_transpose(
            dv_ref[...], column_matrix(ps, 4, 2, 1)
        )
        store_columns(grads, transpose_times(low(x_ref[...]), dq_ref[...]), 0, 1, 0)
        et = e_ref[...].T
        store_columns(grads, matmul(et, dk_ref[...]), 4, 2, 0)
        store_columns(grads, matmul(et, dv_ref[...]), 4, 2, 1)

    outs = [struct((rows, D), F32), struct((keys, D), F32), struct((8, D), F32)] + part_outs()
    scratch = [pltpu.VMEM((rows, D), BF16)] * 2 + [pltpu.VMEM((keys, D), BF16)] * 2
    scratch += [pltpu.VMEM((D, keys), BF16), pltpu.VMEM((D, rows), BF16)]
    return call(kernel, "cross_backward", outs, scratch, back, hat, scale, second, encoded, q, k, v, o, stats, *parts, vectors, flops=2 * 10**10)


def compute(x, y, xc, yc, live, weights, vectors, alive):
    xc = jnp.where(alive, xc, jnp.zeros_like(xc))
    live_tags = jnp.where(alive, live, 0).reshape(1, 1)
    live = live.reshape(1, 1)
    first, hat0, scale0, q, k, v, o, stat = self_forward(x, weights[0], vectors, 0)
    encoded, hat1, scale1, hid, slope = ffn_forward(first, weights[1], vectors, 1)
    second, hat2, scale2, q2, k2, v2, o2, stat2 = self_forward(y, weights[2], vectors, 2, live)
    third, hat3, scale3, q3, k3, v3, o3, stat3 = cross_forward(second, encoded, weights[3], vectors)
    decoded, back, n4, *parts4 = ffn_both(third, yc, live_tags, weights[4], vectors)
    back, d_encoded, n3, *parts3 = cross_backward(
        back, hat3, scale3, second, encoded, q3, k3, v3, o3, stat3, weights[3], vectors
    )
    dy, n2, *parts2 = self_backward(back, hat2, scale2, y, q2, k2, v2, o2, stat2, weights[2], vectors, 2, live)
    back, n1, *parts1 = ffn_backward(xc, d_encoded, hat1, scale1, first, hid, slope, weights[1], vectors, 1)
    dx, n0, *parts0 = self_backward(back, hat0, scale0, x, q, k, v, o, stat, weights[0], vectors, 0)
    grads = jnp.concatenate([n[:2] for n in (n0, n1, n2, n3, n4)], axis=0)
    return encoded, decoded, dx, dy, [parts0, parts1, parts2, parts3, parts4], grads


def one_hot(index, count, dtype):
    return (index[:, None] == lax.broadcasted_iota(jnp.int32, (1, count), 1)).astype(dtype)


def local(
    image_tokens,
    tag_tokens,
    image_cotangent,
    tag_cotangent,
    tag_lengths,
    slot_blocks,
    master_blocks,
    left_factor,
    right_factor,
    left_root,
    right_root,
    vector_master,
    vector_moment,
):
    dp = lax.axis_size("dp")
    shards = lax.axis_size("tensor")
    me = lax.axis_index("tensor")
    slots = master_blocks.shape[1]
    items = tag_lengths.shape[0]
    image_length = image_tokens.shape[0] * shards // items
    item_length = tag_tokens.shape[0] * shards // items
    lanes = vector_master.shape[1]
    def rows_of(value):
        return jnp.pad(value, ((0, 16 - value.shape[0]), (0, TILE - value.shape[1])))

    own = jnp.concatenate(
        [
            master_blocks.astype(BF16).reshape(slots * TILE, TILE),
            rows_of(vector_master.astype(BF16)),
        ],
        axis=0,
    )
    pieces = gather_pieces(own, dp)
    ranks = jnp.stack([relative_rank(p, dp) for p in range(dp)])

    def blocks_of(those):
        picked = one_hot(those, dp, jnp.int32)[:, :, None] * slot_blocks.reshape(1, dp, slots)
        return jnp.sum(picked, axis=1).reshape(1, dp * slots)

    tiles = order_tiles(pieces, blocks_of(ranks), slots)
    vector_list = jnp.stack([p[slots * TILE : slots * TILE + 10, :lanes] for p in pieces])
    vectors = jnp.einsum(
        "pr,pvl->vrl", one_hot(ranks, dp, BF16), vector_list, preferred_element_type=F32
    ).reshape(10, dp * lanes)
    weights = [
        gather_group(tiles[c * CHUNK * TILE : (c + 1) * CHUNK * TILE]) for c in range(CHUNKS)
    ]
    x = pull_rows(image_tokens, image_length)
    y = pull_rows(tag_tokens, item_length)
    xc = pull_rows(image_cotangent, image_length)
    yc = pull_rows(tag_cotangent, item_length)
    alive = me < items
    live = jnp.sum(jnp.where(lax.broadcasted_iota(jnp.int32, (items,), 0) == me, tag_lengths, 0))
    live = jnp.where(alive, live, 1)
    encoded, decoded, dx, dy, parts, vector_grads = compute(
        x, y, xc, yc, live, weights, vectors, alive
    )
    sums = [sum_group(p) for p in parts]
    vector_grads = sum_over_group(vector_grads).reshape(10, dp, lanes)
    targets = jnp.stack([target_rank(p, dp) for p in range(dp)])
    vector_rows = jnp.einsum(
        "pr,vrl->pvl",
        one_hot(targets, dp, F32),
        vector_grads,
        precision=lax.Precision.HIGHEST,
    )
    vector_rows = jnp.pad(vector_rows, ((0, 0), (0, 6), (0, TILE - lanes))).astype(BF16)
    outgoing = deal_tiles(sums, vector_rows, blocks_of(targets), slots)
    summed = sum_pieces(outgoing, dp)
    dealt = summed[: slots * TILE].reshape(slots, TILE, TILE)
    dealt = dealt[None]
    vector_gradient = summed[slots * TILE : slots * TILE + 10, :lanes]
    highest = lax.Precision.HIGHEST
    left_updated = STAT_DECAY * left_factor + (1.0 - STAT_DECAY) * jnp.einsum(
        "asij,askj->asik", dealt, dealt, precision=highest
    )
    right_updated = STAT_DECAY * right_factor + (1.0 - STAT_DECAY) * jnp.einsum(
        "asji,asjk->asik", dealt, dealt, precision=highest
    )
    rotated = jnp.einsum("asij,asjk->asik", left_root, dealt, precision=highest)
    master_updated = master_blocks - MATRIX_RATE * jnp.einsum(
        "asij,asjk->asik", rotated, right_root, precision=highest
    )
    moment_updated = (
        STAT_DECAY * vector_moment + (1.0 - STAT_DECAY) * vector_gradient * vector_gradient
    )
    vector_updated = vector_master - VECTOR_RATE * vector_gradient / (
        jnp.sqrt(moment_updated) + 1e-08
    )
    return (
        push_rows(encoded, image_tokens.shape[0]),
        push_rows(decoded, tag_tokens.shape[0]),
        push_rows(dx.astype(BF16), image_tokens.shape[0]).astype(F32),
        push_rows(dy.astype(BF16), tag_tokens.shape[0]).astype(F32),
        dealt,
        left_updated,
        right_updated,
        master_updated,
        master_updated.astype(BF16),
        vector_gradient,
        moment_updated,
        vector_updated,
    )

def solution(mesh):
    in_specs = (
        P(("dp", "tensor"), None),
        P(("dp", "tensor"), None),
        P(("dp", "tensor"), None),
        P(("dp", "tensor"), None),
        P("dp"),
        P(),
        P("tensor", "dp", None, None),
        P("tensor", "dp", None, None),
        P("tensor", "dp", None, None),
        P("tensor", "dp", None, None),
        P("tensor", "dp", None, None),
        P(None, "dp"),
        P(None, "dp"),
    )
    out_specs = (
        P(("dp", "tensor"), None),
        P(("dp", "tensor"), None),
        P(("dp", "tensor"), None),
        P(("dp", "tensor"), None),
        P("tensor", "dp", None, None),
        P("tensor", "dp", None, None),
        P("tensor", "dp", None, None),
        P("tensor", "dp", None, None),
        P("tensor", "dp", None, None),
        P(None, "dp"),
        P(None, "dp"),
        P(None, "dp"),
    )
    return jax.shard_map(local, mesh=mesh, in_specs=in_specs, out_specs=out_specs, check_vma=False)
```

```python
import jax
import jax.numpy as jnp
from jax import lax
from jax.experimental import pallas as pl
from jax.experimental.pallas import tpu as pltpu
from jax.sharding import PartitionSpec as P

D = 512
HEADS = 8
HEAD_DIM = 64
FF = 1024
TILE = 128
CHUNK = 16
CHUNKS = 5

NORM_EPSILON = 1e-05
MATRIX_RATE = 0.5
VECTOR_RATE = 0.2
STAT_DECAY = 0.5
MASKED_SCORE = -1e30

F32 = jnp.float32
BF16 = jnp.bfloat16
ANY = pl.BlockSpec(memory_space=pl.ANY)
VM = pl.BlockSpec(memory_space=pltpu.VMEM)
SM = pl.BlockSpec(memory_space=pltpu.SMEM)
HB = pl.BlockSpec(memory_space=pltpu.HBM)


def core_pairs():
    return [(i, i ^ 1) for i in range(4)]


def chip_pairs():
    return [(i, i ^ 2) for i in range(4)]


def y_pairs():
    return [(i, i ^ 1) for i in range(8)]


def z_shift(step):
    return [(2 * z + y, 2 * ((z + step) % 4) + y) for z in range(4) for y in range(2)]


def relative_rank(position, size):
    me = lax.axis_index("dp")
    if size != 8:
        return jnp.int32(position)
    swapped, step = divmod(position, 4)
    return 2 * lax.rem(me // 2 - step + 4, 4) + lax.rem(me + swapped, 2)


def target_rank(position, size):
    me = lax.axis_index("dp")
    if size != 8:
        return jnp.int32(position)
    swapped, step = divmod(position, 4)
    return 2 * lax.rem(me // 2 + step, 4) + lax.rem(me + swapped, 2)


def gather_pieces(piece, size):
    if size != 8:
        return list(lax.all_gather(piece, "dp", axis=0, tiled=False))
    z = {step: lax.ppermute(piece, "dp", z_shift(step)) for step in (1, 2, 3)}
    other = lax.ppermute(piece, "dp", y_pairs())
    y3 = lax.ppermute(lax.optimization_barrier((z[3], other))[0], "dp", y_pairs())
    y1 = lax.ppermute(lax.optimization_barrier((z[1], other))[0], "dp", y_pairs())
    y2 = lax.ppermute(lax.optimization_barrier((z[2], y3))[0], "dp", y_pairs())
    return [piece, z[1], z[2], z[3], other, y1, y2, y3]


def sum_pieces(pieces, size):
    if size != 8:
        whole = lax.psum_scatter(
            jnp.stack(pieces).astype(F32), "dp", scatter_dimension=0, tiled=False
        )
        return [whole.astype(BF16)], pieces[0]
    column, ready, mark = [pieces[0]], [], None
    for at, step in enumerate((2, 1, 3, 0)):
        piece = pieces[4 + step]
        if at > 1:
            piece = lax.optimization_barrier((piece, ready[at - 2]))[0]
        other = lax.ppermute(piece, "dp", y_pairs())
        if step == 0:
            column.append(other)
            continue
        both = (pieces[step].astype(F32) + other.astype(F32)).astype(BF16)
        ready.append(both)
        column.append(lax.ppermute(both, "dp", z_shift(step)))
    return column, pieces[0]


def send_near(part):
    return lax.ppermute(part[1], "tensor", core_pairs())


def sum_far(part, near):
    rows = CHUNK * TILE
    return (part[2].astype(F32) + near[rows : rows + part[2].shape[0]].astype(F32)).astype(BF16)


def send_far(value):
    return lax.ppermute(value, "tensor", chip_pairs())


def pull_rows(arrays, lengths, me, keep):
    shards = lax.axis_size("tensor")
    later = lax.ppermute(
        jnp.concatenate(arrays, axis=0), "tensor", [(i + 1, i) for i in range(shards - 1)]
    )
    n = len(arrays)

    def kernel(me_ref, *refs):
        owns, more, outs = refs[:n], refs[n], refs[n + 1 :]
        for t in range(shards):

            @pl.when(me_ref[0, 0] == t)
            def _(t=t):
                first = 0
                for own, out, length in zip(owns, outs, lengths):
                    rows = own.shape[0]
                    first += rows
                    if t == shards - 1:
                        if keep:
                            both = jnp.concatenate([own[...].astype(F32), own[...].astype(F32)[: length - rows, :]], axis=0)
                        else:
                            both = jnp.zeros(out.shape, F32)
                    else:
                        start = (length - rows) * t
                        both = jnp.concatenate(
                            [
                                own[...].astype(F32)[start:, :],
                                more[...].astype(F32)[first - rows : first - rows + length - rows + start, :],
                            ],
                            axis=0,
                        )
                    out[...] = both.astype(BF16)

    return pl.pallas_call(
        kernel,
        out_shape=[jax.ShapeDtypeStruct((length, D), BF16) for length in lengths],
        in_specs=[SM] + [VM] * (n + 1),
        out_specs=[VM] * n,
        compiler_params=pltpu.CompilerParams(vmem_limit_bytes=24 * 2**20),
        name="pull_rows",
    )(me, *arrays, later)


def push_rows(items, tails, counts, dtypes, me):
    shards = lax.axis_size("tensor")
    earlier = [
        lax.ppermute(a, "tensor", [(i, i + 1) for i in range(shards - 1)]) for a in tails
    ]
    n = len(items)

    def kernel(me_ref, *refs):
        owns, befores, outs = refs[:n], refs[n : 2 * n], refs[2 * n :]
        for t in range(shards):

            @pl.when(me_ref[0, 0] == t)
            def _(t=t):
                for own, before, out in zip(owns, befores, outs):
                    count, length = out.shape[0], own.shape[0]
                    mine = count - (length - count) * t
                    rows = own[...].astype(F32)[:mine, :]
                    if t:
                        skip = before.shape[0] - count + mine
                        rows = jnp.concatenate([before[...].astype(F32)[skip:, :], rows], axis=0) if mine else before[...].astype(F32)[skip:, :]
                    out[...] = rows.astype(out.dtype)

    return pl.pallas_call(
        kernel,
        out_shape=[jax.ShapeDtypeStruct((c, D), d) for c, d in zip(counts, dtypes)],
        in_specs=[SM] + [VM] * (2 * n),
        out_specs=[VM] * n,
        compiler_params=pltpu.CompilerParams(vmem_limit_bytes=24 * 2**20),
        name="push_rows",
    )(me, *items, *earlier)


def order_tiles(pieces, block_ids, slots):
    total = CHUNK * CHUNKS

    def kernel(ids, *refs):
        sources, out = refs[:-1], refs[-1]
        for p, source in enumerate(sources):
            for j in range(slots):
                block = ids[0, p * slots + j]

                @pl.when(block < total)
                def _(source=source, j=j, block=block):
                    out[pl.ds(pl.multiple_of(block * TILE, TILE), TILE), :] = source[
                        j * TILE : (j + 1) * TILE, :
                    ]

    return pl.pallas_call(
        kernel,
        out_shape=jax.ShapeDtypeStruct((total * TILE, TILE), BF16),
        in_specs=[SM] + [VM] * len(pieces),
        out_specs=VM,
        compiler_params=pltpu.CompilerParams(vmem_limit_bytes=16 * 2**20),
        name="order_tiles",
    )(block_ids, *pieces)


def sum_chunks(sums, after):
    part = CHUNK * TILE
    count = len(sums)

    def kernel(*refs):
        sources, out = refs[: 3 * count], refs[3 * count + 1]
        for c in range(count):
            own, near, far = sources[3 * c : 3 * c + 3]
            out[c * part : (c + 1) * part, :] = (
                own[...].astype(F32) + near[...].astype(F32) + far[...].astype(F32)
            ).astype(BF16)

    flat = [(own, near, far) for own, near, far in sums]
    return call(
        kernel,
        "sum_chunks",
        [Held(struct((count * part, TILE), BF16))],
        [],
        *[Part((a, 0, part)) for chunk in flat for a in chunk],
        Part((after, 0, TILE)),
    )[0]


def deal_tiles(chunk, early, extra, block_ids, ranks, slots, lanes):
    count = ranks.shape[1]
    total = CHUNK * CHUNKS
    part = CHUNK * TILE
    rows = slots * TILE + 16

    def kernel(ids, to, own, near, near_extra, far, v_ref, rest, *refs):
        outs, held = refs[:-1], refs[-1]
        held[:part, :] = (
            own[...].astype(F32) + near[...].astype(F32) + far[:part, :].astype(F32)
        ).astype(BF16)
        held[part : total * TILE, :] = rest[...]
        held[total * TILE :, :] = jnp.zeros((TILE, TILE), BF16)
        summed = (
            v_ref[...].astype(F32) + near_extra[...].astype(F32) + far[part:, :].astype(F32)
        ).astype(BF16)
        summed = jnp.concatenate([summed[16 * j : 16 * (j + 1)] for j in range(4)], axis=1)
        feature = lax.broadcasted_iota(jnp.int32, (D, TILE), 0)
        lane = lax.broadcasted_iota(jnp.int32, (D, TILE), 1)
        for p, out in enumerate(outs):
            for j in range(slots):
                block = jnp.minimum(ids[0, p * slots + j], total)
                out[j * TILE : (j + 1) * TILE, :] = held[
                    pl.ds(pl.multiple_of(block * TILE, TILE), TILE), :
                ]
            pick = ((feature == to[0, p] * lanes + lane) & (lane < lanes)).astype(BF16)
            out[slots * TILE :, :] = matmul(summed, pick).astype(BF16)

    own, near, far = chunk
    return call(
        kernel,
        "deal_tiles",
        [struct((rows, TILE), BF16)] * count,
        [pltpu.VMEM(((total + 1) * TILE, TILE), BF16)],
        block_ids,
        ranks,
        Part((own, 0, part)),
        Part((near, 0, part)),
        Part((near, 2 * part, VECTOR_ROWS)),
        Part((far, 0, part + VECTOR_ROWS)),
        Held(extra),
        Held(early),
    )


def shampoo(terms, master, left, right, left_root, right_root, vector_master, vector_moment):
    slots = master.shape[1]
    lanes = vector_master.shape[1]

    def exact(a, b, dims):
        return lax.dot_general(
            a, b, (dims, ((), ())), precision=lax.Precision.HIGHEST, preferred_element_type=F32
        )

    def kernel(*refs):
        parts, refs = refs[: len(terms)], refs[len(terms) :]
        m_ref, l_ref, r_ref, lr_ref, rr_ref, vm_ref, vn_ref = refs[:7]
        g_out, l_out, r_out, m_out, c_out, vg_out, vn_out, vm_out = refs[7:]

        def rows_at(a, b):
            total = parts[0][a:b, :].astype(F32)
            for part in parts[1:]:
                total = total + part[a:b, :].astype(F32)
            return total

        for s in range(slots):
            g = rows_at(s * TILE, (s + 1) * TILE)
            g_out[0, s] = g
            l_out[0, s] = STAT_DECAY * l_ref[0, s] + (1.0 - STAT_DECAY) * exact(g, g, ((1,), (1,)))
            r_out[0, s] = STAT_DECAY * r_ref[0, s] + (1.0 - STAT_DECAY) * exact(g, g, ((0,), (0,)))
            rotated = exact(lr_ref[0, s], g, ((1,), (0,)))
            updated = m_ref[0, s] - MATRIX_RATE * exact(rotated, rr_ref[0, s], ((1,), (0,)))
            m_out[0, s] = updated
            c_out[0, s] = updated.astype(BF16)
        g = rows_at(slots * TILE, slots * TILE + 16)[:10, :lanes]
        moment = STAT_DECAY * vn_ref[...] + (1.0 - STAT_DECAY) * g * g
        vg_out[...] = g
        vn_out[...] = moment
        vm_out[...] = vm_ref[...] - VECTOR_RATE * g / (jnp.sqrt(moment) + 1e-08)

    whole = jax.ShapeDtypeStruct(master.shape, F32)
    row = jax.ShapeDtypeStruct(vector_master.shape, F32)
    outs = [whole] * 4 + [jax.ShapeDtypeStruct(master.shape, BF16)] + [row] * 3
    return pl.pallas_call(
        kernel,
        out_shape=outs,
        in_specs=[VM] * (len(terms) + 7),
        out_specs=[VM] * len(outs),
        compiler_params=pltpu.CompilerParams(vmem_limit_bytes=24 * 2**20),
        name="shampoo",
    )(*terms, master, left, right, left_root, right_root, vector_master, vector_moment)


LOG2E = 1.4426950408889634
SCORE_SCALE = HEAD_DIM ** (-0.5)
SCORE_LOG2 = SCORE_SCALE * LOG2E
PAIRS = HEADS // 2


def matmul(former, latter):
    return jnp.dot(former, latter, preferred_element_type=F32)


def times_transpose(former, latter):
    return lax.dot_general(former, latter, (((1,), (1,)), ((), ())), preferred_element_type=F32)


def transpose_times(former, latter):
    return lax.dot_general(former, latter, (((0,), (0,)), ((), ())), preferred_element_type=F32)


def low(value):
    return value.astype(BF16)


def tile_at(part, index):
    return part[index * TILE : (index + 1) * TILE, :]


def column_matrix(parts, first, count, column):
    return jnp.concatenate(
        [
            jnp.concatenate([tile_at(p, first + a * count + column) for p in parts], axis=1)
            for a in range(4)
        ],
        axis=0,
    )


def row_matrix(parts, first, group):
    return jnp.concatenate(
        [
            jnp.concatenate([tile_at(p, first + 4 * group + b) for b in range(4)], axis=1)
            for p in parts
        ],
        axis=0,
    )


def store_columns(parts, gradient, first, count, column):
    for r, part in enumerate(parts):
        for a in range(4):
            at = (first + a * count + column) * TILE
            part[at : at + TILE, :] = low(
                gradient[a * TILE : (a + 1) * TILE, r * TILE : (r + 1) * TILE]
            )


def store_rows(parts, gradient, first, group):
    for r, part in enumerate(parts):
        for b in range(4):
            at = (first + 4 * group + b) * TILE
            part[at : at + TILE, :] = low(
                gradient[r * TILE : (r + 1) * TILE, b * TILE : (b + 1) * TILE]
            )


def spans(count):
    half = (count // 2 + 15) // 16 * 16
    return [(0, half), (half, count)]


def norm_rows(value):
    mean = jnp.mean(value, axis=-1, keepdims=True)
    centered = value - mean
    scale = lax.rsqrt(jnp.mean(centered * centered, axis=-1, keepdims=True) + NORM_EPSILON)
    return centered * scale, scale


def norm_back(gradient, normed, scale, gain):
    scaled = gradient * gain
    return scale * (
        scaled
        - jnp.mean(scaled, axis=-1, keepdims=True)
        - normed * jnp.mean(scaled * normed, axis=-1, keepdims=True)
    )


def gate_both(value):
    size = jnp.abs(value) * (0.5**0.5)
    turn = 1.0 / (1.0 + 0.3275911 * size)
    bell = jnp.exp2(value * value * (-0.5 * LOG2E))
    series = turn * (
        0.254829592
        + turn * (-0.284496736 + turn * (1.421413741 + turn * (-1.453152027 + turn * 1.061405429)))
    )
    tail = 0.5 * series * bell
    phi = jnp.where(value < 0, tail, 1.0 - tail)
    return value * phi, phi + value * bell * 0.3989422804014327


STATS = 16


def store_stats(stat_ref, stats, scale):
    lane = lax.broadcasted_iota(jnp.int32, stats.shape, 1)
    stat_ref[...] = jnp.where(lane == HEADS, scale, stats).T[:STATS, :]


def norm_scale(stat_ref):
    return jnp.concatenate([stat_ref[...]] * (TILE // STATS), axis=0).T[:, HEADS : HEADS + 1]


def half_mask(which):
    lane = lax.broadcasted_iota(jnp.int32, (1, TILE), 1)
    return (lane < HEAD_DIM) if which == 0 else (lane >= HEAD_DIM)


def attend_pairs(q_ref, k_ref, v_ref, o_ref, bias):
    count = q_ref.shape[0]
    keys = k_ref.shape[0]
    ones = jnp.ones((keys, TILE), BF16)
    lane = lax.broadcasted_iota(jnp.int32, (count, TILE), 1)
    stats = jnp.zeros((count, TILE), F32)
    for pair in range(PAIRS):
        cut = slice(pair * TILE, (pair + 1) * TILE)
        queries, key_rows = q_ref[:, cut], k_ref[:, cut]
        values = jnp.concatenate([v_ref[:, cut], ones], axis=1)
        mixed = []
        for which in range(2):
            masked = jnp.where(half_mask(which), queries, jnp.zeros_like(queries))
            scores = times_transpose(masked, key_rows) * SCORE_LOG2
            if bias is not None:
                scores = scores + bias
            top = jnp.max(scores, axis=1, keepdims=True)
            weights = low(jnp.exp2(scores - top))
            both = matmul(weights, values)
            total = both[:, TILE:]
            mixed.append(both[:, :TILE] / total)
            stats = jnp.where(lane == 2 * pair + which, top + jnp.log2(total), stats)
        o_ref[:, cut] = low(jnp.where(half_mask(0), mixed[0], mixed[1]))
    return stats


def pair_back(queries, key_rows, value_rows, incoming, stats, deltas, bias):
    key_columns = key_rows.T
    dk = dv = None
    dq = []
    for which in range(2):
        mask = half_mask(which)
        q_one = jnp.where(mask, queries, jnp.zeros_like(queries))
        do_one = jnp.where(mask, incoming, jnp.zeros_like(incoming))
        scores = times_transpose(key_rows, q_one) * SCORE_LOG2
        if bias is not None:
            scores = scores + bias
        weights = jnp.exp2(scores - stats[which])
        d_weights = times_transpose(value_rows, do_one)
        d_scores = low(weights * (d_weights - deltas[which]))
        dv_one = matmul(low(weights), do_one)
        dk_one = matmul(d_scores, q_one)
        dv = dv_one if dv is None else dv + dv_one
        dk = dk_one if dk is None else dk + dk_one
        rows = slice(which * HEAD_DIM, (which + 1) * HEAD_DIM)
        dq.append(low(matmul(key_columns[rows, :], d_scores) * SCORE_SCALE))
    return jnp.concatenate(dq, axis=0).T, low(dk * SCORE_SCALE), low(dv)


def pair_columns(pair):
    return slice(pair * TILE, (pair + 1) * TILE)


def pair_rows(ref, pair):
    return [ref[h : h + 1, :] for h in (2 * pair, 2 * pair + 1)]


def row_products(incoming, mixed):
    product = incoming * mixed
    first = low(product)
    rest = low(product - first.astype(F32))
    lane = lax.broadcasted_iota(jnp.int32, (TILE, D), 1) // HEAD_DIM
    row = lax.broadcasted_iota(jnp.int32, (TILE, D), 0)
    pick = (lane == row).astype(BF16)
    return times_transpose(pick, first) + times_transpose(pick, rest)


def struct(shape, dtype):
    return jax.ShapeDtypeStruct(shape, dtype)


class Inward:
    def __init__(self, source, held, sem):
        self.shape = held.shape
        self.copy, self.held, self.waiting = pltpu.make_async_copy(source, held, sem), held, True
        self.copy.start()

    def wait(self):
        if self.waiting:
            self.copy.wait()
            self.waiting = False

    def __getitem__(self, index):
        self.wait()
        return self.held[index]


class Outward:
    def __init__(self, held, target, sem):
        self.held, self.target, self.sem, self.copies = held, target, sem, []
        self.shape, self.dtype = held.shape, held.dtype

    @property
    def at(self):
        return self.held.at

    def __getitem__(self, index):
        return self.held[index]

    def __setitem__(self, index, value):
        self.held[index] = value

    def send(self, *spans_of):
        for a, b in spans_of or ((0, self.shape[0]),):
            rows = pl.ds(a, b - a)
            copy = pltpu.make_async_copy(
                self.held.at[rows], self.target.at[rows], self.sem.at[len(self.copies)]
            )
            copy.start()
            self.copies.append(copy)

    def finish(self):
        if not self.copies:
            self.send()


SENDS = 4


class Part(tuple):
    pass


class Held:
    def __init__(self, array):
        self.array = array


def call(kernel, name, outs, scratch, *args, flops=0, limit=56):
    plain, held, takes = [], [], []
    for arg in args:
        part = None
        if isinstance(arg, Held):
            plain.append(pltpu.with_memory_space_constraint(arg.array, pltpu.VMEM))
            takes.append(None)
            continue
        free = isinstance(arg, Part)
        if isinstance(arg, tuple):
            arg, *part = arg
        if arg.dtype == jnp.int32:
            plain.append(arg)
            takes.append(None)
            continue
        plain.append(arg if free else pltpu.with_memory_space_constraint(arg, pltpu.HBM))
        if part is None:
            part = (0, arg.shape[0])
        columns = part[2] if len(part) > 2 else slice(0, arg.shape[1])
        takes.append((part[0], part[1], columns, free))
        held.append(pltpu.VMEM((part[1], columns.stop - columns.start), arg.dtype))
    n, m = len(plain), len(outs)
    sent = [o for o in outs if not isinstance(o, Held)]

    def body(*refs):
        sources, targets, rest = refs[:n], refs[n : n + m], refs[n + m :]
        in_held, rest = list(rest[: len(held)]), rest[len(held) :]
        out_held, rest = list(rest[: len(sent)]), rest[len(sent) :]
        in_sem, out_sem, rest = rest[0], rest[1], rest[2:]
        ins = []
        for source, take in zip(sources, takes):
            if take is None:
                ins.append(source)
                continue
            first, rows, columns, _ = take
            source = source.at[pl.ds(first, rows), pl.ds(columns.start, columns.stop - columns.start)]
            at = len(held) - len(in_held)
            ins.append(Inward(source, in_held.pop(0), in_sem.at[at]))
        finished = []
        for out, target in zip(outs, targets):
            if not isinstance(out, Held):
                at = len(sent) - len(out_held)
                target = Outward(out_held.pop(0), target, out_sem.at[at])
            finished.append(target)
        kernel(*ins, *finished, *rest)
        for value in ins:
            if isinstance(value, Inward):
                value.wait()
        finished = [f for f in finished if isinstance(f, Outward)]
        for out in finished:
            out.finish()
        for out in finished:
            for copy in out.copies:
                copy.wait()

    shapes = [pltpu.VMEM(o.array.shape, o.array.dtype) if isinstance(o, Held) else pltpu.HBM(o.shape, o.dtype) for o in outs]
    return pl.pallas_call(
        body,
        out_shape=shapes,
        in_specs=[
            SM if a.dtype == jnp.int32 else VM if take is None else ANY if take[3] else HB for a, take in zip(plain, takes)
        ],
        out_specs=[VM if isinstance(o, Held) else HB for o in outs],
        scratch_shapes=[
            *held,
            *[pltpu.VMEM(o.shape, o.dtype) for o in sent],
            pltpu.SemaphoreType.DMA((max(1, len(held)),)),
            pltpu.SemaphoreType.DMA((max(1, len(sent)), SENDS)),
            *scratch,
        ],
        compiler_params=pltpu.CompilerParams(vmem_limit_bytes=limit * 2**20),
        cost_estimate=pl.CostEstimate(flops=flops, bytes_accessed=4000000, transcendentals=0),
        name=name,
    )(*plain)


def part_outs():
    rows = CHUNK * TILE
    return [struct((rows, TILE), BF16), struct((2 * rows, TILE), BF16), struct((rows, TILE), BF16)]


def four_parts(own, near, far):
    rows = CHUNK * TILE
    return (own, near.at[pl.ds(0, rows)], far, near.at[pl.ds(rows, rows)])


def rows_of(chunk, first=0, count=CHUNK):
    own, near, far, far_near, at = chunk
    start = (at * CHUNK + first) * TILE
    size = count * TILE
    return [
        Part((own, start, size)),
        Part((near, start, size)),
        Part((far, first * TILE, size)),
        Part((far_near, first * TILE, size)),
    ]


def causal_bias(count, live, queries_on_rows):
    a = lax.broadcasted_iota(jnp.int32, (count, count), 0)
    b = lax.broadcasted_iota(jnp.int32, (count, count), 1)
    query, key = (a, b) if queries_on_rows else (b, a)
    return jnp.where((key <= query) & (key < live), 0.0, MASKED_SCORE)


def self_forward(x, parts, vectors, norm, live=None):
    rows = x.shape[0]

    def kernel(*refs):
        if live is not None:
            live_ref, *refs = refs
        x_ref, p0, p1, p2, p3, g_ref, first_ref, low_ref, hat_ref, q_ref, k_ref, v_ref, o_ref, stat_ref = refs
        ps = (p0, p1, p2, p3)
        tokens = x_ref[...]
        for column, ref in enumerate((q_ref, k_ref, v_ref)):
            ref[...] = low(matmul(tokens, column_matrix(ps, 0, 3, column)))
            ref.send()
        bias = None if live is None else causal_bias(rows, live_ref[0, 0], True)
        stats = attend_pairs(q_ref, k_ref, v_ref, o_ref, bias)
        o_ref.send()
        wo = row_matrix(ps, 12, 0)
        scales = []
        for a, b in spans(rows):
            hat, scale = norm_rows(tokens[a:b].astype(F32) + matmul(o_ref[a:b, :], wo))
            first = hat * g_ref[2 * norm : 2 * norm + 1, :] + g_ref[2 * norm + 1 : 2 * norm + 2, :]
            first_ref[a:b, :] = first
            low_ref[a:b, :] = low(first)
            hat_ref[a:b, :] = low(hat)
            for out in (hat_ref, low_ref):
                out.send((a, b))
            scales.append(scale)
        store_stats(stat_ref, stats, jnp.concatenate(scales, axis=0))

    outs = [Held(struct((rows, D), F32))] + [struct((rows, D), BF16)] * 6 + [struct((STATS, rows), F32)]
    args = ([] if live is None else [live]) + [x, *rows_of(parts), vectors]
    return call(kernel, f"self_forward_{norm}", outs, [], *args, flops=10**10)


def ffn_weights(ps):
    w1 = jnp.concatenate([column_matrix(ps, 0, 2, c) for c in range(2)], axis=1)
    w2 = jnp.concatenate([row_matrix(ps, 8, c) for c in range(2)], axis=0)
    return w1, w2


def tail_rows(length, count):
    return (length - count) // 16 * 16


def column_as_row(column):
    return jnp.broadcast_to(column, (column.shape[0], TILE)).T[:8, :]


def row_as_column(ref):
    return jnp.concatenate([ref[...]] * STATS, axis=0).T[:, :1]


def ffn_forward(first, parts, vectors, norm, tail):
    rows = first.shape[0]

    def kernel(f_ref, p0, p1, p2, p3, g_ref, enc_ref, hat_ref, scale_ref, hid_ref, slope_ref, tail_ref):
        w1, w2 = ffn_weights((p0, p1, p2, p3))
        scales = []
        for a, b in spans(rows):
            first_rows = f_ref[a:b, :]
            value, slope = gate_both(matmul(low(first_rows), w1))
            value = low(value)
            hid_ref[a:b, :] = value
            hid_ref.send((a, b))
            slope_ref[a:b, :] = low(slope)
            slope_ref.send((a, b))
            hat, scale = norm_rows(first_rows + matmul(value, w2))
            enc_ref[a:b, :] = low(hat * g_ref[2 * norm : 2 * norm + 1, :] + g_ref[2 * norm + 1 : 2 * norm + 2, :])
            hat_ref[a:b, :] = low(hat)
            for out in (hat_ref, enc_ref):
                out.send((a, b))
            scales.append(scale)
        tail_ref[...] = enc_ref[tail:, :]
        scale_ref[...] = column_as_row(jnp.concatenate(scales, axis=0))

    outs = [struct((rows, D), BF16), struct((rows, D), BF16), struct((8, rows), F32)]
    outs += [struct((rows, FF), BF16)] * 2 + [struct((rows - tail, D), BF16)]
    return call(kernel, f"ffn_forward_{norm}", outs, [], Held(first), *rows_of(parts), vectors, flops=3 * 10**9)


def cross_forward(second, encoded, parts, vectors):
    rows, keys = second.shape[0], encoded.shape[0]

    def kernel(s_ref, p0, p1, p2, p3, e_ref, g_ref, third_ref, hat_ref, q_ref, k_ref, v_ref, o_ref, stat_ref):
        ps = (p0, p1, p2, p3)
        q_ref[...] = low(matmul(low(s_ref[...]), column_matrix(ps, 0, 1, 0)))
        k_ref[...] = low(matmul(e_ref[...], column_matrix(ps, 4, 2, 0)))
        v_ref[...] = low(matmul(e_ref[...], column_matrix(ps, 4, 2, 1)))
        for ref in (q_ref, k_ref, v_ref):
            ref.send()
        stats = attend_pairs(q_ref, k_ref, v_ref, o_ref, None)
        o_ref.send()
        hat, scale = norm_rows(s_ref[...] + matmul(o_ref[...], row_matrix(ps, 12, 0)))
        third_ref[...] = hat * g_ref[6:7, :] + g_ref[7:8, :]
        hat_ref[...] = low(hat)
        hat_ref.send()
        store_stats(stat_ref, stats, scale)

    outs = [Held(struct((rows, D), F32)), struct((rows, D), BF16)]
    outs += [struct((rows, D), BF16), struct((keys, D), BF16), struct((keys, D), BF16)]
    outs += [struct((rows, D), BF16), struct((STATS, rows), F32)]
    return call(kernel, "cross_forward", outs, [], Held(second), *rows_of(parts), encoded, vectors, flops=5 * 10**9)


def store_norm(ref, gradient, hat):
    ref[0:1, :] = jnp.sum(gradient * hat, axis=0, keepdims=True)
    ref[1:2, :] = jnp.sum(gradient, axis=0, keepdims=True)


def send_parts(outs, first, count):
    a, b, rows = first * TILE, (first + count) * TILE, CHUNK * TILE
    own, near, far = outs
    near.send((a, b), (rows + a, rows + b))
    far.send((a, b))
    own.send((a, b))


def ffn_weight_gradients(inputs, hid_ref, dh_ref, db_ref, grads, outs):
    for c in range(2):
        store_columns(grads, transpose_times(inputs, dh_ref[:, c * D : (c + 1) * D]), 0, 2, c)
    send_parts(outs, 0, 8)
    for c in range(2):
        store_rows(grads, transpose_times(hid_ref[:, c * D : (c + 1) * D], db_ref[...]), 8, c)
    send_parts(outs, 8, 8)


def ffn_both(third, cotangent, live, parts, vectors, tail):
    rows = third.shape[0]

    def kernel(live_ref, t_ref, p0, p1, p2, p3, g_ref, c_ref, dec_ref, tail_ref, back_ref, n_ref, d0, d1, d2, hid_ref, dh_ref, db_ref):
        w1, w2 = ffn_weights((p0, p1, p2, p3))
        grads = four_parts(d0, d1, d2)
        gain = g_ref[8:9, :]
        for part, (a, b) in enumerate(spans(rows)):
            third_rows = t_ref[a:b, :]
            value, slope = gate_both(matmul(low(third_rows), w1))
            value = low(value)
            hid_ref[a:b, :] = value
            hat, scale = norm_rows(third_rows + matmul(value, w2))
            dec_ref[a:b, :] = low(hat * gain + g_ref[9:10, :])
            row = lax.broadcasted_iota(jnp.int32, (b - a, 1), 0) + a
            incoming = jnp.where(row < live_ref[0, 0], c_ref[a:b, :].astype(F32), 0.0)
            if part == 0:
                n_ref[...] = jnp.zeros_like(n_ref)
            n_ref[0:1, :] += jnp.sum(incoming * hat, axis=0, keepdims=True)
            n_ref[1:2, :] += jnp.sum(incoming, axis=0, keepdims=True)
            back = norm_back(incoming, hat, scale, gain)
            back_low = low(back)
            db_ref[a:b, :] = back_low
            dh = low(slope * times_transpose(back_low, w2))
            dh_ref[a:b, :] = dh
            back_ref[a:b, :] = back + times_transpose(dh, w1)
            dec_ref.send((a, b))
        tail_ref[...] = dec_ref[tail:, :]
        tail_ref.send()
        ffn_weight_gradients(low(t_ref[...]), hid_ref, dh_ref, db_ref, grads, (d0, d1, d2))

    outs = [struct((rows, D), BF16), struct((rows - tail, D), BF16), Held(struct((rows, D), F32))]
    outs += [struct((8, D), F32)] + part_outs()
    scratch = [pltpu.VMEM((rows, FF), BF16), pltpu.VMEM((rows, FF), BF16), pltpu.VMEM((rows, D), BF16)]
    return call(kernel, "ffn_both", outs, scratch, live, Held(third), *rows_of(parts), vectors, cotangent, flops=10**10)


def ffn_backward(cotangent, more, hat, scale, first, hid, slope, parts, vectors, norm):
    rows = first.shape[0]

    def kernel(m_ref, c_ref, h_ref, s_ref, g_ref, p0, p1, p2, p3, slope_ref, f_ref, hid_ref, back_ref, n_ref, d0, d1, d2, dh_ref, db_ref):
        grads = four_parts(d0, d1, d2)
        n_ref[...] = jnp.zeros_like(n_ref)
        scale = row_as_column(s_ref)
        for a, b in spans(rows):
            incoming = c_ref[a:b, :].astype(F32) + m_ref[a:b, :]
            hat_rows = h_ref[a:b, :].astype(F32)
            n_ref[0:1, :] += jnp.sum(incoming * hat_rows, axis=0, keepdims=True)
            n_ref[1:2, :] += jnp.sum(incoming, axis=0, keepdims=True)
            back = norm_back(incoming, hat_rows, scale[a:b], g_ref[2 * norm : 2 * norm + 1, :])
            back_low = low(back)
            db_ref[a:b, :] = back_low
            if not a:
                w1, w2 = ffn_weights((p0, p1, p2, p3))
            dh = low(slope_ref[a:b, :].astype(F32) * times_transpose(back_low, w2))
            dh_ref[a:b, :] = dh
            back_ref[a:b, :] = back + times_transpose(dh, w1)
        ffn_weight_gradients(f_ref[...], hid_ref, dh_ref, db_ref, grads, (d0, d1, d2))

    outs = [Held(struct((rows, D), F32)), struct((8, D), F32)] + part_outs()
    scratch = [pltpu.VMEM((rows, FF), BF16), pltpu.VMEM((rows, D), BF16)]
    return call(kernel, f"ffn_backward_{norm}", outs, scratch, Held(more), cotangent, hat, scale, vectors, *rows_of(parts), slope, first, hid, flops=10**10)


def before_heads(b_ref, h_ref, stat_ref, gain, wo, n_ref):
    incoming = b_ref[...]
    hat_rows = h_ref[...].astype(F32)
    n_ref[...] = jnp.zeros_like(n_ref)
    store_norm(n_ref, incoming, hat_rows)
    branch = norm_back(incoming, hat_rows, norm_scale(stat_ref), gain)
    branch_low = low(branch)
    return branch, branch_low, low(times_transpose(branch_low, wo()))


def self_backward(back, hat, x, q, k, v, o, stats, parts, vectors, norm, live, tail):
    rows = x.shape[0]

    def kernel(live_ref, b_ref, h_ref, stat_ref, g_ref, w0, w1, w2, w3, o_ref, q_ref, k_ref, v_ref, x_ref, p0, p1, p2, p3,
               dx_ref, tail_ref, n_ref, d0, d1, d2, do_ref, dq_ref, dk_ref, dv_ref):
        ps, grads = (p0, p1, p2, p3), four_parts(d0, d1, d2)
        branch, branch_low, do = before_heads(
            b_ref, h_ref, stat_ref, g_ref[2 * norm : 2 * norm + 1, :], lambda: row_matrix((w0, w1, w2, w3), 0, 0), n_ref
        )
        do_ref[...] = do
        store_rows(grads, transpose_times(o_ref[...], branch_low), 12, 0)
        send_parts((d0, d1, d2), 12, 4)
        delta = row_products(do.astype(F32), o_ref[...].astype(F32))
        bias = causal_bias(rows, live_ref[0, 0], False)
        for pair in range(PAIRS):
            cut = pair_columns(pair)
            dq_ref[:, cut], dk_ref[:, cut], dv_ref[:, cut] = pair_back(
                q_ref[:, cut], k_ref[:, cut], v_ref[:, cut], do_ref[:, cut],
                pair_rows(stat_ref, pair), pair_rows(delta, pair), bias,
            )
        xt = x_ref[...].T
        for column, ref in enumerate((dq_ref, dk_ref, dv_ref)):
            store_columns(grads, matmul(xt, ref[...]), 0, 3, column)
        send_parts((d0, d1, d2), 0, 12)
        total = branch
        for column, ref in enumerate((dq_ref, dk_ref, dv_ref)):
            total = total + times_transpose(ref[...], column_matrix(ps, 0, 3, column))
        dx_ref[...] = low(total)
        dx_ref.send()
        tail_ref[...] = dx_ref[tail:, :]

    outs = [struct((rows, D), BF16), struct((rows - tail, D), BF16), struct((8, D), F32)] + part_outs()
    scratch = [pltpu.VMEM((rows, D), BF16)] * 4
    args = [live, Held(back), hat, stats, vectors, *rows_of(parts, 12, 4), o, q, k, v, x, *rows_of(parts, 0, 12)]
    return call(kernel, f"self_backward_{norm}", outs, scratch, *args, flops=2 * 10**10)


def cross_backward(back, hat, second, encoded, q, k, v, o, stats, parts, vectors):
    rows, keys = second.shape[0], encoded.shape[0]

    def kernel(b_ref, h_ref, stat_ref, g_ref, w0, w1, w2, w3, o_ref, q_ref, k_ref, v_ref, x_ref, e_ref, p0, p1, p2, p3,
               dx_ref, de_ref, n_ref, d0, d1, d2, do_ref, dq_ref, dk_ref, dv_ref):
        ps, grads = (p0, p1, p2, p3), four_parts(d0, d1, d2)
        branch, branch_low, do = before_heads(
            b_ref, h_ref, stat_ref, g_ref[6:7, :], lambda: row_matrix((w0, w1, w2, w3), 0, 0), n_ref
        )
        do_ref[...] = do
        store_rows(grads, transpose_times(o_ref[...], branch_low), 12, 0)
        send_parts((d0, d1, d2), 12, 4)
        delta = row_products(do.astype(F32), o_ref[...].astype(F32))
        for pair in range(PAIRS):
            cut = pair_columns(pair)
            dq_ref[:, cut], dk_ref[:, cut], dv_ref[:, cut] = pair_back(
                q_ref[:, cut], k_ref[:, cut], v_ref[:, cut], do_ref[:, cut],
                pair_rows(stat_ref, pair), pair_rows(delta, pair), None,
            )
        store_columns(grads, transpose_times(x_ref[...], dq_ref[...]), 0, 1, 0)
        et = e_ref[...].T
        store_columns(grads, matmul(et, dk_ref[...]), 4, 2, 0)
        store_columns(grads, matmul(et, dv_ref[...]), 4, 2, 1)
        send_parts((d0, d1, d2), 0, 12)
        dx_ref[...] = branch + times_transpose(dq_ref[...], column_matrix(ps, 0, 1, 0))
        de_ref[...] = times_transpose(dk_ref[...], column_matrix(ps, 4, 2, 0)) + times_transpose(
            dv_ref[...], column_matrix(ps, 4, 2, 1)
        )

    outs = [Held(struct((rows, D), F32)), Held(struct((keys, D), F32)), struct((8, D), F32)] + part_outs()
    scratch = [pltpu.VMEM((rows, D), BF16)] * 2 + [pltpu.VMEM((keys, D), BF16)] * 2
    return call(kernel, "cross_backward", outs, scratch, Held(back), hat, stats, vectors, *rows_of(parts, 12, 4),
                o, q, k, v, second, encoded, *rows_of(parts, 0, 12), flops=2 * 10**10)


def column_tiles(out, gradient, column):
    for a in range(4):
        at = (a * 3 + column) * TILE
        out[at : at + TILE, :] = low(gradient[a * TILE : (a + 1) * TILE, :])


VECTOR_ROWS = 64


def first_backward(back, hat, x, q, k, v, o, stats, parts, vectors, norms):
    rows = x.shape[0]
    size = CHUNK * TILE

    def kernel(b_ref, h_ref, stat_ref, g_ref, w0, w1, w2, w3, o_ref, q_ref, k_ref, v_ref, x_ref, n1, n2, n3, n4,
               branch_ref, do_ref, delta_ref, v_out, near_ref, out0_ref, out2_ref, xt_ref, dq_ref, dk_ref, dv_ref, n_ref):
        branch, branch_low, do = before_heads(
            b_ref, h_ref, stat_ref, g_ref[0:1, :], lambda: row_matrix((w0, w1, w2, w3), 0, 0), n_ref
        )
        branch_ref[...] = branch
        branch_ref.send()
        do_ref[...] = do
        do_ref.send()
        norms_low = low(jnp.concatenate([n[:2, :] for n in (n_ref, n1, n2, n3, n4)] + [jnp.zeros((6, D), F32)], axis=0))
        for j in range(4):
            v_out[16 * j : 16 * (j + 1), :] = norms_low[:, j * TILE : (j + 1) * TILE]
        near_ref[2 * size :, :] = v_out[...]
        near_ref.send((2 * size, 2 * size + VECTOR_ROWS))
        wo = low(transpose_times(o_ref[...], branch_low))
        for r, (ref, at) in enumerate(
            ((out0_ref, 0), (near_ref, 12 * TILE), (out2_ref, 0), (near_ref, size + 12 * TILE))
        ):
            for b in range(4):
                ref[at + b * TILE : at + (b + 1) * TILE, :] = wo[
                    r * TILE : (r + 1) * TILE, b * TILE : (b + 1) * TILE
                ]
        delta_ref[...] = row_products(do.astype(F32), o_ref[...].astype(F32))[:STATS, :]
        xt = x_ref[...].T
        xt_ref[...] = xt
        for out in (xt_ref, out0_ref, out2_ref, delta_ref):
            out.send()
        for at, pair in enumerate((1, 3)):
            cut = pair_columns(pair)
            grads = pair_back(
                q_ref[:, cut], k_ref[:, cut], v_ref[:, cut], do_ref[:, cut],
                pair_rows(stat_ref, pair), pair_rows(delta_ref, pair), None,
            )
            for column, (ref, value) in enumerate(zip((dq_ref, dk_ref, dv_ref), grads)):
                ref[:, at * TILE : (at + 1) * TILE] = value
                column_tiles(near_ref.at[pl.ds(at * size, size)], matmul(xt, value), column)
            near_ref.send((at * size, (at + 1) * size))

    outs = [struct((rows, D), F32), struct((rows, D), BF16), struct((STATS, rows), F32)]
    outs += [struct((VECTOR_ROWS, TILE), BF16), struct((2 * size + VECTOR_ROWS, TILE), BF16)]
    outs += [struct((4 * TILE, TILE), BF16)] * 2 + [struct((D, rows), BF16)]
    outs += [struct((rows, 2 * TILE), BF16)] * 3
    return call(kernel, "first_backward", outs, [pltpu.VMEM((8, D), F32)], Held(back), hat, stats, vectors,
                *rows_of(parts, 12, 4), o, q, k, v, x, *norms, flops=2 * 10**10)


def pair_arguments(pair, rows, *arrays):
    return [(a, 0, rows, pair_columns(pair)) for a in arrays]


def pair_backward(pair, xt, q, k, v, do, stats, delta, wo_part, extra):
    rows = q.shape[0]

    def kernel(q_ref, k_ref, do_ref, v_ref, stat_ref, delta_ref, xt_ref, wo_ref, v_ref2, out_ref, dq_ref, dk_ref, dv_ref):
        grads = pair_back(
            q_ref[...], k_ref[...], v_ref[...], do_ref[...],
            pair_rows(stat_ref, pair), pair_rows(delta_ref, pair), None,
        )
        for column, (ref, value) in enumerate(zip((dq_ref, dk_ref, dv_ref), grads)):
            ref[...] = value
            column_tiles(out_ref, matmul(xt_ref[...], value), column)
        out_ref[12 * TILE : CHUNK * TILE, :] = wo_ref[...]
        out_ref[CHUNK * TILE :, :] = v_ref2[...]

    outs = [struct((CHUNK * TILE + VECTOR_ROWS, TILE), BF16)] + [struct((rows, TILE), BF16)] * 3
    return call(kernel, f"pair_backward_{pair}", outs, [], *pair_arguments(pair, rows, q, k, do, v), stats, delta,
                xt, wo_part, extra, flops=5 * 10**9)


def last_backward(xt, q, k, v, do, stats, delta, wo_part, branch, odd, two, parts, tail):
    rows = branch.shape[0]

    def kernel(q_ref, k_ref, do_ref, v_ref, stat_ref, delta_ref, xt_ref, wo_ref, b_ref, *refs):
        refs, ps, (out_ref, dx_ref, tail_ref) = refs[:6], refs[6:10], refs[10:]
        grads = pair_back(
            q_ref[...], k_ref[...], v_ref[...], do_ref[...],
            pair_rows(stat_ref, 0), pair_rows(delta_ref, 0), None,
        )
        for column, value in enumerate(grads):
            column_tiles(out_ref, matmul(xt_ref[...], value), column)
        out_ref[12 * TILE :, :] = wo_ref[...]
        out_ref.send()
        total = b_ref[...]
        for column, zero in enumerate(grads):
            pairs, single = refs[column], refs[3 + column]
            rows_in = jnp.concatenate([zero, pairs[:, :TILE], single[...], pairs[:, TILE:]], axis=1)
            total = total + times_transpose(rows_in, column_matrix(ps, 0, 3, column))
        dx_ref[...] = low(total)
        dx_ref.send()
        tail_ref[...] = dx_ref[tail:, :]

    outs = [struct((CHUNK * TILE, TILE), BF16), struct((rows, D), BF16), struct((rows - tail, D), BF16)]
    return call(kernel, "last_backward", outs, [], *pair_arguments(0, rows, q, k, do, v), stats, delta, xt, wo_part,
                branch, *odd, *two, *rows_of(parts, 0, 12), flops=10**10)


def tie(value, *others):
    return lax.optimization_barrier((value, *others))[0]


def compute(x, y, xc, yc, live, tiles, near, vectors, alive, image_rows, tag_rows):
    live_tags = jnp.where(alive, live, 0).reshape(1, 1)
    live = live.reshape(1, 1)
    image_tail = tail_rows(x.shape[0], image_rows)
    tag_tail = tail_rows(y.shape[0], tag_rows)

    def far_part(c, *others):
        part = tiles[c * CHUNK * TILE : (c + 1) * CHUNK * TILE]
        return lax.ppermute(tie(part, *others) if others else part, "tensor", chip_pairs())

    def chunk(c, far, *others):
        return (tiles, near, far, lax.ppermute(tie(far, *others) if others else far, "tensor", core_pairs()), c)

    fars = [far_part(0)]
    chunk0 = chunk(0, fars[0])
    fars += [far_part(1), far_part(2)]
    first, first_low, hat0, q, k, v, o, stat = self_forward(x, chunk0, vectors, 0)
    fars += [far_part(3, first), far_part(4, first)]
    chunk1 = chunk(1, fars[1], first)
    encoded, hat1, scale1, hid, slope, encoded_tail = ffn_forward(
        first, chunk1, vectors, 1, image_tail
    )
    chunk2 = chunk(2, fars[2], encoded)
    second, second_low, hat2, q2, k2, v2, o2, stat2 = self_forward(y, chunk2, vectors, 2, live)
    chunk3 = chunk(3, fars[3], second)
    third, hat3, q3, k3, v3, o3, stat3 = cross_forward(second, encoded, chunk3, vectors)
    chunk4 = chunk(4, fars[4], third)
    decoded, decoded_tail, back, n4, *part4 = ffn_both(third, yc, live_tags, chunk4, vectors, tag_tail)
    near4 = send_near(part4)
    back, d_encoded, n3, *part3 = cross_backward(
        back, hat3, second_low, encoded, q3, k3, v3, o3, stat3, chunk3, vectors
    )
    far4 = send_far(sum_far(part4, tie(near4, back)))
    near3 = send_near(part3)
    d_first, n1, *part1 = ffn_backward(
        xc, d_encoded, hat1, scale1, first_low, hid, slope, chunk1, vectors, 1
    )
    far3 = send_far(sum_far(part3, tie(near3, d_first)))
    near1 = send_near(part1)
    back = tie(back, d_first, far4)
    dy, dy_tail, n2, *part2 = self_backward(
        back, hat2, y, q2, k2, v2, o2, stat2, chunk2, vectors, 2, live, tag_tail
    )
    near2 = send_near(part2)
    far_sum1 = sum_far(part1, tie(near1, dy))
    far1 = send_far(far_sum1)
    d_first = tie(d_first, dy, far3, far_sum1)
    branch, do, delta, extra, near_part0, out0, out2, xt, *odd = first_backward(
        d_first, hat0, x, q, k, v, o, stat, chunk0, vectors, (n1, n2, n3, n4)
    )
    near0 = send_near([None, near_part0])
    far_sum2 = sum_far(part2, tie(near2, branch))
    far2 = send_far(far_sum2)
    far_part0, *two = pair_backward(
        2, tie(xt, near_part0, far_sum2), q, k, v, do, stat, delta, out2, extra
    )
    far_sum0 = sum_far([None, None, far_part0], tie(near0, far_part0))
    far0 = send_far(far_sum0)
    own_part0, dx, dx_tail = last_backward(
        tie(xt, far_sum0), q, k, v, do, stat, delta, out0, branch, odd, two, chunk0, image_tail
    )
    owns = [own_part0, part1[0], part2[0], part3[0], part4[0]]
    nears, fars = [near0, near1, near2, near3, near4], [far0, far1, far2, far3, far4]
    items = [encoded, decoded, dx, dy]
    tails = [encoded_tail, decoded_tail, dx_tail, dy_tail]
    return items, tails, list(zip(owns, nears, fars)), extra, dx


def one_hot(index, count, dtype):
    return (index[:, None] == lax.broadcasted_iota(jnp.int32, (1, count), 1)).astype(dtype)


def local(
    image_tokens,
    tag_tokens,
    image_cotangent,
    tag_cotangent,
    tag_lengths,
    slot_blocks,
    master_blocks,
    left_factor,
    right_factor,
    left_root,
    right_root,
    vector_master,
    vector_moment,
):
    dp = lax.axis_size("dp")
    shards = lax.axis_size("tensor")
    me = lax.axis_index("tensor")
    slots = master_blocks.shape[1]
    items = tag_lengths.shape[0]
    image_length = image_tokens.shape[0] * shards // items
    item_length = tag_tokens.shape[0] * shards // items
    lanes = vector_master.shape[1]
    def rows_of(value):
        return jnp.pad(value, ((0, 16 - value.shape[0]), (0, TILE - value.shape[1])))

    own = jnp.concatenate(
        [
            master_blocks.astype(BF16).reshape(slots * TILE, TILE),
            rows_of(vector_master.astype(BF16)),
        ],
        axis=0,
    )
    pieces = gather_pieces(own, dp)
    alive = me < items
    rank = me.reshape(1, 1)
    tokens = lax.optimization_barrier((image_tokens, tag_tokens, pieces[3]))[:2]
    x, y = pull_rows(tokens, (image_length, item_length), rank, True)
    cotangents = lax.optimization_barrier((image_cotangent, tag_cotangent, pieces[1]))[:2]
    xc, yc = pull_rows(cotangents, (image_length, item_length), rank, False)
    x, y, xc, yc, *pieces = lax.optimization_barrier((x, y, xc, yc, *pieces))
    ranks = jnp.stack([relative_rank(p, dp) for p in range(dp)])

    def blocks_of(those):
        picked = one_hot(those, dp, jnp.int32)[:, :, None] * slot_blocks.reshape(1, dp, slots)
        return jnp.sum(picked, axis=1).reshape(1, dp * slots)

    tiles = order_tiles(pieces, blocks_of(ranks), slots)
    vector_list = jnp.stack([p[slots * TILE : slots * TILE + 10, :lanes] for p in pieces])
    vectors = jnp.einsum(
        "pr,pvl->vrl", one_hot(ranks, dp, BF16), vector_list, preferred_element_type=F32
    ).reshape(10, dp * lanes)
    near = lax.ppermute(tiles, "tensor", core_pairs())
    live = jnp.sum(jnp.where(lax.broadcasted_iota(jnp.int32, (items,), 0) == me, tag_lengths, 0))
    live = jnp.where(alive, live, 1)
    wholes, tails, sums, extra, dx = compute(
        x,
        y,
        xc,
        yc,
        live,
        tiles,
        near,
        vectors,
        alive,
        image_tokens.shape[0],
        tag_tokens.shape[0],
    )
    targets = jnp.stack([target_rank(p, dp) for p in range(dp)])
    early = sum_chunks(sums[1:], sums[0][0])
    outgoing = deal_tiles(sums[0], early, extra, blocks_of(targets), targets.reshape(1, dp), slots, lanes)
    terms, mark = sum_pieces(outgoing, dp)
    tails = [lax.optimization_barrier((tail, mark))[0] for tail in tails]
    images, tags = image_tokens.shape[0], tag_tokens.shape[0]
    rows = push_rows(wholes, tails, (images, tags, images, tags), (BF16, BF16, F32, F32), rank)
    updates = shampoo(
        terms,
        master_blocks,
        left_factor,
        right_factor,
        left_root,
        right_root,
        vector_master,
        vector_moment,
    )
    return (*rows, *updates)


def solution(mesh):
    in_specs = (
        P(("dp", "tensor"), None),
        P(("dp", "tensor"), None),
        P(("dp", "tensor"), None),
        P(("dp", "tensor"), None),
        P("dp"),
        P(),
        P("tensor", "dp", None, None),
        P("tensor", "dp", None, None),
        P("tensor", "dp", None, None),
        P("tensor", "dp", None, None),
        P("tensor", "dp", None, None),
        P(None, "dp"),
        P(None, "dp"),
    )
    out_specs = (
        P(("dp", "tensor"), None),
        P(("dp", "tensor"), None),
        P(("dp", "tensor"), None),
        P(("dp", "tensor"), None),
        P("tensor", "dp", None, None),
        P("tensor", "dp", None, None),
        P("tensor", "dp", None, None),
        P("tensor", "dp", None, None),
        P("tensor", "dp", None, None),
        P(None, "dp"),
        P(None, "dp"),
        P(None, "dp"),
    )
    return jax.shard_map(local, mesh=mesh, in_specs=in_specs, out_specs=out_specs, check_vma=False)
```

```python
import jax
import jax.numpy as jnp
from jax import lax
from jax.experimental import pallas as pl
from jax.experimental.pallas import tpu as pltpu
from jax.sharding import PartitionSpec as P

D = 512
HEADS = 8
HEAD_DIM = 64
FF = 1024
TILE = 128
CHUNK = 16
CHUNKS = 5

NORM_EPSILON = 1e-05
MATRIX_RATE = 0.5
VECTOR_RATE = 0.2
STAT_DECAY = 0.5
MASKED_SCORE = -1e30

F32 = jnp.float32
BF16 = jnp.bfloat16
ANY = pl.BlockSpec(memory_space=pl.ANY)
VM = pl.BlockSpec(memory_space=pltpu.VMEM)
SM = pl.BlockSpec(memory_space=pltpu.SMEM)
HB = pl.BlockSpec(memory_space=pltpu.HBM)


def core_pairs():
    return [(i, i ^ 1) for i in range(4)]


def chip_pairs():
    return [(i, i ^ 2) for i in range(4)]


def diagonal_pairs():
    return [(i, i ^ 3) for i in range(4)]


def y_pairs():
    return [(i, i ^ 1) for i in range(8)]


def z_shift(step):
    return [(2 * z + y, 2 * ((z + step) % 4) + y) for z in range(4) for y in range(2)]


def relative_rank(position, size):
    me = lax.axis_index("dp")
    if size != 8:
        return jnp.int32(position)
    swapped, step = divmod(position, 4)
    return 2 * lax.rem(me // 2 - step + 4, 4) + lax.rem(me + swapped, 2)


def target_rank(position, size):
    me = lax.axis_index("dp")
    if size != 8:
        return jnp.int32(position)
    swapped, step = divmod(position, 4)
    return 2 * lax.rem(me // 2 + step, 4) + lax.rem(me + swapped, 2)


def after(value, *others):
    return lax.optimization_barrier((value, *others))[0]


def together(*arrived):
    return lax.optimization_barrier(arrived)


def gather_rows(image, tags, cotangents, piece, size, meanwhile, ready):
    shards = lax.axis_size("tensor")
    split = tags.shape[0]

    def near(value):
        return lax.ppermute(value, "tensor", core_pairs())

    def far(value):
        return lax.ppermute(value, "tensor", chip_pairs())

    def later(value):
        return lax.ppermute(value, "tensor", [(i + 1, i) for i in range(shards - 1)])

    both = jnp.concatenate([tags, image], axis=0)
    if size != 8:
        pieces = list(lax.all_gather(piece, "dp", axis=0, tiled=False))
        near_both, far_image, far_tags = near(both), far(image), far(tags)
        last_image, last_tags, moved = near(far_image), near(far_tags), later(cotangents)
        images = meanwhile([(image, 0), (near_both, split), (far_image, 0), (last_image, 0)], ready[0])
    else:

        def column(part, step):
            return lax.ppermute(part, "dp", z_shift(step))

        def row(part):
            return lax.ppermute(part, "dp", y_pairs())

        one, three, other, far_image, near_both, *ready = together(
            column(piece, 1), column(piece, 3), row(piece), far(image), near(both), *ready
        )
        two, row_one, row_three, far_tags, last_image = together(
            column(after(piece, other), 2), row(one), row(three), far(after(tags, other)), near(far_image)
        )
        images = [(image, 0), (near_both, split), (far_image, 0), (last_image, 0)]
        images, row_two, last_tags, moved = together(
            meanwhile(images, ready[0]), row(two), near(far_tags), later(after(cotangents, two))
        )
        pieces = [piece, one, two, three, other, row_one, row_two, row_three]
    sequences = [(tags, 0), (near_both, 0), (far_tags, 0), (last_tags, 0)]
    return pieces, images, sequences, moved, ready


def sum_pieces(pieces, size):
    if size != 8:
        whole = lax.psum_scatter(
            jnp.stack(pieces).astype(F32), "dp", scatter_dimension=0, tiled=False
        )
        return [whole.astype(BF16)], pieces[0]
    column, ready, mark = [pieces[0]], [], None
    for at, step in enumerate((2, 1, 3, 0)):
        piece = pieces[4 + step]
        if at > 1:
            piece = lax.optimization_barrier((piece, ready[at - 2]))[0]
        other = lax.ppermute(piece, "dp", y_pairs())
        if step == 0:
            column.append(other)
            continue
        both = (pieces[step].astype(F32) + other.astype(F32)).astype(BF16)
        ready.append(both)
        column.append(lax.ppermute(both, "dp", z_shift(step)))
    return column, pieces[0]


GROUPS = ((12, 20), (44, 20), (64, 16))


def send_near(part):
    return lax.ppermute(part[1], "tensor", core_pairs())


def sum_far(part, near):
    rows = part[0].shape[0]
    return (part[2].astype(F32) + near[rows : rows + part[2].shape[0]].astype(F32)).astype(BF16)


def send_far(value):
    return lax.ppermute(value, "tensor", chip_pairs())


def spread(pieces):
    return [
        pieces[0],
        lax.ppermute(pieces[1], "tensor", core_pairs()),
        lax.ppermute(pieces[2], "tensor", chip_pairs()),
        lax.ppermute(pieces[3], "tensor", diagonal_pairs()),
    ]


def whole_group(parts, info, name):
    shards = len(parts)
    count = parts[0][0].shape[0]

    def kernel(info_ref, *refs):
        refs, out = refs[:-1], refs[-1]
        refs = [ref.at[pl.ds(first, count)] for ref, (_, first) in zip(refs, parts)]
        for t in range(shards):

            @pl.when(info_ref[0, 1] == t)
            def _(t=t):
                out[...] = jnp.concatenate([refs[r ^ t][...].astype(F32) for r in range(shards)], axis=0).astype(BF16)

    return pl.pallas_call(
        kernel,
        out_shape=jax.ShapeDtypeStruct((count * shards, D), BF16),
        in_specs=[SM] + [VM] * shards,
        out_specs=VM,
        compiler_params=pltpu.CompilerParams(vmem_limit_bytes=56 * 2**20),
        name=name,
    )(info, *[a for a, _ in parts])


def fill_item(info_ref, own, later, out):
    shards = 4
    own, later = own[...].astype(F32), later[...].astype(F32)
    rows, length = own.shape[0], out.shape[0]
    for t in range(shards):

        @pl.when(info_ref[0, 1] == t)
        def _(t=t):
            if t == shards - 1:
                both = jnp.zeros(out.shape, F32)
            else:
                start = (length - rows) * t
                both = jnp.concatenate([own[start:, :], later[: length - rows + start, :]], axis=0)
            out[...] = both.astype(BF16)


def push_tails(tails):
    shards = lax.axis_size("tensor")
    return lax.ppermute(tails, "tensor", [(i, i + 1) for i in range(shards - 1)])


def push_rows(items, pushed, counts, sums, info):
    shards = lax.axis_size("tensor")
    n = len(items)
    sizes = [item.shape[0] - tail_rows(item.shape[0], count) for item, count in zip(items, counts)]
    extra = [a for terms in sums if terms for a, _ in terms]

    def kernel(info_ref, *refs):
        owns, before, more, outs = refs[:n], refs[n], refs[n + 1 : -n], refs[-n:]
        for t in range(shards):

            @pl.when(info_ref[0, 1] == t)
            def _(t=t):
                used = end = 0
                for own, size, out, terms in zip(owns, sizes, outs, sums):
                    end += size
                    count, length = out.shape[0], own.shape[0]
                    mine = count - (length - count) * t
                    rows = [before[...].astype(F32)[end - count + mine : end, :]] if t else []
                    if mine:
                        rows.append(own[...].astype(F32)[:mine, :])
                    rows = jnp.concatenate(rows, axis=0) if len(rows) > 1 else rows[0]
                    if terms:
                        piece, whole = piece_size(count), count * shards
                        skip = count * t - min(count * t // 16 * 16, whole - piece)
                        added = None
                        for _, begin in terms:
                            term = more[used][begin : begin + piece, :].astype(F32)
                            added = term if added is None else added + term
                            used += 1
                        rows = rows + added[skip : skip + count, :]
                    out[...] = rows.astype(out.dtype)

    return pl.pallas_call(
        kernel,
        out_shape=[jax.ShapeDtypeStruct((c, D), F32 if terms else BF16) for c, terms in zip(counts, sums)],
        in_specs=[SM] + [VM] * (n + 1 + len(extra)),
        out_specs=[VM] * n,
        compiler_params=pltpu.CompilerParams(vmem_limit_bytes=32 * 2**20),
        name="push_gradients" if extra else "push_outputs",
    )(info, *items, pushed, *extra)


def order_tiles(pieces, block_ids, ranks, slots, lanes):
    total = CHUNK * CHUNKS

    def kernel(ids, to, *refs):
        sources, (out, *groups, vector_ref) = refs[: -2 - len(GROUPS)], refs[-2 - len(GROUPS) :]
        feature = lax.broadcasted_iota(jnp.int32, (TILE, D), 1)
        lane = lax.broadcasted_iota(jnp.int32, (TILE, D), 0)
        vectors = jnp.zeros((16, D), F32)
        for p, source in enumerate(sources):
            for j in range(slots):
                block = ids[p, j]
                tile = source[j * TILE : (j + 1) * TILE, :]

                @pl.when(block < total)
                def _(block=block, tile=tile):
                    out.held[pl.ds(pl.multiple_of(block * TILE, TILE), TILE), :] = tile

            pick = ((feature == to[p] * lanes + lane) & (lane < lanes)).astype(BF16)
            vectors = vectors + matmul(source[slots * TILE :, :], pick)
        vector_ref[...] = vectors
        out.send()
        for (first, number), ref in zip(GROUPS, groups):
            ref[...] = out[first * TILE : (first + number) * TILE, :]

    args = [Part((piece, 0, slots * TILE + 16)) for piece in pieces]
    outs = [struct((total * TILE, TILE), BF16)] + [Held(struct((number * TILE, TILE), BF16)) for _, number in GROUPS]
    outs.append(struct((16, D), F32))
    return call(kernel, "order_tiles", outs, [], block_ids, ranks, *args)


def deal_tiles(groups, finals, extra, block_ids, ranks, slots, lanes):
    count = ranks.shape[0]
    total = CHUNK * CHUNKS
    rows = slots * TILE + 16
    sizes = [number * TILE for _, number in GROUPS[: len(groups)]]
    order = tuple(reversed(range(len(groups))))

    def kernel(ids, to, *refs):
        done, refs = refs[: len(finals)], refs[len(finals) :]
        sources, refs = refs[: 3 * len(groups)], refs[3 * len(groups) :]
        near_extra, far_extra, v_ref, *outs, held = refs
        held[total * TILE :, :] = jnp.zeros((TILE, TILE), BF16)
        for (block, array), ref in zip(finals, done):
            held[block * TILE : block * TILE + array.shape[0], :] = ref[...]
        for place, at in enumerate(order):
            own, near, far = sources[3 * place : 3 * place + 3]
            first = GROUPS[at][0] * TILE
            held[first : first + sizes[at], :] = (
                own[...].astype(F32) + near[...].astype(F32) + far[...].astype(F32)
            ).astype(BF16)
        summed = (
            v_ref[...].astype(F32) + near_extra[...].astype(F32) + far_extra[...].astype(F32)
        ).astype(BF16)
        summed = jnp.concatenate([summed[16 * j : 16 * (j + 1)] for j in range(4)], axis=1)
        feature = lax.broadcasted_iota(jnp.int32, (D, TILE), 0)
        lane = lax.broadcasted_iota(jnp.int32, (D, TILE), 1)
        for p, out in enumerate(outs):
            for j in range(slots):
                block = jnp.minimum(ids[p, j], total)
                out[j * TILE : (j + 1) * TILE, :] = held[
                    pl.ds(pl.multiple_of(block * TILE, TILE), TILE), :
                ]
            pick = ((feature == to[p] * lanes + lane) & (lane < lanes)).astype(BF16)
            out[slots * TILE :, :] = matmul(summed, pick).astype(BF16)
            send(out)

    flat = [Part((a, 0, sizes[at])) for at in order for a in groups[at]]
    _, near, far = groups[0]
    return call(
        kernel,
        "deal_tiles",
        [Held(struct((rows, TILE), BF16)) if count == 8 else struct((rows, TILE), BF16)] * count,
        [pltpu.VMEM(((total + 1) * TILE, TILE), BF16)],
        block_ids,
        ranks,
        *[Part((a, 0, a.shape[0])) for _, a in finals],
        *flat,
        Part((near, 2 * sizes[0], VECTOR_ROWS)),
        Part((far, sizes[0], VECTOR_ROWS)),
        extra,
    )


def sum_group(own, near, far):
    size = own.shape[0]

    def kernel(own_ref, near_ref, far_ref, out):
        out[...] = (
            own_ref[...].astype(F32) + near_ref[...].astype(F32) + far_ref[...].astype(F32)
        ).astype(BF16)

    return call(kernel, "sum_group", [struct((size, TILE), BF16)], [], *[Part((a, 0, size)) for a in (own, near, far)])[0]


def shampoo(terms, master, left, right, left_root, right_root, vector_master, vector_moment):
    slots = master.shape[1]
    lanes = vector_master.shape[1]

    def split(a):
        high = a.astype(BF16)
        return high, (a - high.astype(F32)).astype(BF16)

    def exact(a, b, dims):
        def product(x, y):
            return lax.dot_general(x, y, (dims, ((), ())), preferred_element_type=F32)

        return product(a[0], b[0]) + (product(a[0], b[1]) + product(a[1], b[0]))

    def kernel(*refs):
        parts, refs = refs[: len(terms)], refs[len(terms) :]
        m_ref, l_ref, r_ref, lr_ref, rr_ref, vm_ref, vn_ref = refs[:7]
        targets, (vg_out, vn_out, vm_out) = refs[7:12], refs[12:15]
        held, sem = refs[15:20], refs[20]

        def rows_at(a, b):
            total = parts[0][a:b, :].astype(F32)
            for part in parts[1:]:
                total = total + part[a:b, :].astype(F32)
            return total

        copies = []
        for s in range(slots):
            g = rows_at(s * TILE, (s + 1) * TILE)
            gs = split(g)
            rotated = exact(split(lr_ref[0, s]), gs, ((1,), (0,)))
            updated = m_ref[0, s] - MATRIX_RATE * exact(split(rotated), split(rr_ref[0, s]), ((1,), (0,)))
            values = (
                g,
                STAT_DECAY * l_ref[0, s] + (1.0 - STAT_DECAY) * exact(gs, gs, ((1,), (1,))),
                STAT_DECAY * r_ref[0, s] + (1.0 - STAT_DECAY) * exact(gs, gs, ((0,), (0,))),
                updated,
                updated.astype(BF16),
            )
            for k, value in enumerate(values):
                held[k][0, s] = value
                copy = pltpu.make_async_copy(held[k].at[0, s], targets[k].at[0, s], sem.at[k, s])
                copy.start()
                copies.append(copy)
        g = rows_at(slots * TILE, slots * TILE + 16)[:10, :lanes]
        moment = STAT_DECAY * vn_ref[...] + (1.0 - STAT_DECAY) * g * g
        vg_out[...] = g
        vn_out[...] = moment
        vm_out[...] = vm_ref[...] - VECTOR_RATE * g / (jnp.sqrt(moment) + 1e-08)
        for copy in copies:
            copy.wait()

    whole = jax.ShapeDtypeStruct(master.shape, F32)
    row = jax.ShapeDtypeStruct(vector_master.shape, F32)
    outs = [whole] * 4 + [jax.ShapeDtypeStruct(master.shape, BF16)] + [row] * 3
    return pl.pallas_call(
        kernel,
        out_shape=outs,
        in_specs=[VM] * (len(terms) + 7),
        out_specs=[HB] * 5 + [VM] * 3,
        scratch_shapes=[
            *[pltpu.VMEM(o.shape, o.dtype) for o in outs[:5]],
            pltpu.SemaphoreType.DMA((5, slots)),
        ],
        compiler_params=pltpu.CompilerParams(vmem_limit_bytes=24 * 2**20),
        name="shampoo",
    )(*terms, master, left, right, left_root, right_root, vector_master, vector_moment)


LOG2E = 1.4426950408889634
SCORE_SCALE = HEAD_DIM ** (-0.5)
SCORE_LOG2 = SCORE_SCALE * LOG2E
PAIRS = HEADS // 2


def matmul(former, latter):
    return jnp.dot(former, latter, preferred_element_type=F32)


def times_transpose(former, latter):
    return lax.dot_general(former, latter, (((1,), (1,)), ((), ())), preferred_element_type=F32)


def transpose_times(former, latter):
    return lax.dot_general(former, latter, (((0,), (0,)), ((), ())), preferred_element_type=F32)


def low(value):
    return value.astype(BF16)


def tile_at(part, index):
    return part[index * TILE : (index + 1) * TILE, :]


def column_matrix(parts, first, count, column):
    return jnp.concatenate(
        [
            jnp.concatenate([tile_at(p, first + a * count + column) for p in parts], axis=1)
            for a in range(4)
        ],
        axis=0,
    )


def row_matrix(parts, first, group):
    return jnp.concatenate(
        [
            jnp.concatenate([tile_at(p, first + 4 * group + b) for b in range(4)], axis=1)
            for p in parts
        ],
        axis=0,
    )


def store_columns(parts, gradient, first, count, column):
    for r, part in enumerate(parts):
        for a in range(4):
            at = (first + a * count + column) * TILE
            part[at : at + TILE, :] = low(
                gradient[a * TILE : (a + 1) * TILE, r * TILE : (r + 1) * TILE]
            )


def store_rows(parts, gradient, first, group):
    for r, part in enumerate(parts):
        for b in range(4):
            at = (first + 4 * group + b) * TILE
            part[at : at + TILE, :] = low(
                gradient[r * TILE : (r + 1) * TILE, b * TILE : (b + 1) * TILE]
            )


def spans(count):
    half = (count // 2 + 15) // 16 * 16
    return [(0, half), (half, count)]


def norm_rows(value):
    mean = jnp.mean(value, axis=-1, keepdims=True)
    centered = value - mean
    scale = lax.rsqrt(jnp.mean(centered * centered, axis=-1, keepdims=True) + NORM_EPSILON)
    return centered * scale, scale


def norm_back(gradient, normed, scale, gain):
    scaled = gradient * gain
    return scale * (
        scaled
        - jnp.mean(scaled, axis=-1, keepdims=True)
        - normed * jnp.mean(scaled * normed, axis=-1, keepdims=True)
    )


def gate_both(value):
    size = jnp.abs(value) * (0.5**0.5)
    turn = 1.0 / (1.0 + 0.3275911 * size)
    bell = jnp.exp2(value * value * (-0.5 * LOG2E))
    series = turn * (
        0.254829592
        + turn * (-0.284496736 + turn * (1.421413741 + turn * (-1.453152027 + turn * 1.061405429)))
    )
    tail = 0.5 * series * bell
    phi = jnp.where(value < 0, tail, 1.0 - tail)
    return value * phi, phi + value * bell * 0.3989422804014327


STATS = 16


def store_stats(stat_ref, stats, *scales):
    if stats is None:
        stats = jnp.zeros((scales[0].shape[0], TILE), F32)
    lane = lax.broadcasted_iota(jnp.int32, stats.shape, 1)
    for at, scale in enumerate(scales):
        stats = jnp.where(lane == HEADS + at, scale, stats)
    stat_ref[...] = stats.T[:STATS, :]


def norm_scales(stat_ref, count):
    columns = jnp.concatenate([stat_ref[...]] * (TILE // STATS), axis=0).T
    return [columns[:, HEADS + at : HEADS + at + 1] for at in range(count)]


def half_mask(which):
    lane = lax.broadcasted_iota(jnp.int32, (1, TILE), 1)
    return (lane < HEAD_DIM) if which == 0 else (lane >= HEAD_DIM)


def attend_pair(queries, key_rows, value_rows, bias, first, stats):
    values = jnp.concatenate([value_rows, jnp.ones_like(value_rows)], axis=1)
    lane = lax.broadcasted_iota(jnp.int32, stats.shape, 1)
    mixed = []
    for which in range(2):
        masked = jnp.where(half_mask(which), queries, jnp.zeros_like(queries))
        scores = times_transpose(masked, key_rows) * SCORE_LOG2
        if bias is not None:
            scores = scores + bias
        top = jnp.max(scores, axis=1, keepdims=True)
        both = matmul(low(jnp.exp2(scores - top)), values)
        total = both[:, TILE:]
        mixed.append(both[:, :TILE] / total)
        stats = jnp.where(lane == first + which, top + jnp.log2(total), stats)
    return low(jnp.where(half_mask(0), mixed[0], mixed[1])), stats


def pair_back(queries, key_rows, value_rows, incoming, stats, deltas, bias):
    key_columns = key_rows.T
    dk = dv = None
    dq = []
    for which in range(2):
        mask = half_mask(which)
        q_one = jnp.where(mask, queries, jnp.zeros_like(queries))
        do_one = jnp.where(mask, incoming, jnp.zeros_like(incoming))
        scores = times_transpose(key_rows, q_one) * SCORE_LOG2
        if bias is not None:
            scores = scores + bias
        weights = jnp.exp2(scores - stats[which])
        d_weights = times_transpose(value_rows, do_one)
        d_scores = low(weights * (d_weights - deltas[which]))
        dv_one = matmul(low(weights), do_one)
        dk_one = matmul(d_scores, q_one)
        dv = dv_one if dv is None else dv + dv_one
        dk = dk_one if dk is None else dk + dk_one
        rows = slice(which * HEAD_DIM, (which + 1) * HEAD_DIM)
        dq.append(low(matmul(key_columns[rows, :], d_scores) * SCORE_SCALE))
    return jnp.concatenate(dq, axis=0).T, low(dk * SCORE_SCALE), low(dv)


def pair_columns(pair):
    return slice(pair * TILE, (pair + 1) * TILE)


def pair_rows(ref, pair):
    return [ref[h : h + 1, :] for h in (2 * pair, 2 * pair + 1)]


def row_products(incoming, mixed):
    product = incoming * mixed
    first = low(product)
    rest = low(product - first.astype(F32))
    lane = lax.broadcasted_iota(jnp.int32, (STATS, product.shape[1]), 1) // HEAD_DIM
    row = lax.broadcasted_iota(jnp.int32, (STATS, product.shape[1]), 0)
    pick = (lane == row).astype(BF16)
    return times_transpose(pick, first) + times_transpose(pick, rest)


def struct(shape, dtype):
    return jax.ShapeDtypeStruct(shape, dtype)


class Inward:
    def __init__(self, source, held, sem):
        self.shape = held.shape
        self.copy, self.held, self.waiting = pltpu.make_async_copy(source, held, sem), held, True
        self.copy.start()

    def wait(self):
        if self.waiting:
            self.copy.wait()
            self.waiting = False

    def __getitem__(self, index):
        self.wait()
        return self.held[index]


class Outward:
    def __init__(self, held, target, sem):
        self.held, self.target, self.sem, self.copies = held, target, sem, []
        self.shape, self.dtype = held.shape, held.dtype

    @property
    def at(self):
        return self.held.at

    def __getitem__(self, index):
        return self.held[index]

    def __setitem__(self, index, value):
        self.held[index] = value

    def send(self, *spans_of):
        for a, b in spans_of or ((0, self.shape[0]),):
            rows = pl.ds(a, b - a)
            copy = pltpu.make_async_copy(
                self.held.at[rows], self.target.at[rows], self.sem.at[len(self.copies)]
            )
            copy.start()
            self.copies.append(copy)

    def finish(self):
        if not self.copies:
            self.send()


def send(out, *spans_of):
    if isinstance(out, Outward):
        out.send(*spans_of)


SENDS = 4


class Part(tuple):
    pass


class Own(tuple):
    pass


class Held:
    def __init__(self, array):
        self.array = array


def call(kernel, name, outs, scratch, *args, flops=0, limit=52):
    plain, held, takes = [], [], []
    for arg in args:
        part = None
        if isinstance(arg, Held):
            plain.append(pltpu.with_memory_space_constraint(arg.array, pltpu.VMEM))
            takes.append(None)
            continue
        free = isinstance(arg, Part)
        if isinstance(arg, Own):
            array, rows = arg
            plain.append(pltpu.with_memory_space_constraint(array, pltpu.HBM))
            takes.append((None, rows, slice(0, array.shape[1]), False))
            held.append(pltpu.VMEM((rows, array.shape[1]), array.dtype))
            continue
        if isinstance(arg, tuple):
            arg, *part = arg
        if arg.dtype == jnp.int32:
            plain.append(arg)
            takes.append(None)
            continue
        plain.append(arg if free else pltpu.with_memory_space_constraint(arg, pltpu.HBM))
        if part is None:
            part = (0, arg.shape[0])
        columns = part[2] if len(part) > 2 else slice(0, arg.shape[1])
        takes.append((part[0], part[1], columns, free))
        held.append(pltpu.VMEM((part[1], columns.stop - columns.start), arg.dtype))
    n, m = len(plain), len(outs)
    sent = [o for o in outs if not isinstance(o, Held)]

    def body(*refs):
        sources, targets, rest = refs[:n], refs[n : n + m], refs[n + m :]
        in_held, rest = list(rest[: len(held)]), rest[len(held) :]
        out_held, rest = list(rest[: len(sent)]), rest[len(sent) :]
        in_sem, out_sem, rest = rest[0], rest[1], rest[2:]
        ins = []
        for source, take in zip(sources, takes):
            if take is None:
                ins.append(source)
                continue
            first, rows, columns, _ = take
            if first is None:
                first = pl.multiple_of(sources[0][0, 0] * rows, 16)
            source = source.at[pl.ds(first, rows), pl.ds(columns.start, columns.stop - columns.start)]
            at = len(held) - len(in_held)
            ins.append(Inward(source, in_held.pop(0), in_sem.at[at]))
        finished = []
        for out, target in zip(outs, targets):
            if not isinstance(out, Held):
                at = len(sent) - len(out_held)
                target = Outward(out_held.pop(0), target, out_sem.at[at])
            finished.append(target)
        kernel(*ins, *finished, *rest)
        for value in ins:
            if isinstance(value, Inward):
                value.wait()
        finished = [f for f in finished if isinstance(f, Outward)]
        for out in finished:
            out.finish()
        for out in finished:
            for copy in out.copies:
                copy.wait()

    shapes = [pltpu.VMEM(o.array.shape, o.array.dtype) if isinstance(o, Held) else pltpu.HBM(o.shape, o.dtype) for o in outs]
    return pl.pallas_call(
        body,
        out_shape=shapes,
        in_specs=[
            SM if a.dtype == jnp.int32 else VM if take is None else ANY if take[3] else HB for a, take in zip(plain, takes)
        ],
        out_specs=[VM if isinstance(o, Held) else HB for o in outs],
        scratch_shapes=[
            *held,
            *[pltpu.VMEM(o.shape, o.dtype) for o in sent],
            pltpu.SemaphoreType.DMA((max(1, len(held)),)),
            pltpu.SemaphoreType.DMA((max(1, len(sent)), SENDS)),
            *scratch,
        ],
        compiler_params=pltpu.CompilerParams(vmem_limit_bytes=limit * 2**20),
        cost_estimate=pl.CostEstimate(flops=flops, bytes_accessed=4000000, transcendentals=0),
        name=name,
    )(*plain)


VECTOR_ROWS = 64


def part_outs(count, extra=0):
    rows = count * TILE
    return [struct((rows, TILE), BF16), Held(struct((2 * rows + extra, TILE), BF16)), Held(struct((rows + extra, TILE), BF16))]


def four_parts(own, near, far):
    rows = own.shape[0]
    return (own, near.at[pl.ds(0, rows)], far, near.at[pl.ds(rows, rows)])


def send_parts(outs, first, count):
    own, near, far = outs
    a, b, rows = first * TILE, (first + count) * TILE, own.shape[0]
    send(near, (a, b), (rows + a, rows + b))
    send(far, (a, b))
    send(own, (a, b))


def rows_of(group, first=0, count=None):
    own, near, far, far_near, at = group
    begin, number = GROUPS[at]
    count = number - first if count is None else count
    start, size = (begin + first) * TILE, count * TILE
    first = first * TILE
    return [Part((own, start, size)), Part((near, start, size)), Part((far, first, size)), Part((far_near, first, size))]


def causal_bias(count, live, queries_on_rows):
    a = lax.broadcasted_iota(jnp.int32, (count, count), 0)
    b = lax.broadcasted_iota(jnp.int32, (count, count), 1)
    query, key = (a, b) if queries_on_rows else (b, a)
    return jnp.where((key <= query) & (key < live), 0.0, MASKED_SCORE)


def tail_rows(length, count):
    return (length - count) // 16 * 16


def column_as_row(column):
    return jnp.broadcast_to(column, (column.shape[0], TILE)).T[:8, :]


def row_as_column(ref):
    return jnp.concatenate([ref[...]] * STATS, axis=0).T[:, :1]


def store_norm(ref, gradient, hat):
    ref[0:1, :] = jnp.sum(gradient * hat, axis=0, keepdims=True)
    ref[1:2, :] = jnp.sum(gradient, axis=0, keepdims=True)


def ffn_weights(ps, first=0):
    w1 = jnp.concatenate([column_matrix(ps, first, 2, c) for c in range(2)], axis=1)
    w2 = jnp.concatenate([row_matrix(ps, first + 8, c) for c in range(2)], axis=0)
    return w1, w2


def heads_weights(part):
    return jnp.concatenate(
        [jnp.concatenate([tile_at(part, 3 * a + c) for c in range(3)], axis=1) for a in range(4)], axis=0
    )


def heads_forward(name, info, rows_all, tiles, first, causal):
    count = 3
    rows = rows_all.shape[0] // count

    def kernel(info_ref, w_ref, *refs):
        xs, (qkv_ref, o_ref, stat_ref, *pieces) = refs[:count], refs[count:]
        weights = heads_weights(w_ref)
        for j in range(count):
            span = slice(j * rows, (j + 1) * rows)
            packed = low(matmul(xs[j][...], weights))
            qkv_ref[span, :] = packed
            qkv_ref.send((span.start, span.stop))
            bias = causal_bias(rows, info_ref[0, 5 + j], True) if causal else None
            mixed, stats = attend_pair(
                packed[:, :TILE], packed[:, TILE : 2 * TILE], packed[:, 2 * TILE :], bias, 0, jnp.zeros((rows, TILE), F32)
            )
            o_ref[span, :] = mixed
            stat_ref[j * STATS : (j + 1) * STATS, :] = stats.T[:STATS, :]
        o_ref.send()
        for r, piece in enumerate(pieces):
            piece[...] = o_ref[pl.ds(pl.multiple_of(info_ref[0, 2 + r] * rows, 16), rows), :]

    outs = [struct((count * rows, 3 * TILE), BF16), struct((count * rows, TILE), BF16)]
    outs += [struct((count * STATS, rows), F32)] + [Held(struct((rows, TILE), BF16))] * 3
    return call(
        kernel, name, outs, [], info, Part((tiles, first * TILE, 12 * TILE)),
        *[(rows_all, j * rows, rows) for j in range(count)], flops=10**10,
    )


def piece_size(share):
    return share if share % 16 == 0 else (share + 15) // 16 * 16 + 16


def heads_backward(name, info, rows_all, tiles, first, qkv, mixed, stats, incoming, causal, piece_rows):
    count = 3
    rows = rows_all.shape[0] // count
    shards = 4
    share = count * rows // shards

    def kernel(info_ref, i0, i1, i2, i3, o_ref, stat_ref, *refs):
        qkvs, xs, (w_ref, own_ref, near_ref, far_ref, tile_ref, do_ref, dx_ref) = (
            refs[:count], refs[count : 2 * count], refs[2 * count :]
        )
        for r, ref in enumerate((i0, i1, i2, i3)):
            do_ref[r * rows : (r + 1) * rows, :] = ref[...]
        total = None
        weights = None
        for j in range(count):
            span = slice(j * rows, (j + 1) * rows)
            do = do_ref[pl.ds(pl.multiple_of(info_ref[0, 9 + j] * rows, 16), rows), :]
            delta = row_products(do.astype(F32), o_ref[span, :].astype(F32))
            packed = qkvs[j][...]
            bias = causal_bias(rows, info_ref[0, 5 + j], False) if causal else None
            at = j * STATS
            grads = pair_back(
                packed[:, :TILE], packed[:, TILE : 2 * TILE], packed[:, 2 * TILE :], do,
                [stat_ref[at : at + 1, :], stat_ref[at + 1 : at + 2, :]], [delta[0:1, :], delta[1:2, :]], bias,
            )
            grads = jnp.concatenate(grads, axis=1)
            gradient = transpose_times(xs[j][...], grads)
            total = gradient if total is None else total + gradient
            if weights is None:
                weights = heads_weights(w_ref)
            dx_ref[span, :] = low(times_transpose(grads, weights))
        for a in range(4):
            for c in range(3):
                at = (3 * a + c) * TILE
                tile_ref[at : at + TILE, :] = low(total[a * TILE : (a + 1) * TILE, c * TILE : (c + 1) * TILE])
        tile_ref.send()
        for r, (ref, at) in enumerate(((near_ref, 0), (near_ref, piece_rows), (far_ref, 0), (own_ref, 0))):
            rank = info_ref[0, 1] ^ (1, 3, 2, 0)[r]
            begin = jnp.minimum(rank * share // 16 * 16, count * rows - piece_rows)
            ref[at : at + piece_rows, :] = dx_ref[pl.ds(pl.multiple_of(begin, 16), piece_rows), :]

    outs = [struct((piece_rows, D), BF16), Held(struct((2 * piece_rows, D), BF16)), struct((piece_rows, D), BF16)]
    outs += [struct((12 * TILE, TILE), BF16)]
    scratch = [pltpu.VMEM((shards * rows, TILE), BF16), pltpu.VMEM((count * rows, D), BF16)]
    return call(
        kernel, name, outs, scratch, info, *incoming, mixed, stats,
        *[(qkv, j * rows, rows) for j in range(count)], *[(rows_all, j * rows, rows) for j in range(count)],
        Part((tiles, first * TILE, 12 * TILE)), flops=2 * 10**10,
    )


def join(refs):
    return jnp.concatenate([r[...] for r in refs], axis=1)


def ffn_forward(info, rows_all, mixed, group, vectors, tail):
    rows = mixed[1].shape[0]

    def kernel(info_ref, o0, o1, o2, o3, p0, p1, p2, p3, x_ref, g_ref,
               enc_ref, hat0_ref, hat_ref, stat_ref, low_ref, hid_ref, slope_ref, tail_ref):
        ps = (p0, p1, p2, p3)
        wo = row_matrix(ps, 0, 0)
        branch = matmul(join((o0, o1, o2, o3)), wo)
        w1, w2 = ffn_weights(ps, 4)
        scales0, scales = [], []
        for a, b in spans(rows):
            hat, scale = norm_rows(x_ref[a:b, :].astype(F32) + branch[a:b])
            scales0.append(scale)
            hat0_ref[a:b, :] = low(hat)
            first_rows = hat * g_ref[0:1, :] + g_ref[1:2, :]
            first_low = low(first_rows)
            low_ref[a:b, :] = first_low
            value, slope = gate_both(matmul(first_low, w1))
            value = low(value)
            hid_ref[a:b, :] = value
            slope_ref[a:b, :] = low(slope)
            for out in (hat0_ref, low_ref, hid_ref, slope_ref):
                out.send((a, b))
            hat, scale = norm_rows(first_rows + matmul(value, w2))
            enc_ref[a:b, :] = low(hat * g_ref[2:3, :] + g_ref[3:4, :])
            hat_ref[a:b, :] = low(hat)
            for out in (hat_ref, enc_ref):
                out.send((a, b))
            scales.append(scale)
        tail_ref[...] = enc_ref[tail:, :]
        store_stats(stat_ref, None, jnp.concatenate(scales0, axis=0), jnp.concatenate(scales, axis=0))

    outs = [struct((rows, D), BF16)] * 3 + [struct((STATS, rows), F32), struct((rows, D), BF16)]
    outs += [struct((rows, FF), BF16)] * 2 + [struct((rows - tail, D), BF16)]
    return call(kernel, "ffn_forward", outs, [], info, Own((mixed[0], rows)), *mixed[1:], *rows_of(group),
                Own((rows_all, rows)), vectors, flops=8 * 10**9)


def cross_forward(info, rows_all, mixed, encoded, group, vectors):
    rows, keys = mixed[1].shape[0], encoded.shape[0]

    def kernel(info_ref, o0, o1, o2, o3, p0, p1, p2, p3, y_ref, e_ref, g_ref,
               third_ref, hat2_ref, low_ref, hat_ref, q_ref, k_ref, v_ref, o_ref, stat_ref):
        ps = (p0, p1, p2, p3)
        hat, scale2 = norm_rows(y_ref[...].astype(F32) + matmul(join((o0, o1, o2, o3)), row_matrix(ps, 0, 0)))
        hat2_ref[...] = low(hat)
        second = hat * g_ref[4:5, :] + g_ref[5:6, :]
        second_low = low(second)
        low_ref[...] = second_low
        third_ref[...] = second
        q_ref[...] = low(matmul(second_low, column_matrix(ps, 4, 1, 0)))
        k_ref[...] = low(matmul(e_ref[...], column_matrix(ps, 8, 2, 0)))
        v_ref[...] = low(matmul(e_ref[...], column_matrix(ps, 8, 2, 1)))
        for ref in (hat2_ref, low_ref, q_ref, k_ref, v_ref):
            ref.send()
        stats = jnp.zeros((rows, TILE), F32)
        for pair in range(PAIRS):
            cut = pair_columns(pair)
            o_ref[:, cut], stats = attend_pair(q_ref[:, cut], k_ref[:, cut], v_ref[:, cut], None, 2 * pair, stats)
        o_ref.send()
        hat, scale = norm_rows(third_ref[...] + matmul(o_ref[...], row_matrix(ps, 16, 0)))
        third_ref[...] = hat * g_ref[6:7, :] + g_ref[7:8, :]
        hat_ref[...] = low(hat)
        hat_ref.send()
        store_stats(stat_ref, stats, scale, scale2)

    outs = [Held(struct((rows, D), F32))] + [struct((rows, D), BF16)] * 3
    outs += [struct((rows, D), BF16), struct((keys, D), BF16), struct((keys, D), BF16)]
    outs += [struct((rows, D), BF16), struct((STATS, rows), F32)]
    return call(kernel, "cross_forward", outs, [], info, Own((mixed[0], rows)), *mixed[1:], *rows_of(group),
                Own((rows_all, rows)), encoded, vectors, flops=8 * 10**9)


def ffn_weight_gradients(inputs, hid_ref, dh_ref, db_ref, grads, outs, first=0):
    for c in range(2):
        store_columns(grads, transpose_times(inputs, dh_ref[:, c * D : (c + 1) * D]), first, 2, c)
    send_parts(outs, first, 8)
    for c in range(2):
        store_rows(grads, transpose_times(hid_ref[:, c * D : (c + 1) * D], db_ref[...]), first + 8, c)
    send_parts(outs, first + 8, 8)


def ffn_both(info, third, cotangent, encoded_tail, group, vectors, tail):
    rows = third.shape[0]

    def kernel(info_ref, t_ref, p0, p1, p2, p3, g_ref, c_own, c_later, e_ref, dec_ref, tail_ref, back_ref, n_ref, d0, d1,
               d2, hid_ref, dh_ref, db_ref, c_ref):
        fill_item(info_ref, c_own, c_later, c_ref)
        w1, w2 = ffn_weights((p0, p1, p2, p3))
        grads = four_parts(d0, d1, d2)
        gain = g_ref[8:9, :]
        n_ref[...] = jnp.zeros_like(n_ref)
        for a, b in spans(rows):
            third_rows = t_ref[a:b, :]
            value, slope = gate_both(matmul(low(third_rows), w1))
            value = low(value)
            hid_ref[a:b, :] = value
            hat, scale = norm_rows(third_rows + matmul(value, w2))
            dec_ref[a:b, :] = low(hat * gain + g_ref[9:10, :])
            dec_ref.send((a, b))
            row = lax.broadcasted_iota(jnp.int32, (b - a, 1), 0) + a
            incoming = jnp.where(row < info_ref[0, 8], c_ref[a:b, :].astype(F32), 0.0)
            n_ref[0:1, :] += jnp.sum(incoming * hat, axis=0, keepdims=True)
            n_ref[1:2, :] += jnp.sum(incoming, axis=0, keepdims=True)
            back = norm_back(incoming, hat, scale, gain)
            back_low = low(back)
            db_ref[a:b, :] = back_low
            dh = low(slope * times_transpose(back_low, w2))
            dh_ref[a:b, :] = dh
            back_ref[a:b, :] = back + times_transpose(dh, w1)
        tail_ref[: encoded_tail.shape[0], :] = e_ref[...]
        tail_ref[encoded_tail.shape[0] :, :] = dec_ref[tail:, :]
        tail_ref.send()
        ffn_weight_gradients(low(t_ref[...]), hid_ref, dh_ref, db_ref, grads, (d0, d1, d2))

    outs = [struct((rows, D), BF16), struct((encoded_tail.shape[0] + rows - tail, D), BF16)]
    outs += [Held(struct((rows, D), F32))]
    outs += [struct((8, D), F32)] + part_outs(16)
    scratch = [pltpu.VMEM((rows, FF), BF16), pltpu.VMEM((rows, FF), BF16)] + [pltpu.VMEM((rows, D), BF16)] * 2
    return call(kernel, "ffn_both", outs, scratch, info, Held(third), *rows_of(group), vectors, *cotangent, encoded_tail,
                flops=10**10)


def norm_and_branch(incoming, hat_rows, scale, gain, n_ref):
    n_ref[...] = jnp.zeros_like(n_ref)
    store_norm(n_ref, incoming, hat_rows)
    branch = norm_back(incoming, hat_rows, scale, gain)
    return branch, low(branch)


def spread_heads(do, refs):
    for r, ref in enumerate(refs):
        ref[...] = do[:, r * TILE : (r + 1) * TILE]
        send(ref)


def cross_backward(info, back, hat, low_rows, encoded, q, k, v, o, stats, hat2, mixed, group, vectors, tail):
    rows, keys = low_rows.shape[0], encoded.shape[0]

    def kernel(info_ref, b_ref, h_ref, stat_ref, g_ref, w0, w1, w2, w3, o_ref, q_ref, k_ref, v_ref, x_ref, e_ref,
               p0, p1, p2, p3, h2_ref, m0, m1, m2, m3,
               de_ref, branch_ref, tail_ref, e0, e1, e2, e3, n_ref, n2_ref, d0, d1, d2, do_ref, dq_ref, dk_ref, dv_ref):
        ps, grads = (p0, p1, p2, p3), four_parts(d0, d1, d2)
        scale, scale2 = norm_scales(stat_ref, 2)
        branch, branch_low = norm_and_branch(b_ref[...], h_ref[...].astype(F32), scale, g_ref[6:7, :], n_ref)
        do = low(times_transpose(branch_low, row_matrix((w0, w1, w2, w3), 0, 0)))
        do_ref[...] = do
        store_rows(grads, transpose_times(o_ref[...], branch_low), 16, 0)
        delta = row_products(do.astype(F32), o_ref[...].astype(F32))
        for pair in range(PAIRS):
            cut = pair_columns(pair)
            dq_ref[:, cut], dk_ref[:, cut], dv_ref[:, cut] = pair_back(
                q_ref[:, cut], k_ref[:, cut], v_ref[:, cut], do_ref[:, cut],
                pair_rows(stat_ref, pair), pair_rows(delta, pair), None,
            )
        incoming = branch + times_transpose(dq_ref[...], column_matrix(ps, 4, 1, 0))
        branch, branch_low = norm_and_branch(incoming, h2_ref[...].astype(F32), scale2, g_ref[4:5, :], n2_ref)
        spread_heads(low(times_transpose(branch_low, row_matrix(ps, 0, 0))), (e0, e1, e2, e3))
        branch_ref[...] = branch_low
        branch_ref.send()
        tail_ref[...] = branch_ref[tail:, :]
        store_rows(grads, transpose_times(join((m0, m1, m2, m3)), branch_low), 0, 0)
        store_columns(grads, transpose_times(x_ref[...], dq_ref[...]), 4, 1, 0)
        et = e_ref[...].T
        store_columns(grads, matmul(et, dk_ref[...]), 8, 2, 0)
        store_columns(grads, matmul(et, dv_ref[...]), 8, 2, 1)
        send_parts((d0, d1, d2), 0, 20)
        de_ref[...] = times_transpose(dk_ref[...], column_matrix(ps, 8, 2, 0)) + times_transpose(
            dv_ref[...], column_matrix(ps, 8, 2, 1)
        )

    outs = [Held(struct((keys, D), F32)), struct((rows, D), BF16), struct((rows - tail, D), BF16)]
    outs += [struct((rows, TILE), BF16)] + [Held(struct((rows, TILE), BF16))] * 3 + [struct((8, D), F32)] * 2 + part_outs(20)
    scratch = [pltpu.VMEM((rows, D), BF16)] * 2 + [pltpu.VMEM((keys, D), BF16)] * 2
    return call(kernel, "cross_backward", outs, scratch, info, Held(back), hat, stats, vectors, *rows_of(group, 16, 4),
                o, q, k, v, low_rows, encoded, *rows_of(group, 0, 16), hat2, Own((mixed[0], rows)), *mixed[1:],
                flops=2 * 10**10)


def ffn_backward(info, cotangent, more, hat, stats, low_rows, hid, slope, hat0, mixed, norms, branch2_tail, group, vectors, tail):
    rows = low_rows.shape[0]

    def kernel(info_ref, m_ref, c_own, c_later, h_ref, stat_ref, g_ref, p0, p1, p2, p3, slope_ref, h0_ref, f_ref, hid_ref,
               m0, m1, m2, m3, n2, n3, n4, t2_ref,
               branch_ref, tail_ref, e0, e1, e2, e3, v_ref, d0, d1, d2, back_ref, dh_ref, db_ref, c_ref, n1_ref, n0_ref):
        fill_item(info_ref, c_own, c_later, c_ref)
        grads = four_parts(d0, d1, d2)
        n1_ref[...] = jnp.zeros_like(n1_ref)
        scale0, scale = norm_scales(stat_ref, 2)
        for a, b in spans(rows):
            incoming = c_ref[a:b, :].astype(F32) + m_ref[a:b, :]
            hat_rows = h_ref[a:b, :].astype(F32)
            n1_ref[0:1, :] += jnp.sum(incoming * hat_rows, axis=0, keepdims=True)
            n1_ref[1:2, :] += jnp.sum(incoming, axis=0, keepdims=True)
            back = norm_back(incoming, hat_rows, scale[a:b], g_ref[2:3, :])
            back_low = low(back)
            db_ref[a:b, :] = back_low
            if not a:
                w1, w2 = ffn_weights((p0, p1, p2, p3), 4)
            dh = low(slope_ref[a:b, :].astype(F32) * times_transpose(back_low, w2))
            dh_ref[a:b, :] = dh
            back_ref[a:b, :] = back + times_transpose(dh, w1)
        branch, branch_low = norm_and_branch(back_ref[...], h0_ref[...].astype(F32), scale0, g_ref[0:1, :], n0_ref)
        spread_heads(low(times_transpose(branch_low, row_matrix((p0, p1, p2, p3), 0, 0))), (e0, e1, e2, e3))
        branch_ref[...] = branch_low
        branch_ref.send()
        tail_ref[: rows - tail, :] = branch_ref[tail:, :]
        tail_ref[rows - tail :, :] = t2_ref[...]
        norms_low = low(jnp.concatenate([n[:2, :] for n in (n0_ref, n1_ref, n2, n3, n4)] + [jnp.zeros((6, D), F32)], axis=0))
        size = d0.shape[0]
        for j in range(4):
            v_ref[16 * j : 16 * (j + 1), :] = norms_low[:, j * TILE : (j + 1) * TILE]
        d1[2 * size :, :] = v_ref[...]
        d2[size:, :] = v_ref[...]
        send(d1, (2 * size, 2 * size + VECTOR_ROWS))
        send(d2, (size, size + VECTOR_ROWS))
        store_rows(grads, transpose_times(join((m0, m1, m2, m3)), branch_low), 0, 0)
        for c in range(2):
            store_columns(grads, transpose_times(f_ref[...], dh_ref[:, c * D : (c + 1) * D]), 4, 2, c)
        send_parts((d0, d1, d2), 0, 12)
        for c in range(2):
            store_rows(grads, transpose_times(hid_ref[:, c * D : (c + 1) * D], db_ref[...]), 12, c)
        send_parts((d0, d1, d2), 12, 8)

    outs = [struct((rows, D), BF16), struct((rows - tail + branch2_tail.shape[0], D), BF16)]
    outs += [struct((rows, TILE), BF16)] + [Held(struct((rows, TILE), BF16))] * 3
    outs += [struct((VECTOR_ROWS, TILE), BF16)] + part_outs(20, VECTOR_ROWS)
    scratch = [pltpu.VMEM((rows, D), F32), pltpu.VMEM((rows, FF), BF16)] + [pltpu.VMEM((rows, D), BF16)] * 2
    scratch += [pltpu.VMEM((8, D), F32)] * 2
    return call(kernel, "ffn_backward", outs, scratch, info, Held(more), *cotangent, hat, stats, vectors, *rows_of(group),
                slope, hat0, low_rows, hid, Own((mixed[0], rows)), *mixed[1:], *norms, branch2_tail, flops=12 * 10**9)


def beside(outs, *arrived):
    both = lax.optimization_barrier((*outs, *arrived))
    return list(both[: len(outs)]), list(both[len(outs) :])


def compute(info, x_all, y_all, image_cotangent, yc, tiles, group_tiles, near, vectors, image_rows, tag_rows):
    items = 3
    image_tail = tail_rows(x_all.shape[0] // items, image_rows)
    tag_tail = tail_rows(y_all.shape[0] // items, tag_rows)

    def far_part(g, *others):
        part = group_tiles[g]
        return lax.ppermute(after(part, *others) if others else part, "tensor", chip_pairs())

    def across(far):
        return lax.ppermute(far, "tensor", core_pairs())

    far_a = far_part(0)
    outs = heads_forward("heads_forward_0", info, x_all, tiles, 0, False)
    (qkv0, mixed0, stats0, *pieces0), (near, far_a, y_all) = beside(outs, near, far_a, y_all)
    mixed0 = spread([mixed0, *pieces0])
    last_a = across(far_a)
    outs = heads_forward("heads_forward_2", info, after(y_all, qkv0), tiles, 32, True)
    (qkv2, mixed2, stats2, *pieces2), (*mixed0, last_a) = beside(outs, *mixed0, last_a)
    mixed2 = spread([mixed2, *pieces2])
    far_b = far_part(1, qkv2)
    outs = ffn_forward(info, after(x_all, qkv2), mixed0, (tiles, near, far_a, last_a, 0), vectors, image_tail)
    (encoded, hat0, hat1, stats1, low1, hid, slope, encoded_tail), (*mixed2, far_b) = beside(outs, *mixed2, far_b)
    last_b = across(far_b)
    far_c = far_part(2, last_b)
    outs = cross_forward(info, after(y_all, last_b), mixed2, encoded, (tiles, near, far_b, last_b, 1), vectors)
    (third, hat2, low2, hat3, q3, k3, v3, o3, stats3), (far_c,) = beside(outs, far_c)
    last_c = across(far_c)
    moved = lax.ppermute(after(image_cotangent, third), "tensor", [(i + 1, i) for i in range(3)])
    outs = ffn_both(info, third, yc, encoded_tail, (tiles, near, far_c, last_c, 2), vectors, tag_tail)
    (decoded, output_tails, back, n4, *part_c), (moved,) = beside(outs, moved)
    near_c = send_near(part_c)
    pushed = push_tails(output_tails)
    outs = cross_backward(
        info, back, hat3, low2, encoded, q3, k3, v3, o3, stats3, hat2, mixed2, (tiles, near, far_b, last_b, 1), vectors,
        tag_tail,
    )
    (d_encoded, branch2, branch2_tail, *rest), (near_c, pushed) = beside(outs, near_c, pushed)
    d_mixed2, (n3, n2), part_b = rest[:4], rest[4:6], rest[6:]
    d_mixed2 = spread(d_mixed2)
    far_sum_c = sum_far(part_c, near_c)
    far_c_sum = send_far(far_sum_c)
    near_b = send_near(part_b)
    outs = ffn_backward(
        info, (after(image_cotangent, far_sum_c), moved), d_encoded, hat1, stats1, low1, hid, slope, hat0, mixed0, (n2, n3, n4), branch2_tail,
        (tiles, near, far_a, last_a, 0), vectors, image_tail,
    )
    (branch0, branch_tails, *rest), (*d_mixed2, near_b, far_c_sum) = beside(outs, *d_mixed2, near_b, far_c_sum)
    d_mixed0, extra, part_a = rest[:4], rest[4], rest[5:]
    d_mixed0 = spread(d_mixed0)
    near_a = send_near(part_a)
    far_sum_b = sum_far(part_b, near_b)
    outs = heads_backward(
        "heads_backward_2", info, after(y_all, far_sum_b), tiles, 32, qkv2, mixed2[0], stats2, d_mixed2, True, piece_size(tag_rows)
    )
    sum_c = sum_group(part_c[0], after(near_c, outs[-1]), far_c_sum)
    outs, (*d_mixed0, near_a, sum_c) = beside(outs, *d_mixed0, near_a, sum_c)
    *dy, tiles2 = outs
    far_sum_a = sum_far(part_a, near_a)
    far_a_sum, far_b_sum = send_far(far_sum_a), send_far(far_sum_b)
    came_y = lax.ppermute(dy[1], "tensor", core_pairs())
    branch_pushed = push_tails(after(branch_tails, tiles2))
    outs = heads_backward(
        "heads_backward_0", info, after(x_all, far_sum_a), tiles, 0, qkv0, mixed0[0], stats0, d_mixed0, False,
        piece_size(image_rows),
    )
    outs, (came_y, far_a, far_b, branch_pushed) = beside(outs, came_y, far_a_sum, far_b_sum, branch_pushed)
    *dx, tiles0 = outs
    dy = [dy[0], came_y, dy[2]]
    groups = [(part_a[0], near_a, far_a), (part_b[0], near_b, far_b)]
    finals = [(GROUPS[2][0], sum_c), (32, tiles2), (0, tiles0)]
    outputs = push_rows((encoded, decoded), pushed, (image_rows, tag_rows), (None, None), info)
    return outputs, (branch0, branch2), branch_pushed, (dx, dy), groups, finals, extra


def one_hot(index, count, dtype):
    return (index[:, None] == lax.broadcasted_iota(jnp.int32, (1, count), 1)).astype(dtype)


def local(
    image_tokens,
    tag_tokens,
    image_cotangent,
    tag_cotangent,
    tag_lengths,
    slot_blocks,
    master_blocks,
    left_factor,
    right_factor,
    left_root,
    right_root,
    vector_master,
    vector_moment,
):
    dp = lax.axis_size("dp")
    shards = lax.axis_size("tensor")
    me = lax.axis_index("tensor")
    slots = master_blocks.shape[1]
    items = tag_lengths.shape[0]
    image_length = image_tokens.shape[0] * shards // items
    item_length = tag_tokens.shape[0] * shards // items
    lanes = vector_master.shape[1]
    def rows_of(value):
        return jnp.pad(value, ((0, 16 - value.shape[0]), (0, TILE - value.shape[1])))

    own = jnp.concatenate(
        [
            master_blocks.astype(BF16).reshape(slots * TILE, TILE),
            rows_of(vector_master.astype(BF16)),
        ],
        axis=0,
    )
    at = lax.broadcasted_iota(jnp.int32, (items,), 0)
    live = jnp.sum(jnp.where(at == me, tag_lengths, 0))
    info = jnp.concatenate(
        [
            jnp.stack([jnp.minimum(me, items - 1), me] + [jnp.minimum(me ^ r, items - 1) for r in (1, 2, 3)]),
            tag_lengths,
            live[None],
            me ^ at,
            jnp.zeros((4,), jnp.int32),
        ]
    ).reshape(1, 16)
    ranks = jnp.stack([relative_rank(p, dp) for p in range(dp)])

    def blocks_of(those):
        picked = one_hot(those, dp, jnp.int32)[:, :, None] * slot_blocks.reshape(1, dp, slots)
        return jnp.sum(picked, axis=1)

    targets = jnp.stack([target_rank(p, dp) for p in range(dp)])
    ready = (info, blocks_of(ranks), blocks_of(targets), ranks, targets)
    pieces, x_all, sequences, moved, ready = gather_rows(
        image_tokens, tag_tokens, tag_cotangent, own, dp,
        lambda parts, info: whole_group(parts, info, "whole_images"), ready
    )
    info, source_blocks, target_blocks, ranks, targets = ready
    y_all = whole_group(sequences, info, "whole_sequences")
    tiles, *group_tiles, vectors = order_tiles(pieces, source_blocks, ranks, slots, lanes)
    near = lax.ppermute(tiles, "tensor", core_pairs())
    images, tags = image_tokens.shape[0], tag_tokens.shape[0]
    outputs, branches, pushed, (dx, dy), groups, finals, extra = compute(
        info, x_all, y_all, image_cotangent, (tag_cotangent, moved), tiles, group_tiles, near, vectors, images, tags
    )
    came_x = lax.ppermute(dx[1], "tensor", core_pairs())
    outgoing = deal_tiles(groups, finals, extra, target_blocks, targets, slots, lanes)
    outgoing, (came_x,) = beside(outgoing, came_x)
    terms, mark = sum_pieces(outgoing, dp)
    came = [came_x, dy[1]]
    far = [
        (part[2].astype(F32) + near_part[part[0].shape[0] :].astype(F32)).astype(BF16)
        for part, near_part in zip((dx, dy), came)
    ]
    far = lax.ppermute(after(jnp.concatenate(far, axis=0), mark), "tensor", chip_pairs())
    sums = [
        ((part[0], 0), (near_part, 0), (far, begin))
        for part, near_part, begin in zip((dx, dy), came, (0, dx[0].shape[0]))
    ]
    rows = push_rows(branches, pushed, (images, tags), sums, info)
    updates = shampoo(
        [*terms[:-1], after(terms[-1], *rows)] if dp == 8 else terms,
        master_blocks,
        left_factor,
        right_factor,
        left_root,
        right_root,
        vector_master,
        vector_moment,
    )
    return (*outputs, *rows, *updates)


def solution(mesh):
    in_specs = (
        P(("dp", "tensor"), None),
        P(("dp", "tensor"), None),
        P(("dp", "tensor"), None),
        P(("dp", "tensor"), None),
        P("dp"),
        P(),
        P("tensor", "dp", None, None),
        P("tensor", "dp", None, None),
        P("tensor", "dp", None, None),
        P("tensor", "dp", None, None),
        P("tensor", "dp", None, None),
        P(None, "dp"),
        P(None, "dp"),
    )
    out_specs = (
        P(("dp", "tensor"), None),
        P(("dp", "tensor"), None),
        P(("dp", "tensor"), None),
        P(("dp", "tensor"), None),
        P("tensor", "dp", None, None),
        P("tensor", "dp", None, None),
        P("tensor", "dp", None, None),
        P("tensor", "dp", None, None),
        P("tensor", "dp", None, None),
        P(None, "dp"),
        P(None, "dp"),
        P(None, "dp"),
    )
    return jax.shard_map(local, mesh=mesh, in_specs=in_specs, out_specs=out_specs, check_vma=False)
```

```python
import jax
import jax.numpy as jnp
from jax import lax
from jax.experimental import pallas as pl
from jax.experimental.pallas import tpu as pltpu
from jax.sharding import PartitionSpec as P

D = 512
HEADS = 8
HEAD_DIM = 64
FF = 1024
TILE = 128
CHUNK = 16
CHUNKS = 5

NORM_EPSILON = 1e-05
MATRIX_RATE = 0.5
VECTOR_RATE = 0.2
STAT_DECAY = 0.5
MASKED_SCORE = -1e30

F32 = jnp.float32
BF16 = jnp.bfloat16
ANY = pl.BlockSpec(memory_space=pl.ANY)
VM = pl.BlockSpec(memory_space=pltpu.VMEM)
SM = pl.BlockSpec(memory_space=pltpu.SMEM)
HB = pl.BlockSpec(memory_space=pltpu.HBM)


def core_pairs():
    return [(i, i ^ 1) for i in range(4)]


def chip_pairs():
    return [(i, i ^ 2) for i in range(4)]


def diagonal_pairs():
    return [(i, i ^ 3) for i in range(4)]


def y_pairs():
    return [(i, i ^ 1) for i in range(8)]


def z_shift(step):
    return [(2 * z + y, 2 * ((z + step) % 4) + y) for z in range(4) for y in range(2)]


def relative_rank(position, size):
    me = lax.axis_index("dp")
    if size != 8:
        return jnp.int32(position)
    swapped, step = divmod(position, 4)
    return 2 * lax.rem(me // 2 - step + 4, 4) + lax.rem(me + swapped, 2)


def target_rank(position, size):
    me = lax.axis_index("dp")
    if size != 8:
        return jnp.int32(position)
    swapped, step = divmod(position, 4)
    return 2 * lax.rem(me // 2 + step, 4) + lax.rem(me + swapped, 2)


def after(value, *others):
    return lax.optimization_barrier((value, *others))[0]


def together(*arrived):
    return lax.optimization_barrier(arrived)


def gather_rows(image, tags, cotangents, piece, size, meanwhile, ready):
    shards = lax.axis_size("tensor")
    split = tags.shape[0]

    def near(value):
        return lax.ppermute(value, "tensor", core_pairs())

    def far(value):
        return lax.ppermute(value, "tensor", chip_pairs())

    def later(value):
        return lax.ppermute(value, "tensor", [(i + 1, i) for i in range(shards - 1)])

    both = jnp.concatenate([tags, image], axis=0)
    if size != 8:
        pieces = list(lax.all_gather(piece, "dp", axis=0, tiled=False))
        near_both, far_image, far_tags = near(both), far(image), far(tags)
        last_image, last_tags, moved = near(far_image), near(far_tags), later(cotangents)
        images = meanwhile([(image, 0), (near_both, split), (far_image, 0), (last_image, 0)], ready[0])
    else:

        def column(part, step):
            return lax.ppermute(part, "dp", z_shift(step))

        def row(part):
            return lax.ppermute(part, "dp", y_pairs())

        one, three, other, far_image, near_both, *ready = together(
            column(piece, 1), column(piece, 3), row(piece), far(image), near(both), *ready
        )
        two, row_one, row_three, far_tags, last_image = together(
            column(after(piece, other), 2), row(one), row(three), far(after(tags, other)), near(far_image)
        )
        images = [(image, 0), (near_both, split), (far_image, 0), (last_image, 0)]
        images, row_two, last_tags, moved = together(
            meanwhile(images, ready[0]), row(two), near(far_tags), later(after(cotangents, two))
        )
        pieces = [piece, one, two, three, other, row_one, row_two, row_three]
    sequences = [(tags, 0), (near_both, 0), (far_tags, 0), (last_tags, 0)]
    return pieces, images, sequences, moved, ready


def sum_pieces(pieces, size):
    if size != 8:
        whole = lax.psum_scatter(
            jnp.stack(pieces).astype(F32), "dp", scatter_dimension=0, tiled=False
        )
        return [whole.astype(BF16)], pieces[0]
    column, ready, mark = [pieces[0]], [], None
    for at, step in enumerate((2, 1, 3, 0)):
        piece = pieces[4 + step]
        if at > 1:
            piece = lax.optimization_barrier((piece, ready[at - 2]))[0]
        other = lax.ppermute(piece, "dp", y_pairs())
        if step == 0:
            column.append(other)
            continue
        both = (pieces[step].astype(F32) + other.astype(F32)).astype(BF16)
        ready.append(both)
        column.append(lax.ppermute(both, "dp", z_shift(step)))
    return column, pieces[0]


GROUPS = ((12, 20), (44, 20), (64, 16))


def send_near(part):
    return lax.ppermute(part[1], "tensor", core_pairs())


def sum_far(part, near):
    rows = part[0].shape[0]
    return (part[2].astype(F32) + near[rows : rows + part[2].shape[0]].astype(F32)).astype(BF16)


def send_far(value):
    return lax.ppermute(value, "tensor", chip_pairs())


def spread(pieces):
    return [
        pieces[0],
        lax.ppermute(pieces[1], "tensor", core_pairs()),
        lax.ppermute(pieces[2], "tensor", chip_pairs()),
        lax.ppermute(pieces[3], "tensor", diagonal_pairs()),
    ]


def whole_group(parts, info, name):
    shards = len(parts)
    count = parts[0][0].shape[0]

    def kernel(info_ref, *refs):
        refs, out = refs[:-1], refs[-1]
        refs = [ref.at[pl.ds(first, count)] for ref, (_, first) in zip(refs, parts)]
        for t in range(shards):

            @pl.when(info_ref[0, 1] == t)
            def _(t=t):
                out[...] = jnp.concatenate([refs[r ^ t][...].astype(F32) for r in range(shards)], axis=0).astype(BF16)

    return pl.pallas_call(
        kernel,
        out_shape=jax.ShapeDtypeStruct((count * shards, D), BF16),
        in_specs=[SM] + [VM] * shards,
        out_specs=VM,
        compiler_params=pltpu.CompilerParams(vmem_limit_bytes=56 * 2**20),
        name=name,
    )(info, *[a for a, _ in parts])


def fill_item(info_ref, own, later, out):
    shards = 4
    own, later = own[...].astype(F32), later[...].astype(F32)
    rows, length = own.shape[0], out.shape[0]
    for t in range(shards):

        @pl.when(info_ref[0, 1] == t)
        def _(t=t):
            if t == shards - 1:
                both = jnp.zeros(out.shape, F32)
            else:
                start = (length - rows) * t
                both = jnp.concatenate([own[start:, :], later[: length - rows + start, :]], axis=0)
            out[...] = both.astype(BF16)


def push_tails(tails):
    shards = lax.axis_size("tensor")
    return lax.ppermute(tails, "tensor", [(i, i + 1) for i in range(shards - 1)])


def push_rows(items, pushed, counts, sums, info):
    shards = lax.axis_size("tensor")
    n = len(items)
    sizes = [item.shape[0] - tail_rows(item.shape[0], count) for item, count in zip(items, counts)]
    extra = [a for terms in sums if terms for a, _ in terms]

    def kernel(info_ref, *refs):
        owns, before, more, outs = refs[:n], refs[n], refs[n + 1 : -n], refs[-n:]
        for t in range(shards):

            @pl.when(info_ref[0, 1] == t)
            def _(t=t):
                used = end = 0
                for own, size, out, terms in zip(owns, sizes, outs, sums):
                    end += size
                    count, length = out.shape[0], own.shape[0]
                    mine = count - (length - count) * t
                    rows = [before[...].astype(F32)[end - count + mine : end, :]] if t else []
                    if mine:
                        rows.append(own[...].astype(F32)[:mine, :])
                    rows = jnp.concatenate(rows, axis=0) if len(rows) > 1 else rows[0]
                    if terms:
                        piece, whole = piece_size(count), count * shards
                        skip = count * t - min(count * t // 16 * 16, whole - piece)
                        added = None
                        for _, begin in terms:
                            term = more[used][begin : begin + piece, :].astype(F32)
                            added = term if added is None else added + term
                            used += 1
                        rows = rows + added[skip : skip + count, :]
                    out[...] = rows.astype(out.dtype)

    return pl.pallas_call(
        kernel,
        out_shape=[jax.ShapeDtypeStruct((c, D), F32 if terms else BF16) for c, terms in zip(counts, sums)],
        in_specs=[SM] + [VM] * (n + 1 + len(extra)),
        out_specs=[VM] * n,
        compiler_params=pltpu.CompilerParams(vmem_limit_bytes=32 * 2**20),
        name="push_gradients" if extra else "push_outputs",
    )(info, *items, pushed, *extra)


def order_tiles(pieces, block_ids, ranks, slots, lanes):
    total = CHUNK * CHUNKS

    def kernel(ids, to, *refs):
        sources, (out, *groups, vector_ref) = refs[: -2 - len(GROUPS)], refs[-2 - len(GROUPS) :]
        feature = lax.broadcasted_iota(jnp.int32, (TILE, D), 1)
        lane = lax.broadcasted_iota(jnp.int32, (TILE, D), 0)
        vectors = jnp.zeros((16, D), F32)
        for p, source in enumerate(sources):
            for j in range(slots):
                block = ids[p, j]
                tile = source[j * TILE : (j + 1) * TILE, :]

                @pl.when(block < total)
                def _(block=block, tile=tile):
                    out.held[pl.ds(pl.multiple_of(block * TILE, TILE), TILE), :] = tile

            pick = ((feature == to[p] * lanes + lane) & (lane < lanes)).astype(BF16)
            vectors = vectors + matmul(source[slots * TILE :, :], pick)
        vector_ref[...] = vectors
        out.send()
        for (first, number), ref in zip(GROUPS, groups):
            ref[...] = out[first * TILE : (first + number) * TILE, :]

    args = [Part((piece, 0, slots * TILE + 16)) for piece in pieces]
    outs = [struct((total * TILE, TILE), BF16)] + [Held(struct((number * TILE, TILE), BF16)) for _, number in GROUPS]
    outs.append(struct((16, D), F32))
    return call(kernel, "order_tiles", outs, [], block_ids, ranks, *args)


def deal_tiles(groups, finals, extra, block_ids, ranks, slots, lanes):
    count = ranks.shape[0]
    total = CHUNK * CHUNKS
    rows = slots * TILE + 16
    sizes = [number * TILE for _, number in GROUPS[: len(groups)]]
    order = tuple(reversed(range(len(groups))))

    def kernel(ids, to, *refs):
        done, refs = refs[: len(finals)], refs[len(finals) :]
        sources, refs = refs[: 3 * len(groups)], refs[3 * len(groups) :]
        near_extra, far_extra, v_ref, *outs, held = refs
        held[total * TILE :, :] = jnp.zeros((TILE, TILE), BF16)
        for (block, array), ref in zip(finals, done):
            held[block * TILE : block * TILE + array.shape[0], :] = ref[...]
        for place, at in enumerate(order):
            own, near, far = sources[3 * place : 3 * place + 3]
            first = GROUPS[at][0] * TILE
            held[first : first + sizes[at], :] = (
                own[...].astype(F32) + near[...].astype(F32) + far[...].astype(F32)
            ).astype(BF16)
        summed = (
            v_ref[...].astype(F32) + near_extra[...].astype(F32) + far_extra[...].astype(F32)
        ).astype(BF16)
        summed = jnp.concatenate([summed[16 * j : 16 * (j + 1)] for j in range(4)], axis=1)
        feature = lax.broadcasted_iota(jnp.int32, (D, TILE), 0)
        lane = lax.broadcasted_iota(jnp.int32, (D, TILE), 1)
        for p, out in enumerate(outs):
            for j in range(slots):
                block = jnp.minimum(ids[p, j], total)
                out[j * TILE : (j + 1) * TILE, :] = held[
                    pl.ds(pl.multiple_of(block * TILE, TILE), TILE), :
                ]
            pick = ((feature == to[p] * lanes + lane) & (lane < lanes)).astype(BF16)
            out[slots * TILE :, :] = matmul(summed, pick).astype(BF16)
            send(out)

    flat = [Part((a, 0, sizes[at])) for at in order for a in groups[at]]
    _, near, far = groups[0]
    return call(
        kernel,
        "deal_tiles",
        [Held(struct((rows, TILE), BF16)) if count == 8 else struct((rows, TILE), BF16)] * count,
        [pltpu.VMEM(((total + 1) * TILE, TILE), BF16)],
        block_ids,
        ranks,
        *[Part((a, 0, a.shape[0])) for _, a in finals],
        *flat,
        Part((near, 2 * sizes[0], VECTOR_ROWS)),
        Part((far, sizes[0], VECTOR_ROWS)),
        extra,
    )


def sum_group(own, near, far):
    size = own.shape[0]

    def kernel(own_ref, near_ref, far_ref, out):
        out[...] = (
            own_ref[...].astype(F32) + near_ref[...].astype(F32) + far_ref[...].astype(F32)
        ).astype(BF16)

    return call(kernel, "sum_group", [struct((size, TILE), BF16)], [], *[Part((a, 0, size)) for a in (own, near, far)])[0]


def shampoo(terms, master, left, right, left_root, right_root, vector_master, vector_moment):
    slots = master.shape[1]
    lanes = vector_master.shape[1]

    def split(a):
        high = a.astype(BF16)
        return high, (a - high.astype(F32)).astype(BF16)

    def exact(a, b, dims):
        def product(x, y):
            return lax.dot_general(x, y, (dims, ((), ())), preferred_element_type=F32)

        return product(a[0], b[0]) + (product(a[0], b[1]) + product(a[1], b[0]))

    def kernel(*refs):
        parts, refs = refs[: len(terms)], refs[len(terms) :]
        m_ref, l_ref, r_ref, lr_ref, rr_ref, vm_ref, vn_ref = refs[:7]
        targets, (vg_out, vn_out, vm_out) = refs[7:12], refs[12:15]
        held, sem = refs[15:20], refs[20]

        def rows_at(a, b):
            total = parts[0][a:b, :].astype(F32)
            for part in parts[1:]:
                total = total + part[a:b, :].astype(F32)
            return total

        copies = []
        for s in range(slots):
            g = rows_at(s * TILE, (s + 1) * TILE)
            gs = split(g)
            rotated = exact(split(lr_ref[0, s]), gs, ((1,), (0,)))
            updated = m_ref[0, s] - MATRIX_RATE * exact(split(rotated), split(rr_ref[0, s]), ((1,), (0,)))
            values = (
                g,
                STAT_DECAY * l_ref[0, s] + (1.0 - STAT_DECAY) * exact(gs, gs, ((1,), (1,))),
                STAT_DECAY * r_ref[0, s] + (1.0 - STAT_DECAY) * exact(gs, gs, ((0,), (0,))),
                updated,
                updated.astype(BF16),
            )
            for k, value in enumerate(values):
                held[k][0, s] = value
                copy = pltpu.make_async_copy(held[k].at[0, s], targets[k].at[0, s], sem.at[k, s])
                copy.start()
                copies.append(copy)
        g = rows_at(slots * TILE, slots * TILE + 16)[:10, :lanes]
        moment = STAT_DECAY * vn_ref[...] + (1.0 - STAT_DECAY) * g * g
        vg_out[...] = g
        vn_out[...] = moment
        vm_out[...] = vm_ref[...] - VECTOR_RATE * g / (jnp.sqrt(moment) + 1e-08)
        for copy in copies:
            copy.wait()

    whole = jax.ShapeDtypeStruct(master.shape, F32)
    row = jax.ShapeDtypeStruct(vector_master.shape, F32)
    outs = [whole] * 4 + [jax.ShapeDtypeStruct(master.shape, BF16)] + [row] * 3
    return pl.pallas_call(
        kernel,
        out_shape=outs,
        in_specs=[VM] * (len(terms) + 7),
        out_specs=[HB] * 5 + [VM] * 3,
        scratch_shapes=[
            *[pltpu.VMEM(o.shape, o.dtype) for o in outs[:5]],
            pltpu.SemaphoreType.DMA((5, slots)),
        ],
        compiler_params=pltpu.CompilerParams(vmem_limit_bytes=24 * 2**20),
        name="shampoo",
    )(*terms, master, left, right, left_root, right_root, vector_master, vector_moment)


LOG2E = 1.4426950408889634
SCORE_SCALE = HEAD_DIM ** (-0.5)
SCORE_LOG2 = SCORE_SCALE * LOG2E
PAIRS = HEADS // 2


def matmul(former, latter):
    return jnp.dot(former, latter, preferred_element_type=F32)


def times_transpose(former, latter):
    return lax.dot_general(former, latter, (((1,), (1,)), ((), ())), preferred_element_type=F32)


def transpose_times(former, latter):
    return lax.dot_general(former, latter, (((0,), (0,)), ((), ())), preferred_element_type=F32)


def low(value):
    return value.astype(BF16)


def tile_at(part, index):
    return part[index * TILE : (index + 1) * TILE, :]


def column_matrix(parts, first, count, column):
    return jnp.concatenate(
        [
            jnp.concatenate([tile_at(p, first + a * count + column) for p in parts], axis=1)
            for a in range(4)
        ],
        axis=0,
    )


def row_matrix(parts, first, group):
    return jnp.concatenate(
        [
            jnp.concatenate([tile_at(p, first + 4 * group + b) for b in range(4)], axis=1)
            for p in parts
        ],
        axis=0,
    )


def store_columns(parts, gradient, first, count, column):
    for r, part in enumerate(parts):
        for a in range(4):
            at = (first + a * count + column) * TILE
            part[at : at + TILE, :] = low(
                gradient[a * TILE : (a + 1) * TILE, r * TILE : (r + 1) * TILE]
            )


def store_rows(parts, gradient, first, group):
    for r, part in enumerate(parts):
        for b in range(4):
            at = (first + 4 * group + b) * TILE
            part[at : at + TILE, :] = low(
                gradient[r * TILE : (r + 1) * TILE, b * TILE : (b + 1) * TILE]
            )


def spans(count):
    half = (count // 2 + 15) // 16 * 16
    return [(0, half), (half, count)]


def norm_rows(value):
    mean = jnp.mean(value, axis=-1, keepdims=True)
    centered = value - mean
    scale = lax.rsqrt(jnp.mean(centered * centered, axis=-1, keepdims=True) + NORM_EPSILON)
    return centered * scale, scale


def norm_back(gradient, normed, scale, gain):
    scaled = gradient * gain
    return scale * (
        scaled
        - jnp.mean(scaled, axis=-1, keepdims=True)
        - normed * jnp.mean(scaled * normed, axis=-1, keepdims=True)
    )


def gate_both(value):
    size = jnp.abs(value) * (0.5**0.5)
    turn = 1.0 / (1.0 + 0.3275911 * size)
    bell = jnp.exp2(value * value * (-0.5 * LOG2E))
    series = turn * (
        0.254829592
        + turn * (-0.284496736 + turn * (1.421413741 + turn * (-1.453152027 + turn * 1.061405429)))
    )
    tail = 0.5 * series * bell
    phi = jnp.where(value < 0, tail, 1.0 - tail)
    return value * phi, phi + value * bell * 0.3989422804014327


STATS = 16


def store_stats(stat_ref, stats, *scales):
    if stats is None:
        stats = jnp.zeros((scales[0].shape[0], TILE), F32)
    lane = lax.broadcasted_iota(jnp.int32, stats.shape, 1)
    for at, scale in enumerate(scales):
        stats = jnp.where(lane == HEADS + at, scale, stats)
    stat_ref[...] = stats.T[:STATS, :]


def norm_scales(stat_ref, count):
    columns = jnp.concatenate([stat_ref[...]] * (TILE // STATS), axis=0).T
    return [columns[:, HEADS + at : HEADS + at + 1] for at in range(count)]


def half_mask(which):
    lane = lax.broadcasted_iota(jnp.int32, (1, TILE), 1)
    return (lane < HEAD_DIM) if which == 0 else (lane >= HEAD_DIM)


def attend_pair(queries, key_rows, value_rows, bias, first, stats):
    values = jnp.concatenate([value_rows, jnp.ones_like(value_rows)], axis=1)
    lane = lax.broadcasted_iota(jnp.int32, stats.shape, 1)
    mixed = []
    for which in range(2):
        masked = jnp.where(half_mask(which), queries, jnp.zeros_like(queries))
        scores = times_transpose(masked, key_rows) * SCORE_LOG2
        if bias is not None:
            scores = scores + bias
        top = jnp.max(scores, axis=1, keepdims=True)
        both = matmul(low(jnp.exp2(scores - top)), values)
        total = both[:, TILE:]
        mixed.append(both[:, :TILE] / total)
        stats = jnp.where(lane == first + which, top + jnp.log2(total), stats)
    return low(jnp.where(half_mask(0), mixed[0], mixed[1])), stats


def pair_back(queries, key_rows, value_rows, incoming, stats, deltas, bias):
    key_columns = key_rows.T
    dk = dv = None
    dq = []
    for which in range(2):
        mask = half_mask(which)
        q_one = jnp.where(mask, queries, jnp.zeros_like(queries))
        do_one = jnp.where(mask, incoming, jnp.zeros_like(incoming))
        scores = times_transpose(key_rows, q_one) * SCORE_LOG2
        if bias is not None:
            scores = scores + bias
        weights = jnp.exp2(scores - stats[which])
        d_weights = times_transpose(value_rows, do_one)
        d_scores = low(weights * (d_weights - deltas[which]))
        dv_one = matmul(low(weights), do_one)
        dk_one = matmul(d_scores, q_one)
        dv = dv_one if dv is None else dv + dv_one
        dk = dk_one if dk is None else dk + dk_one
        rows = slice(which * HEAD_DIM, (which + 1) * HEAD_DIM)
        dq.append(low(matmul(key_columns[rows, :], d_scores) * SCORE_SCALE))
    return jnp.concatenate(dq, axis=0).T, low(dk * SCORE_SCALE), low(dv)


def pair_columns(pair):
    return slice(pair * TILE, (pair + 1) * TILE)


def pair_rows(ref, pair):
    return [ref[h : h + 1, :] for h in (2 * pair, 2 * pair + 1)]


def row_products(incoming, mixed):
    product = incoming * mixed
    first = low(product)
    rest = low(product - first.astype(F32))
    lane = lax.broadcasted_iota(jnp.int32, (STATS, product.shape[1]), 1) // HEAD_DIM
    row = lax.broadcasted_iota(jnp.int32, (STATS, product.shape[1]), 0)
    pick = (lane == row).astype(BF16)
    return times_transpose(pick, first) + times_transpose(pick, rest)


def struct(shape, dtype):
    return jax.ShapeDtypeStruct(shape, dtype)


class Inward:
    def __init__(self, source, held, sem):
        self.shape = held.shape
        self.copy, self.held, self.waiting = pltpu.make_async_copy(source, held, sem), held, True
        self.copy.start()

    def wait(self):
        if self.waiting:
            self.copy.wait()
            self.waiting = False

    def __getitem__(self, index):
        self.wait()
        return self.held[index]


class Outward:
    def __init__(self, held, target, sem):
        self.held, self.target, self.sem, self.copies = held, target, sem, []
        self.shape, self.dtype = held.shape, held.dtype

    @property
    def at(self):
        return self.held.at

    def __getitem__(self, index):
        return self.held[index]

    def __setitem__(self, index, value):
        self.held[index] = value

    def send(self, *spans_of):
        for a, b in spans_of or ((0, self.shape[0]),):
            rows = pl.ds(a, b - a)
            copy = pltpu.make_async_copy(
                self.held.at[rows], self.target.at[rows], self.sem.at[len(self.copies)]
            )
            copy.start()
            self.copies.append(copy)

    def finish(self):
        if not self.copies:
            self.send()


def send(out, *spans_of):
    if isinstance(out, Outward):
        out.send(*spans_of)


SENDS = 4


class Part(tuple):
    pass


class Own(tuple):
    pass


class Held:
    def __init__(self, array):
        self.array = array


def call(kernel, name, outs, scratch, *args, flops=0, limit=52):
    plain, held, takes = [], [], []
    for arg in args:
        part = None
        if isinstance(arg, Held):
            plain.append(pltpu.with_memory_space_constraint(arg.array, pltpu.VMEM))
            takes.append(None)
            continue
        free = isinstance(arg, Part)
        if isinstance(arg, Own):
            array, rows = arg
            plain.append(pltpu.with_memory_space_constraint(array, pltpu.HBM))
            takes.append((None, rows, slice(0, array.shape[1]), False))
            held.append(pltpu.VMEM((rows, array.shape[1]), array.dtype))
            continue
        if isinstance(arg, tuple):
            arg, *part = arg
        if arg.dtype == jnp.int32:
            plain.append(arg)
            takes.append(None)
            continue
        plain.append(arg if free else pltpu.with_memory_space_constraint(arg, pltpu.HBM))
        if part is None:
            part = (0, arg.shape[0])
        columns = part[2] if len(part) > 2 else slice(0, arg.shape[1])
        takes.append((part[0], part[1], columns, free))
        held.append(pltpu.VMEM((part[1], columns.stop - columns.start), arg.dtype))
    n, m = len(plain), len(outs)
    sent = [o for o in outs if not isinstance(o, Held)]

    def body(*refs):
        sources, targets, rest = refs[:n], refs[n : n + m], refs[n + m :]
        in_held, rest = list(rest[: len(held)]), rest[len(held) :]
        out_held, rest = list(rest[: len(sent)]), rest[len(sent) :]
        in_sem, out_sem, rest = rest[0], rest[1], rest[2:]
        ins = []
        for source, take in zip(sources, takes):
            if take is None:
                ins.append(source)
                continue
            first, rows, columns, _ = take
            if first is None:
                first = pl.multiple_of(sources[0][0, 0] * rows, 16)
            source = source.at[pl.ds(first, rows), pl.ds(columns.start, columns.stop - columns.start)]
            at = len(held) - len(in_held)
            ins.append(Inward(source, in_held.pop(0), in_sem.at[at]))
        finished = []
        for out, target in zip(outs, targets):
            if not isinstance(out, Held):
                at = len(sent) - len(out_held)
                target = Outward(out_held.pop(0), target, out_sem.at[at])
            finished.append(target)
        kernel(*ins, *finished, *rest)
        for value in ins:
            if isinstance(value, Inward):
                value.wait()
        finished = [f for f in finished if isinstance(f, Outward)]
        for out in finished:
            out.finish()
        for out in finished:
            for copy in out.copies:
                copy.wait()

    shapes = [pltpu.VMEM(o.array.shape, o.array.dtype) if isinstance(o, Held) else pltpu.HBM(o.shape, o.dtype) for o in outs]
    return pl.pallas_call(
        body,
        out_shape=shapes,
        in_specs=[
            SM if a.dtype == jnp.int32 else VM if take is None else ANY if take[3] else HB for a, take in zip(plain, takes)
        ],
        out_specs=[VM if isinstance(o, Held) else HB for o in outs],
        scratch_shapes=[
            *held,
            *[pltpu.VMEM(o.shape, o.dtype) for o in sent],
            pltpu.SemaphoreType.DMA((max(1, len(held)),)),
            pltpu.SemaphoreType.DMA((max(1, len(sent)), SENDS)),
            *scratch,
        ],
        compiler_params=pltpu.CompilerParams(vmem_limit_bytes=limit * 2**20),
        cost_estimate=pl.CostEstimate(flops=flops, bytes_accessed=4000000, transcendentals=0),
        name=name,
    )(*plain)


VECTOR_ROWS = 64


def part_outs(count, extra=0):
    rows = count * TILE
    return [struct((rows, TILE), BF16), Held(struct((2 * rows + extra, TILE), BF16)), Held(struct((rows + extra, TILE), BF16))]


def four_parts(own, near, far):
    rows = own.shape[0]
    return (own, near.at[pl.ds(0, rows)], far, near.at[pl.ds(rows, rows)])


def send_parts(outs, first, count):
    own, near, far = outs
    a, b, rows = first * TILE, (first + count) * TILE, own.shape[0]
    send(near, (a, b), (rows + a, rows + b))
    send(far, (a, b))
    send(own, (a, b))


def rows_of(group, first=0, count=None):
    own, near, far, far_near, at = group
    begin, number = GROUPS[at]
    count = number - first if count is None else count
    start, size = (begin + first) * TILE, count * TILE
    first = first * TILE
    return [Part((own, start, size)), Part((near, start, size)), Part((far, first, size)), Part((far_near, first, size))]


def causal_bias(count, live, queries_on_rows):
    a = lax.broadcasted_iota(jnp.int32, (count, count), 0)
    b = lax.broadcasted_iota(jnp.int32, (count, count), 1)
    query, key = (a, b) if queries_on_rows else (b, a)
    return jnp.where((key <= query) & (key < live), 0.0, MASKED_SCORE)


def tail_rows(length, count):
    return (length - count) // 16 * 16


def column_as_row(column):
    return jnp.broadcast_to(column, (column.shape[0], TILE)).T[:8, :]


def row_as_column(ref):
    return jnp.concatenate([ref[...]] * STATS, axis=0).T[:, :1]


def store_norm(ref, gradient, hat):
    ref[0:1, :] = jnp.sum(gradient * hat, axis=0, keepdims=True)
    ref[1:2, :] = jnp.sum(gradient, axis=0, keepdims=True)


def ffn_weights(ps, first=0):
    w1 = jnp.concatenate([column_matrix(ps, first, 2, c) for c in range(2)], axis=1)
    w2 = jnp.concatenate([row_matrix(ps, first + 8, c) for c in range(2)], axis=0)
    return w1, w2


def heads_weights(part):
    return jnp.concatenate(
        [jnp.concatenate([tile_at(part, 3 * a + c) for c in range(3)], axis=1) for a in range(4)], axis=0
    )


def heads_forward(name, info, rows_all, tiles, first, causal):
    count = 3
    rows = rows_all.shape[0] // count

    def kernel(info_ref, w_ref, *refs):
        xs, (qkv_ref, o_ref, stat_ref, *pieces) = refs[:count], refs[count:]
        weights = heads_weights(w_ref)
        for j in range(count):
            span = slice(j * rows, (j + 1) * rows)
            packed = low(matmul(xs[j][...], weights))
            qkv_ref[span, :] = packed
            qkv_ref.send((span.start, span.stop))
            bias = causal_bias(rows, info_ref[0, 5 + j], True) if causal else None
            mixed, stats = attend_pair(
                packed[:, :TILE], packed[:, TILE : 2 * TILE], packed[:, 2 * TILE :], bias, 0, jnp.zeros((rows, TILE), F32)
            )
            o_ref[span, :] = mixed
            stat_ref[j * STATS : (j + 1) * STATS, :] = stats.T[:STATS, :]
        o_ref.send()
        for r, piece in enumerate(pieces):
            piece[...] = o_ref[pl.ds(pl.multiple_of(info_ref[0, 2 + r] * rows, 16), rows), :]

    outs = [struct((count * rows, 3 * TILE), BF16), struct((count * rows, TILE), BF16)]
    outs += [struct((count * STATS, rows), F32)] + [Held(struct((rows, TILE), BF16))] * 3
    return call(
        kernel, name, outs, [], info, Part((tiles, first * TILE, 12 * TILE)),
        *[(rows_all, j * rows, rows) for j in range(count)], flops=10**10,
    )


def piece_size(share):
    return share if share % 16 == 0 else (share + 15) // 16 * 16 + 16


def heads_backward(name, info, rows_all, tiles, first, qkv, mixed, stats, incoming, causal, piece_rows):
    count = 3
    rows = rows_all.shape[0] // count
    shards = 4
    share = count * rows // shards

    def kernel(info_ref, i0, i1, i2, i3, o_ref, stat_ref, *refs):
        qkvs, xs, (w_ref, own_ref, near_ref, far_ref, tile_ref, do_ref, dx_ref) = (
            refs[:count], refs[count : 2 * count], refs[2 * count :]
        )
        for r, ref in enumerate((i0, i1, i2, i3)):
            do_ref[r * rows : (r + 1) * rows, :] = ref[...]
        total = None
        weights = None
        for j in range(count):
            span = slice(j * rows, (j + 1) * rows)
            do = do_ref[pl.ds(pl.multiple_of(info_ref[0, 9 + j] * rows, 16), rows), :]
            delta = row_products(do.astype(F32), o_ref[span, :].astype(F32))
            packed = qkvs[j][...]
            bias = causal_bias(rows, info_ref[0, 5 + j], False) if causal else None
            at = j * STATS
            grads = pair_back(
                packed[:, :TILE], packed[:, TILE : 2 * TILE], packed[:, 2 * TILE :], do,
                [stat_ref[at : at + 1, :], stat_ref[at + 1 : at + 2, :]], [delta[0:1, :], delta[1:2, :]], bias,
            )
            grads = jnp.concatenate(grads, axis=1)
            gradient = transpose_times(xs[j][...], grads)
            total = gradient if total is None else total + gradient
            if weights is None:
                weights = heads_weights(w_ref)
            dx_ref[span, :] = low(times_transpose(grads, weights))
        for a in range(4):
            for c in range(3):
                at = (3 * a + c) * TILE
                tile_ref[at : at + TILE, :] = low(total[a * TILE : (a + 1) * TILE, c * TILE : (c + 1) * TILE])
        tile_ref.send()
        for r, (ref, at) in enumerate(((near_ref, 0), (near_ref, piece_rows), (far_ref, 0), (own_ref, 0))):
            rank = info_ref[0, 1] ^ (1, 3, 2, 0)[r]
            begin = jnp.minimum(rank * share // 16 * 16, count * rows - piece_rows)
            ref[at : at + piece_rows, :] = dx_ref[pl.ds(pl.multiple_of(begin, 16), piece_rows), :]

    outs = [struct((piece_rows, D), BF16), Held(struct((2 * piece_rows, D), BF16)), struct((piece_rows, D), BF16)]
    outs += [struct((12 * TILE, TILE), BF16)]
    scratch = [pltpu.VMEM((shards * rows, TILE), BF16), pltpu.VMEM((count * rows, D), BF16)]
    return call(
        kernel, name, outs, scratch, info, *incoming, mixed, stats,
        *[(qkv, j * rows, rows) for j in range(count)], *[(rows_all, j * rows, rows) for j in range(count)],
        Part((tiles, first * TILE, 12 * TILE)), flops=2 * 10**10,
    )


def join(refs):
    return jnp.concatenate([r[...] for r in refs], axis=1)


def ffn_forward(info, rows_all, mixed, group, vectors, tail):
    rows = mixed[1].shape[0]

    def kernel(info_ref, o0, o1, o2, o3, p0, p1, p2, p3, x_ref, g_ref,
               enc_ref, hat0_ref, hat_ref, stat_ref, low_ref, hid_ref, slope_ref, tail_ref):
        ps = (p0, p1, p2, p3)
        wo = row_matrix(ps, 0, 0)
        branch = matmul(join((o0, o1, o2, o3)), wo)
        w1, w2 = ffn_weights(ps, 4)
        scales0, scales = [], []
        for a, b in spans(rows):
            hat, scale = norm_rows(x_ref[a:b, :].astype(F32) + branch[a:b])
            scales0.append(scale)
            hat0_ref[a:b, :] = low(hat)
            first_rows = hat * g_ref[0:1, :] + g_ref[1:2, :]
            first_low = low(first_rows)
            low_ref[a:b, :] = first_low
            value, slope = gate_both(matmul(first_low, w1))
            value = low(value)
            hid_ref[a:b, :] = value
            slope_ref[a:b, :] = low(slope)
            for out in (hat0_ref, low_ref, hid_ref, slope_ref):
                out.send((a, b))
            hat, scale = norm_rows(first_rows + matmul(value, w2))
            enc_ref[a:b, :] = low(hat * g_ref[2:3, :] + g_ref[3:4, :])
            hat_ref[a:b, :] = low(hat)
            for out in (hat_ref, enc_ref):
                out.send((a, b))
            scales.append(scale)
        tail_ref[...] = enc_ref[tail:, :]
        store_stats(stat_ref, None, jnp.concatenate(scales0, axis=0), jnp.concatenate(scales, axis=0))

    outs = [struct((rows, D), BF16)] * 3 + [struct((STATS, rows), F32), struct((rows, D), BF16)]
    outs += [struct((rows, FF), BF16)] * 2 + [struct((rows - tail, D), BF16)]
    return call(kernel, "ffn_forward", outs, [], info, Own((mixed[0], rows)), *mixed[1:], *rows_of(group),
                Own((rows_all, rows)), vectors, flops=8 * 10**9)


def cross_forward(info, rows_all, mixed, encoded, group, vectors):
    rows, keys = mixed[1].shape[0], encoded.shape[0]

    def kernel(info_ref, o0, o1, o2, o3, p0, p1, p2, p3, y_ref, e_ref, g_ref,
               third_ref, hat2_ref, low_ref, hat_ref, q_ref, k_ref, v_ref, o_ref, stat_ref):
        ps = (p0, p1, p2, p3)
        hat, scale2 = norm_rows(y_ref[...].astype(F32) + matmul(join((o0, o1, o2, o3)), row_matrix(ps, 0, 0)))
        hat2_ref[...] = low(hat)
        second = hat * g_ref[4:5, :] + g_ref[5:6, :]
        second_low = low(second)
        low_ref[...] = second_low
        third_ref[...] = second
        q_ref[...] = low(matmul(second_low, column_matrix(ps, 4, 1, 0)))
        k_ref[...] = low(matmul(e_ref[...], column_matrix(ps, 8, 2, 0)))
        v_ref[...] = low(matmul(e_ref[...], column_matrix(ps, 8, 2, 1)))
        for ref in (hat2_ref, low_ref, q_ref, k_ref, v_ref):
            ref.send()
        stats = jnp.zeros((rows, TILE), F32)
        for pair in range(PAIRS):
            cut = pair_columns(pair)
            o_ref[:, cut], stats = attend_pair(q_ref[:, cut], k_ref[:, cut], v_ref[:, cut], None, 2 * pair, stats)
        o_ref.send()
        hat, scale = norm_rows(third_ref[...] + matmul(o_ref[...], row_matrix(ps, 16, 0)))
        third_ref[...] = hat * g_ref[6:7, :] + g_ref[7:8, :]
        hat_ref[...] = low(hat)
        hat_ref.send()
        store_stats(stat_ref, stats, scale, scale2)

    outs = [Held(struct((rows, D), F32))] + [struct((rows, D), BF16)] * 3
    outs += [struct((rows, D), BF16), struct((keys, D), BF16), struct((keys, D), BF16)]
    outs += [struct((rows, D), BF16), struct((STATS, rows), F32)]
    return call(kernel, "cross_forward", outs, [], info, Own((mixed[0], rows)), *mixed[1:], *rows_of(group),
                Own((rows_all, rows)), encoded, vectors, flops=8 * 10**9)


def ffn_weight_gradients(inputs, hid_ref, dh_ref, db_ref, grads, outs, first=0):
    for c in range(2):
        store_columns(grads, transpose_times(inputs, dh_ref[:, c * D : (c + 1) * D]), first, 2, c)
    send_parts(outs, first, 8)
    for c in range(2):
        store_rows(grads, transpose_times(hid_ref[:, c * D : (c + 1) * D], db_ref[...]), first + 8, c)
    send_parts(outs, first + 8, 8)


def ffn_both(info, third, cotangent, encoded_tail, group, vectors, tail):
    rows = third.shape[0]

    def kernel(info_ref, t_ref, p0, p1, p2, p3, g_ref, c_own, c_later, e_ref, dec_ref, tail_ref, back_ref, n_ref, d0, d1,
               d2, hid_ref, dh_ref, db_ref, c_ref):
        fill_item(info_ref, c_own, c_later, c_ref)
        w1, w2 = ffn_weights((p0, p1, p2, p3))
        grads = four_parts(d0, d1, d2)
        gain = g_ref[8:9, :]
        n_ref[...] = jnp.zeros_like(n_ref)
        for a, b in spans(rows):
            third_rows = t_ref[a:b, :]
            value, slope = gate_both(matmul(low(third_rows), w1))
            value = low(value)
            hid_ref[a:b, :] = value
            hat, scale = norm_rows(third_rows + matmul(value, w2))
            dec_ref[a:b, :] = low(hat * gain + g_ref[9:10, :])
            dec_ref.send((a, b))
            row = lax.broadcasted_iota(jnp.int32, (b - a, 1), 0) + a
            incoming = jnp.where(row < info_ref[0, 8], c_ref[a:b, :].astype(F32), 0.0)
            n_ref[0:1, :] += jnp.sum(incoming * hat, axis=0, keepdims=True)
            n_ref[1:2, :] += jnp.sum(incoming, axis=0, keepdims=True)
            back = norm_back(incoming, hat, scale, gain)
            back_low = low(back)
            db_ref[a:b, :] = back_low
            dh = low(slope * times_transpose(back_low, w2))
            dh_ref[a:b, :] = dh
            back_ref[a:b, :] = back + times_transpose(dh, w1)
        tail_ref[: encoded_tail.shape[0], :] = e_ref[...]
        tail_ref[encoded_tail.shape[0] :, :] = dec_ref[tail:, :]
        tail_ref.send()
        ffn_weight_gradients(low(t_ref[...]), hid_ref, dh_ref, db_ref, grads, (d0, d1, d2))

    outs = [struct((rows, D), BF16), struct((encoded_tail.shape[0] + rows - tail, D), BF16)]
    outs += [Held(struct((rows, D), F32))]
    outs += [struct((8, D), F32)] + part_outs(16)
    scratch = [pltpu.VMEM((rows, FF), BF16), pltpu.VMEM((rows, FF), BF16)] + [pltpu.VMEM((rows, D), BF16)] * 2
    return call(kernel, "ffn_both", outs, scratch, info, Held(third), *rows_of(group), vectors, *cotangent, encoded_tail,
                flops=10**10)


def norm_and_branch(incoming, hat_rows, scale, gain, n_ref):
    n_ref[...] = jnp.zeros_like(n_ref)
    store_norm(n_ref, incoming, hat_rows)
    branch = norm_back(incoming, hat_rows, scale, gain)
    return branch, low(branch)


def spread_heads(do, refs):
    for r, ref in enumerate(refs):
        ref[...] = do[:, r * TILE : (r + 1) * TILE]
        send(ref)


def cross_backward(info, back, hat, low_rows, encoded, q, k, v, o, stats, hat2, mixed, group, vectors, tail):
    rows, keys = low_rows.shape[0], encoded.shape[0]

    def kernel(info_ref, b_ref, h_ref, stat_ref, g_ref, w0, w1, w2, w3, o_ref, q_ref, k_ref, v_ref, x_ref, e_ref,
               p0, p1, p2, p3, h2_ref, m0, m1, m2, m3,
               de_ref, branch_ref, tail_ref, e0, e1, e2, e3, n_ref, n2_ref, d0, d1, d2, do_ref, dq_ref, dk_ref, dv_ref):
        ps, grads = (p0, p1, p2, p3), four_parts(d0, d1, d2)
        scale, scale2 = norm_scales(stat_ref, 2)
        branch, branch_low = norm_and_branch(b_ref[...], h_ref[...].astype(F32), scale, g_ref[6:7, :], n_ref)
        do = low(times_transpose(branch_low, row_matrix((w0, w1, w2, w3), 0, 0)))
        do_ref[...] = do
        store_rows(grads, transpose_times(o_ref[...], branch_low), 16, 0)
        delta = row_products(do.astype(F32), o_ref[...].astype(F32))
        for pair in range(PAIRS):
            cut = pair_columns(pair)
            dq_ref[:, cut], dk_ref[:, cut], dv_ref[:, cut] = pair_back(
                q_ref[:, cut], k_ref[:, cut], v_ref[:, cut], do_ref[:, cut],
                pair_rows(stat_ref, pair), pair_rows(delta, pair), None,
            )
        incoming = branch + times_transpose(dq_ref[...], column_matrix(ps, 4, 1, 0))
        branch, branch_low = norm_and_branch(incoming, h2_ref[...].astype(F32), scale2, g_ref[4:5, :], n2_ref)
        spread_heads(low(times_transpose(branch_low, row_matrix(ps, 0, 0))), (e0, e1, e2, e3))
        branch_ref[...] = branch_low
        branch_ref.send()
        tail_ref[...] = branch_ref[tail:, :]
        store_rows(grads, transpose_times(join((m0, m1, m2, m3)), branch_low), 0, 0)
        store_columns(grads, transpose_times(x_ref[...], dq_ref[...]), 4, 1, 0)
        et = e_ref[...].T
        store_columns(grads, matmul(et, dk_ref[...]), 8, 2, 0)
        store_columns(grads, matmul(et, dv_ref[...]), 8, 2, 1)
        send_parts((d0, d1, d2), 0, 20)
        de_ref[...] = times_transpose(dk_ref[...], column_matrix(ps, 8, 2, 0)) + times_transpose(
            dv_ref[...], column_matrix(ps, 8, 2, 1)
        )

    outs = [Held(struct((keys, D), F32)), struct((rows, D), BF16), struct((rows - tail, D), BF16)]
    outs += [struct((rows, TILE), BF16)] + [Held(struct((rows, TILE), BF16))] * 3 + [struct((8, D), F32)] * 2 + part_outs(20)
    scratch = [pltpu.VMEM((rows, D), BF16)] * 2 + [pltpu.VMEM((keys, D), BF16)] * 2
    return call(kernel, "cross_backward", outs, scratch, info, Held(back), hat, stats, vectors, *rows_of(group, 16, 4),
                o, q, k, v, low_rows, encoded, *rows_of(group, 0, 16), hat2, Own((mixed[0], rows)), *mixed[1:],
                flops=2 * 10**10)


def ffn_backward(info, cotangent, more, hat, stats, low_rows, hid, slope, hat0, mixed, norms, branch2_tail, group, vectors, tail):
    rows = low_rows.shape[0]

    def kernel(info_ref, m_ref, c_own, c_later, h_ref, stat_ref, g_ref, p0, p1, p2, p3, slope_ref, h0_ref, f_ref, hid_ref,
               m0, m1, m2, m3, n2, n3, n4, t2_ref,
               branch_ref, tail_ref, e0, e1, e2, e3, v_ref, d0, d1, d2, back_ref, dh_ref, db_ref, c_ref, n1_ref, n0_ref):
        fill_item(info_ref, c_own, c_later, c_ref)
        grads = four_parts(d0, d1, d2)
        n1_ref[...] = jnp.zeros_like(n1_ref)
        scale0, scale = norm_scales(stat_ref, 2)
        for a, b in spans(rows):
            incoming = c_ref[a:b, :].astype(F32) + m_ref[a:b, :]
            hat_rows = h_ref[a:b, :].astype(F32)
            n1_ref[0:1, :] += jnp.sum(incoming * hat_rows, axis=0, keepdims=True)
            n1_ref[1:2, :] += jnp.sum(incoming, axis=0, keepdims=True)
            back = norm_back(incoming, hat_rows, scale[a:b], g_ref[2:3, :])
            back_low = low(back)
            db_ref[a:b, :] = back_low
            if not a:
                w1, w2 = ffn_weights((p0, p1, p2, p3), 4)
            dh = low(slope_ref[a:b, :].astype(F32) * times_transpose(back_low, w2))
            dh_ref[a:b, :] = dh
            back_ref[a:b, :] = back + times_transpose(dh, w1)
        branch, branch_low = norm_and_branch(back_ref[...], h0_ref[...].astype(F32), scale0, g_ref[0:1, :], n0_ref)
        spread_heads(low(times_transpose(branch_low, row_matrix((p0, p1, p2, p3), 0, 0))), (e0, e1, e2, e3))
        branch_ref[...] = branch_low
        branch_ref.send()
        tail_ref[: rows - tail, :] = branch_ref[tail:, :]
        tail_ref[rows - tail :, :] = t2_ref[...]
        norms_low = low(jnp.concatenate([n[:2, :] for n in (n0_ref, n1_ref, n2, n3, n4)] + [jnp.zeros((6, D), F32)], axis=0))
        size = d0.shape[0]
        for j in range(4):
            v_ref[16 * j : 16 * (j + 1), :] = norms_low[:, j * TILE : (j + 1) * TILE]
        d1[2 * size :, :] = v_ref[...]
        d2[size:, :] = v_ref[...]
        send(d1, (2 * size, 2 * size + VECTOR_ROWS))
        send(d2, (size, size + VECTOR_ROWS))
        store_rows(grads, transpose_times(join((m0, m1, m2, m3)), branch_low), 0, 0)
        for c in range(2):
            store_columns(grads, transpose_times(f_ref[...], dh_ref[:, c * D : (c + 1) * D]), 4, 2, c)
        send_parts((d0, d1, d2), 0, 12)
        for c in range(2):
            store_rows(grads, transpose_times(hid_ref[:, c * D : (c + 1) * D], db_ref[...]), 12, c)
        send_parts((d0, d1, d2), 12, 8)

    outs = [struct((rows, D), BF16), struct((rows - tail + branch2_tail.shape[0], D), BF16)]
    outs += [struct((rows, TILE), BF16)] + [Held(struct((rows, TILE), BF16))] * 3
    outs += [struct((VECTOR_ROWS, TILE), BF16)] + part_outs(20, VECTOR_ROWS)
    scratch = [pltpu.VMEM((rows, D), F32), pltpu.VMEM((rows, FF), BF16)] + [pltpu.VMEM((rows, D), BF16)] * 2
    scratch += [pltpu.VMEM((8, D), F32)] * 2
    return call(kernel, "ffn_backward", outs, scratch, info, Held(more), *cotangent, hat, stats, vectors, *rows_of(group),
                slope, hat0, low_rows, hid, Own((mixed[0], rows)), *mixed[1:], *norms, branch2_tail, flops=12 * 10**9)


def beside(outs, *arrived):
    both = lax.optimization_barrier((*outs, *arrived))
    return list(both[: len(outs)]), list(both[len(outs) :])


def compute(info, x_all, y_all, image_cotangent, yc, tiles, group_tiles, near, vectors, image_rows, tag_rows):
    items = 3
    image_tail = tail_rows(x_all.shape[0] // items, image_rows)
    tag_tail = tail_rows(y_all.shape[0] // items, tag_rows)

    def far_part(g, *others):
        part = group_tiles[g]
        return lax.ppermute(after(part, *others) if others else part, "tensor", chip_pairs())

    def across(far):
        return lax.ppermute(far, "tensor", core_pairs())

    far_a = far_part(0)
    outs = heads_forward("heads_forward_0", info, x_all, tiles, 0, False)
    (qkv0, mixed0, stats0, *pieces0), (near, far_a, y_all) = beside(outs, near, far_a, y_all)
    mixed0 = spread([mixed0, *pieces0])
    last_a = across(far_a)
    outs = heads_forward("heads_forward_2", info, after(y_all, qkv0), tiles, 32, True)
    (qkv2, mixed2, stats2, *pieces2), (*mixed0, last_a) = beside(outs, *mixed0, last_a)
    mixed2 = spread([mixed2, *pieces2])
    far_b = far_part(1, qkv2)
    outs = ffn_forward(info, after(x_all, qkv2), mixed0, (tiles, near, far_a, last_a, 0), vectors, image_tail)
    (encoded, hat0, hat1, stats1, low1, hid, slope, encoded_tail), (*mixed2, far_b) = beside(outs, *mixed2, far_b)
    last_b = across(far_b)
    far_c = far_part(2, last_b)
    outs = cross_forward(info, after(y_all, last_b), mixed2, encoded, (tiles, near, far_b, last_b, 1), vectors)
    (third, hat2, low2, hat3, q3, k3, v3, o3, stats3), (far_c,) = beside(outs, far_c)
    last_c = across(far_c)
    moved = lax.ppermute(after(image_cotangent, third), "tensor", [(i + 1, i) for i in range(3)])
    outs = ffn_both(info, third, yc, encoded_tail, (tiles, near, far_c, last_c, 2), vectors, tag_tail)
    (decoded, output_tails, back, n4, *part_c), (moved,) = beside(outs, moved)
    near_c = send_near(part_c)
    pushed = push_tails(output_tails)
    outs = cross_backward(
        info, back, hat3, low2, encoded, q3, k3, v3, o3, stats3, hat2, mixed2, (tiles, near, far_b, last_b, 1), vectors,
        tag_tail,
    )
    (d_encoded, branch2, branch2_tail, *rest), (near_c, pushed) = beside(outs, near_c, pushed)
    d_mixed2, (n3, n2), part_b = rest[:4], rest[4:6], rest[6:]
    d_mixed2 = spread(d_mixed2)
    far_sum_c = sum_far(part_c, near_c)
    far_c_sum = send_far(far_sum_c)
    near_b = send_near(part_b)
    outs = ffn_backward(
        info, (after(image_cotangent, far_sum_c), moved), d_encoded, hat1, stats1, low1, hid, slope, hat0, mixed0, (n2, n3, n4), branch2_tail,
        (tiles, near, far_a, last_a, 0), vectors, image_tail,
    )
    (branch0, branch_tails, *rest), (*d_mixed2, near_b, far_c_sum) = beside(outs, *d_mixed2, near_b, far_c_sum)
    d_mixed0, extra, part_a = rest[:4], rest[4], rest[5:]
    d_mixed0 = spread(d_mixed0)
    near_a = send_near(part_a)
    far_sum_b = sum_far(part_b, after(near_b, d_mixed0[1]))
    outs = heads_backward(
        "heads_backward_2", info, after(y_all, far_sum_b), tiles, 32, qkv2, mixed2[0], stats2, d_mixed2, True, piece_size(tag_rows)
    )
    sum_c = sum_group(part_c[0], after(near_c, outs[-1]), far_c_sum)
    outs, (*d_mixed0, near_a, sum_c) = beside(outs, *d_mixed0, near_a, sum_c)
    *dy, tiles2 = outs
    far_sum_a = sum_far(part_a, near_a)
    far_a_sum, far_b_sum = send_far(far_sum_a), send_far(far_sum_b)
    came_y = lax.ppermute(dy[1], "tensor", core_pairs())
    branch_pushed = push_tails(after(branch_tails, tiles2))
    outs = heads_backward(
        "heads_backward_0", info, after(x_all, far_sum_a), tiles, 0, qkv0, mixed0[0], stats0, d_mixed0, False,
        piece_size(image_rows),
    )
    outs, (came_y, far_a, far_b, branch_pushed) = beside(outs, came_y, far_a_sum, far_b_sum, branch_pushed)
    *dx, tiles0 = outs
    dy = [dy[0], came_y, dy[2]]
    groups = [(part_a[0], near_a, far_a), (part_b[0], near_b, far_b)]
    finals = [(GROUPS[2][0], sum_c), (32, tiles2), (0, tiles0)]
    outputs = push_rows((encoded, decoded), pushed, (image_rows, tag_rows), (None, None), info)
    return outputs, (branch0, branch2), branch_pushed, (dx, dy), groups, finals, extra


def one_hot(index, count, dtype):
    return (index[:, None] == lax.broadcasted_iota(jnp.int32, (1, count), 1)).astype(dtype)


def local(
    image_tokens,
    tag_tokens,
    image_cotangent,
    tag_cotangent,
    tag_lengths,
    slot_blocks,
    master_blocks,
    left_factor,
    right_factor,
    left_root,
    right_root,
    vector_master,
    vector_moment,
):
    dp = lax.axis_size("dp")
    shards = lax.axis_size("tensor")
    me = lax.axis_index("tensor")
    slots = master_blocks.shape[1]
    items = tag_lengths.shape[0]
    image_length = image_tokens.shape[0] * shards // items
    item_length = tag_tokens.shape[0] * shards // items
    lanes = vector_master.shape[1]
    def rows_of(value):
        return jnp.pad(value, ((0, 16 - value.shape[0]), (0, TILE - value.shape[1])))

    own = jnp.concatenate(
        [
            master_blocks.astype(BF16).reshape(slots * TILE, TILE),
            rows_of(vector_master.astype(BF16)),
        ],
        axis=0,
    )
    at = lax.broadcasted_iota(jnp.int32, (items,), 0)
    live = jnp.sum(jnp.where(at == me, tag_lengths, 0))
    info = jnp.concatenate(
        [
            jnp.stack([jnp.minimum(me, items - 1), me] + [jnp.minimum(me ^ r, items - 1) for r in (1, 2, 3)]),
            tag_lengths,
            live[None],
            me ^ at,
            jnp.zeros((4,), jnp.int32),
        ]
    ).reshape(1, 16)
    ranks = jnp.stack([relative_rank(p, dp) for p in range(dp)])

    def blocks_of(those):
        picked = one_hot(those, dp, jnp.int32)[:, :, None] * slot_blocks.reshape(1, dp, slots)
        return jnp.sum(picked, axis=1)

    targets = jnp.stack([target_rank(p, dp) for p in range(dp)])
    ready = (info, blocks_of(ranks), blocks_of(targets), ranks, targets)
    pieces, x_all, sequences, moved, ready = gather_rows(
        image_tokens, tag_tokens, tag_cotangent, own, dp,
        lambda parts, info: whole_group(parts, info, "whole_images"), ready
    )
    info, source_blocks, target_blocks, ranks, targets = ready
    y_all = whole_group(sequences, info, "whole_sequences")
    tiles, *group_tiles, vectors = order_tiles(pieces, source_blocks, ranks, slots, lanes)
    near = lax.ppermute(tiles, "tensor", core_pairs())
    images, tags = image_tokens.shape[0], tag_tokens.shape[0]
    outputs, branches, pushed, (dx, dy), groups, finals, extra = compute(
        info, x_all, y_all, image_cotangent, (tag_cotangent, moved), tiles, group_tiles, near, vectors, images, tags
    )
    came_x = lax.ppermute(dx[1], "tensor", core_pairs())
    outgoing = deal_tiles(groups, finals, extra, target_blocks, targets, slots, lanes)
    outgoing, (came_x,) = beside(outgoing, came_x)
    terms, mark = sum_pieces(outgoing, dp)
    came = [came_x, dy[1]]
    far = [
        (part[2].astype(F32) + near_part[part[0].shape[0] :].astype(F32)).astype(BF16)
        for part, near_part in zip((dx, dy), came)
    ]
    far = lax.ppermute(after(jnp.concatenate(far, axis=0), mark), "tensor", chip_pairs())
    sums = [
        ((part[0], 0), (near_part, 0), (far, begin))
        for part, near_part, begin in zip((dx, dy), came, (0, dx[0].shape[0]))
    ]
    rows = push_rows(branches, pushed, (images, tags), sums, info)
    updates = shampoo(
        [*terms[:-1], after(terms[-1], *rows)] if dp == 8 else terms,
        master_blocks,
        left_factor,
        right_factor,
        left_root,
        right_root,
        vector_master,
        vector_moment,
    )
    return (*outputs, *rows, *updates)


def solution(mesh):
    in_specs = (
        P(("dp", "tensor"), None),
        P(("dp", "tensor"), None),
        P(("dp", "tensor"), None),
        P(("dp", "tensor"), None),
        P("dp"),
        P(),
        P("tensor", "dp", None, None),
        P("tensor", "dp", None, None),
        P("tensor", "dp", None, None),
        P("tensor", "dp", None, None),
        P("tensor", "dp", None, None),
        P(None, "dp"),
        P(None, "dp"),
    )
    out_specs = (
        P(("dp", "tensor"), None),
        P(("dp", "tensor"), None),
        P(("dp", "tensor"), None),
        P(("dp", "tensor"), None),
        P("tensor", "dp", None, None),
        P("tensor", "dp", None, None),
        P("tensor", "dp", None, None),
        P("tensor", "dp", None, None),
        P("tensor", "dp", None, None),
        P(None, "dp"),
        P(None, "dp"),
        P(None, "dp"),
    )
    return jax.shard_map(local, mesh=mesh, in_specs=in_specs, out_specs=out_specs, check_vma=False)
```
